32 devices in a mesh: dp: 4 (over y, x), fsdp: 8 (over z, core).
Axes of the slice: x: 2, y: 2, z: 4, core: 2. Of those that a mesh axis runs over, the one named last changes fastest.
Arguments:
- latents: bfloat16 [64, 256, 384], P(('dp', 'fsdp')), may hold values from -6 to 6
- cond: bfloat16 [64, 384], P(('dp', 'fsdp')), may hold values from -6 to 6
- counts: int32 [32], P(('dp', 'fsdp')), may hold values from 1 to 2, as said below
- cotangent: bfloat16 [64, 256, 384], P(('dp', 'fsdp')), may hold values from -6 to 6
- modulation_weight: bfloat16 [384, 2304], P('fsdp'), may hold values from -0.3125 to 0.3125
- modulation_bias: bfloat16 [2304], P('fsdp'), may hold values from -1.796875 to 1.796875
- projection_weight: bfloat16 [384, 1152], P('fsdp'), may hold values from -0.3125 to 0.3125
- query_value_bias: bfloat16 [768], P('fsdp'), may hold values from -1.796875 to 1.796875
- output_weight: bfloat16 [384, 384], P('fsdp'), may hold values from -1.25 to 1.25
- output_bias: bfloat16 [384], P('fsdp'), may hold values from -1.796875 to 1.796875
- up_weight: bfloat16 [384, 1536], P('fsdp'), may hold values from -0.3125 to 0.3125
- up_bias: bfloat16 [1536], P('fsdp'), may hold values from -1.796875 to 1.796875
- down_weight: bfloat16 [1536, 384], P('fsdp'), may hold values from -0.3125 to 0.3125
- down_bias: bfloat16 [384], P('fsdp'), may hold values from -1.796875 to 1.796875
Outputs:
- result: bfloat16 [64, 256, 384], P(('dp', 'fsdp'))
- latent_grad: bfloat16 [64, 256, 384], P(('dp', 'fsdp'))
- cond_grad: bfloat16 [64, 384], P(('dp', 'fsdp'))
- grad_modulation_weight: float32 [384, 2304], P('fsdp')
- grad_modulation_bias: float32 [2304], P('fsdp')
- grad_projection_weight: float32 [384, 1152], P('fsdp')
- grad_query_value_bias: float32 [768], P('fsdp')
- grad_output_weight: float32 [384, 384], P('fsdp')
- grad_output_bias: float32 [384], P('fsdp')
- grad_up_weight: float32 [384, 1536], P('fsdp')
- grad_up_bias: float32 [1536], P('fsdp')
- grad_down_weight: float32 [1536, 384], P('fsdp')
- grad_down_bias: float32 [384], P('fsdp')
The draws below stay inside these ranges and needn't reach their ends.
Inputs may be any that keep to these rules, and one draw needn't show every extreme that they name: `counts`: slots i of a device with i < its count hold live latents, the others padding; some device holds 2 live latents and some holds 1.
All inputs are finite; a program needn't handle non-finite values.
Results may differ from the reference program's by a relative error of at most 0.015.
The reference program's roundings to bfloat16 on the way count: a program that leaves them out, or rounds other values in their place, can miss the bound.
Values may be sent and summed in bfloat16 or wider, within the bound.
No kernel may reach another device: no remote copies, remote signals or barrier semaphores. Data moves between devices by JAX's collectives and lax.ppermute only.
A program may use at most 128 MiB of HBM per device.

```python
import jax
import jax.numpy as jnp
from jax import lax

D = 384
HEADS = 6
HEAD_DIM = 64
FF = 1536
SEQ = 256
LAT_DEV = 2
LATENTS = 64


def draw_counts(key, part):
    key = jax.random.fold_in(key, 7)
    devices = LATENTS // LAT_DEV
    first_key, second_key, third_key = jax.random.split(key, 3)
    drawn = jax.random.randint(first_key, (devices,), 1, LAT_DEV + 1)
    highest = jax.random.randint(second_key, (), 0, devices)
    lowest = (highest + 1 + jax.random.randint(third_key, (), 0, devices - 1)) % devices
    drawn = drawn.at[highest].set(LAT_DEV).at[lowest].set(1)
    return drawn.astype(jnp.int32)


def shard_levels(rng, extent, shards, low, largest):
    gain, own = 1.0, jax.random.fold_in(rng, 6)
    for axis_at, parts in shards:
        heights = jnp.exp(jax.random.uniform(jax.random.fold_in(own, axis_at), (parts,), jnp.float32, low / len(shards), largest / len(shards)))
        gain = gain * jnp.repeat(heights, extent[axis_at] // parts).reshape([-1 if axis == axis_at else 1 for axis in range(len(extent))])
    return gain


def noise(own_key, shape, width, limit, cuts=(), kind=jnp.bfloat16):
    values = jax.random.normal(own_key, shape, jnp.float32) * width
    if len(cuts) > 0:
        values = shard_levels(own_key, shape, cuts, -0.22, 0.18) * values
    return jnp.clip(values, min=-limit, max=limit).astype(kind)


def setup_inputs(seed: int = 0) -> dict:
    key_list = jax.random.split(jax.random.key(seed), 15)
    return {
        "latents": noise(key_list[0], (LATENTS, SEQ, D), 1.0, 6.0, ((0, 32),)),
        "cond": noise(key_list[1], (LATENTS, D), 1.0, 6.0, ((0, 32),)),
        "counts": draw_counts(jax.random.fold_in(key_list[14], 71), 0),
        "cotangent": noise(key_list[3], (LATENTS, SEQ, D), 1.0, 6.0, ((0, 32),)),
        "modulation_weight": noise(key_list[4], (D, 6 * D), D ** -0.5, 0.3125, ((0, 8),)),
        "modulation_bias": noise(key_list[5], (6 * D,), 0.3, 1.796875, ((0, 8),)),
        "projection_weight": noise(key_list[6], (D, 3 * D), D ** -0.5, 0.3125, ((0, 8),)),
        "query_value_bias": noise(key_list[7], (2 * D,), 0.3, 1.796875, ((0, 8),)),
        "output_weight": noise(key_list[8], (D, D), (D // 16) ** -0.5, 1.25, ((0, 8),)),
        "output_bias": noise(key_list[9], (D,), 0.3, 1.796875, ((0, 8),)),
        "up_weight": noise(key_list[10], (D, FF), D ** -0.5, 0.3125, ((0, 8),)),
        "up_bias": noise(key_list[11], (FF,), 0.3, 1.796875, ((0, 8),)),
        "down_weight": noise(key_list[12], (FF, D), (FF // 4) ** -0.5, 0.3125, ((0, 8),)),
        "down_bias": noise(key_list[13], (D,), 0.3, 1.796875, ((0, 8),)),
    }


@jax.custom_vjp
def low(v):
    return lax.optimization_barrier(v.astype(jnp.bfloat16)).astype(jnp.float32)

@jax.custom_vjp
def low_back(v):
    return v

def low_keep(v):
    return (low(v), None)

def low_pass(kept, grad):
    return (grad,)

def back_keep(v):
    return (v, None)

def back_low(kept, grad):
    return (low(grad),)
low.defvjp(low_keep, low_pass)
low_back.defvjp(back_keep, back_low)
exact_mode = lax.Precision.HIGHEST

def layer_norm(vector):
    row_mean = lax.optimization_barrier(jnp.mean(vector, axis=-1, keepdims=True))
    centered = vector - row_mean
    variance = lax.optimization_barrier(jnp.mean(centered * centered, axis=-1, keepdims=True))
    return centered * lax.rsqrt(variance + 1e-06)

def modulate(vector, offset, stretch):
    return layer_norm(vector) * (1.0 + stretch[:, None, :]) + offset[:, None, :]

def block_forward(params, inputs, conditions, alive_mask):
    modulation_weight, modulation_bias, projection_weight, query_value_bias, output_weight, output_bias, up_weight, up_bias, down_weight, down_bias = params
    members, length, features = inputs.shape
    cond_low = low(jax.nn.silu(conditions))
    modulation = low_back(jnp.dot(cond_low, modulation_weight, precision=exact_mode) + modulation_bias)
    shift_one, scale_one, gate_one, shift_two, scale_two, gate_two = jnp.split(modulation, 6, axis=-1)
    normed_one = low(modulate(inputs, shift_one, scale_one))
    zero_bias = jnp.zeros((features,), query_value_bias.dtype)
    joined_bias = jnp.concatenate([query_value_bias[:features], zero_bias, query_value_bias[features:]])
    projected = jnp.einsum('bsd,de->bse', normed_one, projection_weight, precision=exact_mode) + joined_bias
    projected = low(low_back(projected)).reshape(members, length, 3, HEADS, HEAD_DIM)
    queries = projected[:, :, 0]
    key_rows = projected[:, :, 1]
    values = projected[:, :, 2]
    scores = jnp.einsum('bqhd,bkhd->bhqk', queries, key_rows, precision=exact_mode) * HEAD_DIM ** (-0.5)
    scores = low_back(scores)
    row_max = lax.optimization_barrier(jnp.max(scores, axis=-1, keepdims=True))
    exponent = jnp.exp(scores - row_max)
    probability = exponent / lax.optimization_barrier(jnp.sum(exponent, axis=-1, keepdims=True))
    attended = jnp.einsum('bhqk,bkhd->bqhd', low(probability), values, precision=exact_mode)
    attended = low(low_back(attended.reshape(members, length, features)))
    branch = jnp.einsum('bsd,de->bse', attended, output_weight, precision=exact_mode) + output_bias
    branch = low_back(branch)
    middle = inputs + gate_one[:, None, :] * branch
    normed_two = low(modulate(middle, shift_two, scale_two))
    pre_act = low_back(jnp.einsum('bsd,df->bsf', normed_two, up_weight, precision=exact_mode) + up_bias)
    activated = low(jax.nn.gelu(pre_act, approximate=True))
    mlp_out = low_back(jnp.einsum('bsf,fd->bsd', activated, down_weight, precision=exact_mode) + down_bias)
    return (middle + gate_two[:, None, :] * mlp_out) * alive_mask[:, None, None]

def reference(latents, cond, counts, cotangent, modulation_weight, modulation_bias, projection_weight, query_value_bias, output_weight, output_bias, up_weight, up_bias, down_weight, down_bias):
    params = tuple((weight.astype(jnp.float32) for weight in (modulation_weight, modulation_bias, projection_weight, query_value_bias, output_weight, output_bias, up_weight, up_bias, down_weight, down_bias)))
    group_size = 16
    groups = LATENTS // group_size
    slot_index = jnp.arange(LATENTS, dtype=jnp.int32)
    owner_index = slot_index // LAT_DEV
    alive_all = (slot_index % LAT_DEV < counts[owner_index]).astype(jnp.float32)
    grouped = (latents.reshape(groups, group_size, SEQ, D), cond.reshape(groups, group_size, D), alive_all.reshape(groups, group_size), cotangent.reshape(groups, group_size, SEQ, D))

    def group_step(carried, group_item):
        inputs, conditions, alive_mask, upstream = group_item

        def forward(weights, inputs_full, cond_full):
            return block_forward(weights, inputs_full, cond_full, alive_mask)
        output, pullback = jax.vjp(forward, params, inputs.astype(jnp.float32), conditions.astype(jnp.float32))
        grad_params, grad_inputs, grad_cond = pullback(upstream.astype(jnp.float32))
        carried = jax.tree.map(jnp.add, carried, grad_params)
        return (carried, (output.astype(jnp.bfloat16), grad_inputs.astype(jnp.bfloat16), grad_cond.astype(jnp.bfloat16)))
    empty_sums = tuple((jnp.zeros(weight.shape, jnp.float32) for weight in params))
    totals, (outputs, input_grads, cond_grads) = lax.scan(group_step, empty_sums, grouped)
    return (outputs.reshape(LATENTS, SEQ, D), input_grads.reshape(LATENTS, SEQ, D), cond_grads.reshape(LATENTS, D), totals[0], totals[1], totals[2], totals[3], totals[4], totals[5], totals[6], totals[7], totals[8], totals[9])
```

```python
import functools

import jax
import jax.numpy as jnp
from jax import lax
from jax.experimental import pallas as pl
from jax.experimental.pallas import tpu as pltpu
from jax.sharding import PartitionSpec as P

HEADS = 6
HEAD_DIM = 64
MICRO = 2
F32 = jnp.float32
BF16 = jnp.bfloat16
BOTH = ("dp", "fsdp")
NN = (((1,), (0,)), ((), ()))
NT = (((1,), (1,)), ((), ()))
TN = (((0,), (0,)), ((), ()))


def dot(left, right, dims=NN):
    return lax.dot_general(left, right, dims, preferred_element_type=F32)


def smem():
    return pl.BlockSpec(memory_space=pltpu.SMEM)


def vmem():
    return pl.BlockSpec(memory_space=pltpu.VMEM)


def call(body, name, ids, ins, outs, scratch=(), flops=0, limit=48):
    moved = sum(a.size * a.dtype.itemsize for a in ins) + sum(
        jnp.dtype(t).itemsize * functools.reduce(lambda a, b: a * b, s, 1) for s, t in outs
    )
    return pl.pallas_call(
        body,
        out_shape=[jax.ShapeDtypeStruct(s, t) for s, t in outs],
        in_specs=[smem()] + [vmem()] * len(ins),
        out_specs=[vmem()] * len(outs),
        scratch_shapes=list(scratch),
        compiler_params=pltpu.CompilerParams(vmem_limit_bytes=limit * 1024 * 1024),
        cost_estimate=pl.CostEstimate(flops=flops, bytes_accessed=moved, transcendentals=0),
        name=name,
    )(ids, *ins)


def offsets(ids):
    d, f = ids[0], ids[1]
    core = lax.rem(f, 2)
    first = 1 + core
    second = 2 - core
    return d, f, (0, first, second, 3), (0, second, first, 3)


def flip(a, b):
    return lax.bitwise_xor(a, b)


def pick_body(ids, proj, outw, up, down, cond, q_po, q_ud, c_low):
    d = ids[0]
    width = outw.shape[1]
    rows = outw.shape[0]

    @pl.when(d < 3)
    def _():
        q_po[...] = proj[:, pl.ds(pl.multiple_of(lax.min(d, 2) * width, 128), width)]

    @pl.when(d == 3)
    def _():
        q_po[...] = outw[...]

    q_ud[0] = up[:, pl.ds(pl.multiple_of(d * width, 128), width)]
    q_ud[1] = down[pl.ds(pl.multiple_of(d * rows, 16), rows), :]
    c = cond[...].astype(F32)
    c_low[...] = (c / (1.0 + jnp.exp(-c))).astype(BF16)


def one_hot(shape, shift):
    r = lax.broadcasted_iota(jnp.int32, shape, 0)
    c = lax.broadcasted_iota(jnp.int32, shape, 1)
    return jnp.where(c == r + shift, 1.0, 0.0).astype(BF16)


def mod_body(ids, c0, c1, c2, c3, wmod, bmod, bqv, bout, bup, bdown, k0, k1, k2, k3, send):
    f = ids[1]
    wide = wmod.shape[1]
    rows = wmod.shape[0]
    feat = c0.shape[1]
    r = lax.broadcasted_iota(jnp.int32, (feat, rows), 0)
    c = lax.broadcasted_iota(jnp.int32, (feat, rows), 1)
    select = jnp.where(r == c + f * rows, 1.0, 0.0).astype(BF16)

    def place(ref, total):
        n = ref.shape[1]
        return dot(ref[...], one_hot((n, total), f * n))

    bias = place(bmod, wide)
    row_two = jnp.concatenate([place(bup, 4 * feat), place(bqv, 2 * feat)], axis=1)
    row_three = jnp.concatenate(
        [place(bout, feat), place(bdown, feat), jnp.zeros((1, 4 * feat), F32)], axis=1
    )
    for zm, (ref, keep) in enumerate(zip((c0, c1, c2, c3), (k0, k1, k2, k3))):
        own = dot(ref[...], select).astype(BF16)
        part = dot(own, wmod[...]) + bias
        keep[0:2, :] = part[0:2]
        keep[2:3, :] = row_two
        keep[3:4, :] = row_three
        send[zm, 0:2, :] = part[2:4]
        send[zm, 2:3, :] = row_two
        send[zm, 3:4, :] = row_three


def norm_parts(x):
    mean = jnp.mean(x, axis=-1, keepdims=True)
    centered = x - mean
    rstd = lax.rsqrt(jnp.mean(centered * centered, axis=-1, keepdims=True) + 1e-06)
    return centered * rstd, rstd


def lane_masks(rows):
    lane = lax.broadcasted_iota(jnp.int32, (rows, 2 * HEAD_DIM), 1)
    return lane < HEAD_DIM


def attend_body(
    ids, w0, w1, w2, w3, o0, o1, o2, o3, p0, p1, p2, p3, lat, wpo, mod, n1, proj, att
):
    d, f, mine, theirs = offsets(ids)
    rows = w0.shape[1]
    feat = w0.shape[2]
    for refs, flips, base in (((w0, w1, w2, w3), mine, f), ((o0, o1, o2, o3), theirs, flip(f, 1))):
        for ref, how in zip(refs, flips):
            block = flip(d, how)
            for zm in range(4):
                at = pl.multiple_of(flip(base, 2 * zm) * rows, 16)
                wpo[block, pl.ds(at, rows), :] = ref[zm]
    mod[...] = (p0[...] + p1[...]) + (p2[...] + p3[...])
    length = lat.shape[1]
    low_half = lane_masks(length)
    qv = mod[2:3, 4 * feat :]

    def one(i, carry):
        at = pl.multiple_of(i * length, 256)
        x = lat[i].astype(F32)
        xhat, rstd = norm_parts(x)
        row = mod[pl.ds(i, 1), :]
        n = (xhat * (1.0 + row[:, feat : 2 * feat]) + row[:, :feat]).astype(BF16)
        n1[pl.ds(at, length), :] = n
        proj[pl.ds(at, length), 0:feat] = (dot(n, wpo[0]) + qv[:, :feat]).astype(BF16)
        proj[pl.ds(at, length), feat : 2 * feat] = dot(n, wpo[1]).astype(BF16)
        proj[pl.ds(at, length), 2 * feat :] = (dot(n, wpo[2]) + qv[:, feat:]).astype(BF16)
        for pair in range(HEADS // 2):
            lo = pair * 2 * HEAD_DIM
            hi = lo + 2 * HEAD_DIM
            q = proj[pl.ds(at, length), lo:hi]
            k = proj[pl.ds(at, length), feat + lo : feat + hi]
            v = proj[pl.ds(at, length), 2 * feat + lo : 2 * feat + hi]
            zero = jnp.zeros_like(q)
            outs = []
            for side in range(2):
                q_one = jnp.where(low_half, q, zero) if side == 0 else jnp.where(low_half, zero, q)
                s = dot(q_one, k, NT) * HEAD_DIM ** (-0.5)
                e = jnp.exp(s - jnp.max(s, axis=-1, keepdims=True))
                inv = 1.0 / jnp.sum(e, axis=-1, keepdims=True)
                outs.append(dot((e * inv).astype(BF16), v))
            att[pl.ds(at, length), lo:hi] = jnp.where(low_half, outs[0], outs[1]).astype(BF16)
        return carry

    lax.fori_loop(0, lat.shape[0], one, 0)


def spread(tmp, at_row, dm, keeps, sends, rows, f, slot=None):
    swapped = (0, 2, 1, 3)[dm]
    for zm in range(4):
        for ref, owner in ((keeps[dm], flip(f, 2 * zm)), (sends[swapped], flip(f, 2 * zm + 1))):
            piece = tmp[pl.ds(pl.multiple_of(at_row(owner), 16), rows), :]
            if slot is None:
                ref[zm] = piece
            else:
                ref[zm, slot] = piece


def mlp_body(
    ids, w0, w1, w2, w3, o0, o1, o2, o3, wout, mod, lat, cot, att,
    res, gmid, gbr, gatt, gsum, gmod, k0, k1, k2, k3, s0, s1, s2, s3,
    wu, wd, n2s, acts, dgs, gmlps, gpres, n2t, tmp, tmpd,
):
    d, f, mine, theirs = offsets(ids)
    count = ids[2]
    rows = w0.shape[2]
    feat = w0.shape[3]
    hidden = wd.shape[0]
    blocks = hidden // feat
    for refs, flips, base in (((w0, w1, w2, w3), mine, f), ((o0, o1, o2, o3), theirs, flip(f, 1))):
        for ref, how in zip(refs, flips):
            block = flip(d, how)
            for zm in range(4):
                owner = flip(base, 2 * zm)
                wu[block, pl.ds(pl.multiple_of(owner * rows, 16), rows), :] = ref[zm, 0]
                wd[pl.ds(pl.multiple_of(owner * 4 * rows + block * rows, 16), rows), :] = ref[zm, 1]
    length = lat.shape[1]
    bup = mod[2:3, : 4 * feat]
    bout = mod[3:4, :feat]
    bdown = mod[3:4, feat : 2 * feat]
    gsum[...] = jnp.zeros_like(gsum)

    def one(i, carry):
        at = pl.multiple_of(i * length, 256)
        part = pl.ds(at, length)
        row = mod[pl.ds(i, 1), :]
        gate_one, shift, scale, gate_two = (row[:, j * feat : (j + 1) * feat] for j in (2, 3, 4, 5))
        alive = jnp.where(i < count, 1.0, 0.0).astype(F32)
        branch = dot(att[part, :], wout[0]) + bout
        middle = lat[i].astype(F32) + gate_one * branch
        xhat, rstd = norm_parts(middle)
        n2 = (xhat * (1.0 + scale) + shift).astype(BF16)
        n2s[part, :] = n2
        mlp = jnp.zeros((length, feat), F32) + bdown
        for j in range(blocks):
            cols = slice(j * feat, (j + 1) * feat)
            v = dot(n2, wu[j]) + bup[:, cols]
            t = jnp.tanh(0.7978845608028654 * (v + 0.044715 * v * v * v))
            half = 0.5 * (1.0 + t)
            act = (v * half).astype(BF16)
            dgs[:, cols] = half + 0.5 * v * (1.0 - t * t) * (
                0.7978845608028654 * (1.0 + 0.134145 * v * v)
            )
            acts[part, cols] = act
            mlp = mlp + dot(act, wd[cols, :])
        res[i] = (alive * (middle + gate_two * mlp)).astype(BF16)
        upstream = alive * cot[i].astype(F32)
        g_gate_two = jnp.sum(upstream * mlp, axis=0, keepdims=True)
        gmlp = (gate_two * upstream).astype(BF16)
        gmlps[part, :] = gmlp
        gn = jnp.zeros((length, feat), F32)
        for j in range(blocks):
            cols = slice(j * feat, (j + 1) * feat)
            gpre = (dot(gmlp, wd[cols, :], NT) * dgs[:, cols]).astype(BF16)
            gpres[part, cols] = gpre
            gn = gn + dot(gpre, wu[j], NT)
            gsum[:, feat + j * feat : 2 * feat + j * feat] += jnp.sum(
                gpre.astype(F32), axis=0, keepdims=True
            )
        g_shift = jnp.sum(gn, axis=0, keepdims=True)
        g_scale = jnp.sum(gn * xhat, axis=0, keepdims=True)
        gx = gn * (1.0 + scale)
        gmiddle = upstream + rstd * (
            gx
            - jnp.mean(gx, axis=-1, keepdims=True)
            - xhat * jnp.mean(gx * xhat, axis=-1, keepdims=True)
        )
        gmid[i] = gmiddle
        g_gate_one = jnp.sum(gmiddle * branch, axis=0, keepdims=True)
        gbranch = (gate_one * gmiddle).astype(BF16)
        gbr[part, :] = gbranch
        gatt[part, :] = dot(gbranch, wout[0], NT).astype(BF16)
        gsum[:, 0:feat] += jnp.sum(gbranch.astype(F32), axis=0, keepdims=True)
        gsum[:, 5 * feat : 6 * feat] += jnp.sum(gmlp.astype(F32), axis=0, keepdims=True)
        gmod[pl.ds(i, 1), :] = jnp.concatenate([g_gate_one, g_shift, g_scale, g_gate_two], axis=1)
        return carry

    lax.fori_loop(0, lat.shape[0], one, 0)
    keeps, sends = (k0, k1, k2, k3), (s0, s1, s2, s3)
    for j in range(blocks):
        cols = slice(j * feat, (j + 1) * feat)
        tmpd[cols, :] = dot(acts[:, cols], gmlps[...], TN).astype(BF16)
    n2t[...] = n2s[...].T
    for dm in (1, 3, 0, 2):
        block = flip(d, mine[dm])
        spread(tmpd, lambda o: (o * 4 + block) * rows, dm, keeps, sends, rows, f, 1)
        tmp[...] = dot(
            n2t[...], gpres[:, pl.ds(pl.multiple_of(block * feat, 128), feat)]
        ).astype(BF16)
        spread(tmp, lambda o: o * rows, dm, keeps, sends, rows, f, 0)


def attend_back_body(
    ids, proj, gatt, att, gbr, n1, gsum, gproj, bias, k0, k1, k2, k3, s0, s1, s2, s3,
    gall, xts, tmp, *, length,
):
    d, f, mine, _ = offsets(ids)
    feat = att.shape[1]
    rows = k0.shape[1]
    low_half = lane_masks(length)

    def one(i, carry):
        part = pl.ds(pl.multiple_of(i * length, 256), length)
        for pair in range(HEADS // 2):
            lo = pair * 2 * HEAD_DIM
            hi = lo + 2 * HEAD_DIM
            q = proj[part, lo:hi]
            k = proj[part, feat + lo : feat + hi]
            v = proj[part, 2 * feat + lo : 2 * feat + hi]
            ga = gatt[part, lo:hi]
            zero = jnp.zeros_like(q)
            gq = jnp.zeros(q.shape, F32)
            gk = jnp.zeros(q.shape, F32)
            gv = jnp.zeros(q.shape, F32)
            for side in range(2):
                own = lambda a: (
                    jnp.where(low_half, a, zero) if side == 0 else jnp.where(low_half, zero, a)
                )
                q_one, ga_one = own(q), own(ga)
                s = dot(k, q_one, NT) * HEAD_DIM ** (-0.5)
                e = jnp.exp(s - jnp.max(s, axis=0, keepdims=True))
                prob = e * (1.0 / jnp.sum(e, axis=0, keepdims=True))
                gv = gv + dot(prob.astype(BF16), ga_one)
                gp = dot(v, ga_one, NT)
                delta = jnp.sum(gp * prob, axis=0, keepdims=True)
                gs = (prob * (gp - delta)).astype(BF16)
                gk = gk + dot(gs, q_one)
                gq = gq + dot(gs, own(k), TN)
            gall[part, lo:hi] = (gq * HEAD_DIM ** (-0.5)).astype(BF16)
            gall[part, feat + lo : feat + hi] = (gk * HEAD_DIM ** (-0.5)).astype(BF16)
            gall[part, 2 * feat + lo : 2 * feat + hi] = gv.astype(BF16)
        return carry

    lax.fori_loop(0, proj.shape[0] // length, one, 0)
    gproj[...] = gall[:, : 3 * feat]
    gall[:, 3 * feat :] = gbr[...]
    xts[0] = n1[...].T
    xts[1] = att[...].T
    keeps, sends = (k0, k1, k2, k3), (s0, s1, s2, s3)
    for dm in (1, 3, 0, 2):
        block = flip(d, mine[dm])
        tmp[...] = dot(
            xts[jnp.where(block == 3, 1, 0)],
            gall[:, pl.ds(pl.multiple_of(block * feat, 128), feat)],
        ).astype(BF16)
        spread(tmp, lambda o: o * rows, dm, keeps, sends, rows, f)
    bias[:, 0:feat] = jnp.sum(gall[:, 0:feat].astype(F32), axis=0, keepdims=True)
    bias[:, feat : 2 * feat] = jnp.sum(
        gall[:, 2 * feat : 3 * feat].astype(F32), axis=0, keepdims=True
    )
    bias[:, 2 * feat :] = gsum[...]


def input_back_body(ids, gproj, wpo, lat, gmid, mod, gmod, lgrad, gm):
    length = lat.shape[1]
    feat = lat.shape[2]

    def one(i, carry):
        part = pl.ds(pl.multiple_of(i * length, 256), length)
        row = mod[pl.ds(i, 1), :]
        xhat, rstd = norm_parts(lat[i].astype(F32))
        gn = dot(gproj[part, 0:feat], wpo[0], NT)
        gn = gn + dot(gproj[part, feat : 2 * feat], wpo[1], NT)
        gn = gn + dot(gproj[part, 2 * feat :], wpo[2], NT)
        g_shift = jnp.sum(gn, axis=0, keepdims=True)
        g_scale = jnp.sum(gn * xhat, axis=0, keepdims=True)
        gx = gn * (1.0 + row[:, feat : 2 * feat])
        lgrad[i] = (
            gmid[i]
            + rstd
            * (
                gx
                - jnp.mean(gx, axis=-1, keepdims=True)
                - xhat * jnp.mean(gx * xhat, axis=-1, keepdims=True)
            )
        ).astype(BF16)
        gm[pl.ds(i, 1), :] = jnp.concatenate(
            [g_shift, g_scale, gmod[pl.ds(i, 1), :]], axis=1
        )
        return carry

    lax.fori_loop(0, lat.shape[0], one, 0)


def cond_back_body(ids, g0, g1, g2, g3, wmod, x0, x1, x2, x3):
    f = ids[1]
    rows = wmod.shape[0]
    place = one_hot((rows, x0.shape[1]), f * rows).astype(F32)
    for ref, out in zip((g0, g1, g2, g3), (x0, x1, x2, x3)):
        part = dot(ref[...], wmod[...], NT)
        out[...] = lax.dot_general(
            part, place, NN, preferred_element_type=F32, precision=lax.Precision.HIGHEST
        )


def mod_weight_body(ids, *refs):
    conds, grads, (wgrad, bgrad) = refs[:4], refs[4:8], refs[8:]
    f = ids[1]
    rows = wgrad.shape[0]
    feat = conds[0].shape[1]
    select = one_hot((rows, feat), f * rows)
    total = None
    sums = None
    for c, g in zip(conds, grads):
        grad = g[...]
        own = dot(select, c[...], NT).astype(BF16)
        term = dot(own, grad)
        total = term if total is None else total + term
        s = jnp.sum(grad.astype(F32), axis=0, keepdims=True)
        sums = s if sums is None else sums + s
    wgrad[...] = total
    bgrad[...] = sums


def final_po_body(ids, g0, g1, g2, g3, gp, go):
    d, _, mine, _ = offsets(ids)
    feat = go.shape[1]
    for ref, how in zip((g0, g1, g2, g3), mine):
        block = flip(d, how)

        @pl.when(block < 3)
        def _():
            at = pl.multiple_of(lax.min(block, 2) * feat, 128)
            gp[:, pl.ds(at, feat)] = ref[...].astype(F32)

        @pl.when(block == 3)
        def _():
            go[...] = ref[...].astype(F32)


def final_ud_body(ids, g0, g1, g2, g3, gu, gd):
    d, _, mine, _ = offsets(ids)
    rows, feat = g0.shape[1:]
    for ref, how in zip((g0, g1, g2, g3), mine):
        block = flip(d, how)
        gu[:, pl.ds(pl.multiple_of(block * feat, 128), feat)] = ref[0].astype(F32)
        gd[pl.ds(pl.multiple_of(block * rows, 16), rows), :] = ref[1].astype(F32)


def routes():
    core, first, second = [], [], []
    levels = {1: [], 2: [], 3: []}
    for d in range(4):
        for f in range(8):
            i = d * 8 + f
            core.append((i, i ^ 1))
            a = 1 if f % 2 == 0 else 2
            first.append((i, (d ^ a) * 8 + f))
            second.append((i, (d ^ (3 - a)) * 8 + f))
            for m in levels:
                levels[m].append((i, d * 8 + (f ^ (2 * m))))
    return core, first, second, levels


def add_low(*parts):
    total = parts[0].astype(F32)
    for part in parts[1:]:
        total = total + part.astype(F32)
    return total.astype(BF16)


def on_device_blocks(
    latents, cond, counts, cotangent, modulation_weight, modulation_bias, projection_weight,
    query_value_bias, output_weight, output_bias, up_weight, up_bias, down_weight, down_bias,
):
    core, first, second, levels = routes()

    def move(x, route):
        return lax.ppermute(x, BOTH, route)

    slots, length, feat = latents.shape
    rows = projection_weight.shape[0]
    hidden = up_weight.shape[1]
    wide = modulation_weight.shape[1]
    tokens = slots * length
    d = lax.axis_index("dp")
    f = lax.axis_index("fsdp")
    ids = jnp.stack([d, f, counts[0]]).astype(jnp.int32)

    q_po, q_ud, c_low = call(
        pick_body, "pick", ids,
        [projection_weight, output_weight, up_weight, down_weight, cond],
        [((rows, feat), BF16), ((2, rows, feat), BF16), ((slots, feat), BF16)],
    )

    def gather(q):
        own = jnp.stack([q] + [move(q, levels[m]) for m in (1, 2, 3)])
        a = move(own, first)
        b = move(own, second)
        ab = move(a, second)
        mine = [own, a, b, ab]
        return mine + [move(x, core) for x in mine]

    c_pair = jnp.concatenate([c_low, move(c_low, core)], axis=0)
    c_all = [c_pair] + [move(c_pair, levels[m]) for m in (1, 2, 3)]
    w_po = gather(q_po)
    *kept, sent = call(
        mod_body, "modulation", ids,
        c_all + [
            modulation_weight, modulation_bias[None], query_value_bias[None],
            output_bias[None], up_bias[None], down_bias[None],
        ],
        [((4, wide), F32)] * 4 + [((4, 4, wide), F32)],
    )
    arrived = move(sent, core)
    paid = [kept[m] + arrived[m] for m in range(4)]
    paid = [paid[0]] + [move(paid[m], levels[m]) for m in (1, 2, 3)]
    w_ud = gather(q_ud)

    wpo, mod, n1, proj, att = call(
        attend_body, "attention", ids, w_po + paid + [latents],
        [((4, feat, feat), BF16), ((4, wide), F32), ((tokens, feat), BF16),
         ((tokens, 3 * feat), BF16), ((tokens, feat), BF16)],
        flops=2 * tokens * feat * (3 * feat + 4 * length),
    )
    wout = wpo[3:4]
    ud_shape = ((4, 2, rows, feat), BF16)
    po_shape = ((4, rows, feat), BF16)
    res, gmid, gbr, gatt, gsum, gmod, *ud = call(
        mlp_body, "mlp", ids, w_ud + [wout, mod, latents, cotangent, att],
        [((slots, length, feat), BF16), ((slots, length, feat), F32), ((tokens, feat), BF16),
         ((tokens, feat), BF16), ((1, 6 * feat), F32), ((slots, 4 * feat), F32)] + [ud_shape] * 8,
        [
            pltpu.VMEM((4, feat, feat), BF16), pltpu.VMEM((hidden, feat), BF16),
            pltpu.VMEM((tokens, feat), BF16), pltpu.VMEM((tokens, hidden), BF16),
            pltpu.VMEM((length, hidden), F32), pltpu.VMEM((tokens, feat), BF16),
            pltpu.VMEM((tokens, hidden), BF16), pltpu.VMEM((feat, tokens), BF16),
            pltpu.VMEM((feat, feat), BF16), pltpu.VMEM((hidden, feat), BF16),
        ],
        flops=2 * tokens * feat * (6 * hidden + 2 * feat),
    )

    def scatter(pieces):
        keeps, sends = pieces[:4], pieces[4:]
        from_core = {m: move(sends[m], core) for m in (1, 3, 0, 2)}
        summed = {m: add_low(keeps[m], from_core[m]) for m in (1, 3, 0, 2)}
        to_zero = move(summed[1], first)
        to_two = move(summed[3], first)
        summed_two = add_low(summed[2], to_two)
        last = move(summed_two, second)
        base = add_low(summed[0], to_zero)
        total = [add_low(base[m], last[m]) for m in range(4)]
        own = add_low(total[0], *[move(total[m], levels[m]) for m in (1, 2, 3)])
        a = move(own, first)
        b = move(own, second)
        return [own, a, b, move(a, second)]

    g_ud = scatter(ud)
    gproj, bias, *po = call(
        functools.partial(attend_back_body, length=length), "attention_back", ids,
        [proj, gatt, att, gbr, n1, gsum],
        [((tokens, 3 * feat), BF16), ((1, 8 * feat), F32)] + [po_shape] * 8,
        [pltpu.VMEM((tokens, 4 * feat), BF16), pltpu.VMEM((2, feat, tokens), BF16),
         pltpu.VMEM((feat, feat), BF16)],
        flops=2 * tokens * feat * (4 * feat + 10 * length),
    )
    g_po = scatter(po)
    lgrad, gm = call(
        input_back_body, "input_back", ids, [gproj, wpo, latents, gmid, mod, gmod],
        [((slots, length, feat), BF16), ((slots, wide), F32)],
        flops=2 * tokens * feat * 3 * feat,
    )
    gm = gm.astype(BF16)

    gm_pair = jnp.concatenate([gm, move(gm, core)], axis=0)
    gm_all = [gm_pair] + [move(gm_pair, levels[m]) for m in (1, 2, 3)]
    back = call(
        cond_back_body, "cond_back", ids, gm_all + [modulation_weight],
        [((2 * slots, feat), F32)] * 4,
    )
    silu_pair = back[0]
    for m in (1, 2, 3):
        silu_pair = silu_pair + move(back[m], levels[m])
    grad_silu = silu_pair[:slots] + move(silu_pair[slots:], core)
    cond_full = cond.astype(F32)
    sig = 1.0 / (1.0 + jnp.exp(-cond_full))
    cond_grad = (grad_silu * (sig * (1.0 + cond_full * (1.0 - sig)))).astype(BF16)

    def over_dp(own):
        a = move(own, first)
        b = move(own, second)
        return [own, a, b, move(a, second)]

    c_every = over_dp(jnp.concatenate(c_all, axis=0))
    gm_every = over_dp(jnp.concatenate(gm_all, axis=0))
    g_mod_weight, g_mod_bias = call(
        mod_weight_body, "mod_weight", ids, c_every + gm_every,
        [((rows, wide), F32), ((1, wide), F32)],
    )

    bias = bias + move(bias, core)
    bias = bias + move(bias, levels[1])
    bias = bias + move(bias, levels[2])
    bias = bias + move(bias, first)
    bias = (bias + move(bias, second))[0]

    def share(vector):
        size = vector.shape[0] // 8
        return lax.dynamic_slice_in_dim(vector, f * size, size)

    g_proj, g_out = call(
        final_po_body, "final_po", ids, g_po, [((rows, 3 * feat), F32), ((rows, feat), F32)]
    )
    g_up, g_down = call(
        final_ud_body, "final_ud", ids, g_ud, [((rows, hidden), F32), ((4 * rows, feat), F32)]
    )
    return (
        res, lgrad, cond_grad, g_mod_weight, share(g_mod_bias[0]), g_proj, share(bias[: 2 * feat]),
        g_out, share(bias[2 * feat : 3 * feat]), g_up, share(bias[3 * feat : 7 * feat]),
        g_down, share(bias[7 * feat :]),
    )


def layer_norm(vector):
    row_mean = jnp.mean(vector, axis=-1, keepdims=True)
    centered = vector - row_mean
    variance = jnp.mean(centered * centered, axis=-1, keepdims=True)
    return centered * lax.rsqrt(variance + 1e-06)


def modulate(vector, offset, stretch):
    return layer_norm(vector) * (1.0 + stretch[:, None, :]) + offset[:, None, :]


def forward_pass(gathered, inputs, conditions):
    (
        modulation_weight,
        modulation_bias,
        projection_weight,
        query_value_bias,
        output_weight,
        output_bias,
        up_weight,
        up_bias,
        down_weight,
        down_bias,
    ) = gathered
    members, length, features = inputs.shape
    flat_rows = members * length
    cond_low = jax.nn.silu(conditions).astype(jnp.bfloat16)
    modulation = jnp.dot(cond_low, modulation_weight, preferred_element_type=jnp.float32)
    modulation = modulation + modulation_bias.astype(jnp.float32)
    pieces = jnp.split(modulation, 6, axis=-1)
    normed_one = (
        modulate(inputs, pieces[0], pieces[1]).astype(jnp.bfloat16).reshape(flat_rows, features)
    )
    bias_full = query_value_bias.astype(jnp.float32)
    joined_bias = jnp.concatenate(
        [bias_full[:features], jnp.zeros((features,), jnp.float32), bias_full[features:]]
    )
    projected = (
        jnp.dot(normed_one, projection_weight, preferred_element_type=jnp.float32) + joined_bias
    )
    projected = projected.astype(jnp.bfloat16).reshape(members, length, 3, HEADS, HEAD_DIM)
    queries = projected[:, :, 0]
    key_rows = projected[:, :, 1]
    values = projected[:, :, 2]
    scores = jnp.einsum(
        "bqhd,bkhd->bhqk", queries, key_rows, preferred_element_type=jnp.float32
    ) * HEAD_DIM ** (-0.5)
    row_max = jnp.max(scores, axis=-1, keepdims=True)
    exponent = jnp.exp(scores - row_max)
    row_total = jnp.sum(exponent, axis=-1, keepdims=True)
    probability = exponent / row_total
    log_total = row_max + jnp.log(row_total)
    attended = jnp.einsum(
        "bhqk,bkhd->bqhd",
        probability.astype(jnp.bfloat16),
        values,
        preferred_element_type=jnp.float32,
    )
    attended = attended.astype(jnp.bfloat16).reshape(flat_rows, features)
    branch = jnp.dot(
        attended, output_weight, preferred_element_type=jnp.float32
    ) + output_bias.astype(jnp.float32)
    branch = branch.reshape(members, length, features)
    middle = inputs + pieces[2][:, None, :] * branch
    normed_two = (
        modulate(middle, pieces[3], pieces[4]).astype(jnp.bfloat16).reshape(flat_rows, features)
    )
    pre_act = jnp.dot(normed_two, up_weight, preferred_element_type=jnp.float32) + up_bias.astype(
        jnp.float32
    )
    activated = jax.nn.gelu(pre_act, approximate=True).astype(jnp.bfloat16)
    mlp_out = jnp.dot(
        activated, down_weight, preferred_element_type=jnp.float32
    ) + down_bias.astype(jnp.float32)
    mlp_out = mlp_out.reshape(members, length, features)
    output = middle + pieces[5][:, None, :] * mlp_out
    return (
        output,
        cond_low,
        pieces,
        normed_one,
        queries,
        key_rows,
        values,
        log_total,
        attended,
        branch,
        middle,
        normed_two,
        pre_act,
        activated,
        mlp_out,
    )


def backward_pass(gathered, saved, inputs, conditions, upstream):
    (
        modulation_weight,
        modulation_bias,
        projection_weight,
        query_value_bias,
        output_weight,
        output_bias,
        up_weight,
        up_bias,
        down_weight,
        down_bias,
    ) = gathered
    (
        output,
        cond_low,
        pieces,
        normed_one,
        queries,
        key_rows,
        values,
        log_total,
        attended,
        branch,
        middle,
        normed_two,
        pre_act,
        activated,
        mlp_out,
    ) = saved
    members, length, features = inputs.shape
    flat_rows = members * length
    grad_gate_two = jnp.sum(upstream * mlp_out, axis=1)
    grad_mlp = (pieces[5][:, None, :] * upstream).astype(jnp.bfloat16).reshape(flat_rows, features)
    grad_down = jnp.einsum("nf,nd->fd", activated, grad_mlp, preferred_element_type=jnp.float32)
    grad_down_b = jnp.sum(grad_mlp.astype(jnp.float32), axis=0)
    grad_activated = jnp.einsum(
        "nd,fd->nf", grad_mlp, down_weight, preferred_element_type=jnp.float32
    )
    gelu_out, gelu_pull = jax.vjp(lambda vector: jax.nn.gelu(vector, approximate=True), pre_act)
    grad_pre = gelu_pull(grad_activated)[0].astype(jnp.bfloat16)
    grad_up = jnp.einsum("nd,nf->df", normed_two, grad_pre, preferred_element_type=jnp.float32)
    grad_up_b = jnp.sum(grad_pre.astype(jnp.float32), axis=0)
    grad_normed_two = jnp.einsum(
        "nf,df->nd", grad_pre, up_weight, preferred_element_type=jnp.float32
    )
    second_out, second_pull = jax.vjp(modulate, middle, pieces[3], pieces[4])
    grad_middle, grad_shift_two, grad_scale_two = second_pull(
        grad_normed_two.reshape(members, length, features)
    )
    grad_middle = grad_middle + upstream
    grad_gate_one = jnp.sum(grad_middle * branch, axis=1)
    grad_branch = (
        (pieces[2][:, None, :] * grad_middle).astype(jnp.bfloat16).reshape(flat_rows, features)
    )
    grad_output = jnp.einsum("nd,ne->de", attended, grad_branch, preferred_element_type=jnp.float32)
    grad_output_b = jnp.sum(grad_branch.astype(jnp.float32), axis=0)
    grad_attended = jnp.einsum(
        "ne,de->nd", grad_branch, output_weight, preferred_element_type=jnp.float32
    )
    grad_attended = grad_attended.astype(jnp.bfloat16).reshape(members, length, HEADS, HEAD_DIM)
    scale_factor = HEAD_DIM ** (-0.5)
    scores = (
        jnp.einsum("bqhd,bkhd->bhqk", queries, key_rows, preferred_element_type=jnp.float32)
        * scale_factor
    )
    probability = jnp.exp(scores - log_total)
    grad_values = jnp.einsum(
        "bhqk,bqhd->bkhd",
        probability.astype(jnp.bfloat16),
        grad_attended,
        preferred_element_type=jnp.float32,
    )
    grad_prob = jnp.einsum(
        "bqhd,bkhd->bhqk", grad_attended, values, preferred_element_type=jnp.float32
    )
    row_delta = jnp.sum(grad_prob * probability, axis=-1, keepdims=True)
    grad_scores = (probability * (grad_prob - row_delta)).astype(jnp.bfloat16)
    grad_queries = (
        jnp.einsum("bhqk,bkhd->bqhd", grad_scores, key_rows, preferred_element_type=jnp.float32)
        * scale_factor
    )
    grad_keys = (
        jnp.einsum("bhqk,bqhd->bkhd", grad_scores, queries, preferred_element_type=jnp.float32)
        * scale_factor
    )
    grad_projected = jnp.stack([grad_queries, grad_keys, grad_values], axis=2)
    grad_projected = grad_projected.astype(jnp.bfloat16).reshape(flat_rows, 3 * features)
    grad_projection = jnp.einsum(
        "nd,ne->de", normed_one, grad_projected, preferred_element_type=jnp.float32
    )
    column_sums = jnp.sum(grad_projected.astype(jnp.float32), axis=0)
    grad_query_value = jnp.concatenate([column_sums[:features], column_sums[2 * features :]])
    grad_normed_one = jnp.einsum(
        "ne,de->nd", grad_projected, projection_weight, preferred_element_type=jnp.float32
    )
    first_out, first_pull = jax.vjp(modulate, inputs, pieces[0], pieces[1])
    grad_input, grad_shift_one, grad_scale_one = first_pull(
        grad_normed_one.reshape(members, length, features)
    )
    grad_input = grad_input + grad_middle
    grad_modulation = jnp.concatenate(
        [
            grad_shift_one,
            grad_scale_one,
            grad_gate_one,
            grad_shift_two,
            grad_scale_two,
            grad_gate_two,
        ],
        axis=-1,
    ).astype(jnp.bfloat16)
    grad_mod_weight = jnp.einsum(
        "bc,be->ce", cond_low, grad_modulation, preferred_element_type=jnp.float32
    )
    grad_mod_bias = jnp.sum(grad_modulation.astype(jnp.float32), axis=0)
    grad_silu = jnp.einsum(
        "be,ce->bc", grad_modulation, modulation_weight, preferred_element_type=jnp.float32
    )
    silu_out, silu_pull = jax.vjp(jax.nn.silu, conditions)
    grad_conditions = silu_pull(grad_silu)[0]
    weight_grads = (
        grad_mod_weight,
        grad_mod_bias,
        grad_projection,
        grad_query_value,
        grad_output,
        grad_output_b,
        grad_up,
        grad_up_b,
        grad_down,
        grad_down_b,
    )
    return (weight_grads, grad_input, grad_conditions)


def on_device(
    latents,
    cond,
    counts,
    cotangent,
    modulation_weight,
    modulation_bias,
    projection_weight,
    query_value_bias,
    output_weight,
    output_bias,
    up_weight,
    up_bias,
    down_weight,
    down_bias,
):
    lat_slots = latents.shape[0]
    per_micro = lat_slots // MICRO
    alive_all = (jnp.arange(lat_slots) < counts[0]).astype(jnp.float32)
    kept = (
        lax.all_gather(modulation_weight, "fsdp", axis=0, tiled=True),
        lax.all_gather(modulation_bias, "fsdp", axis=0, tiled=True),
        lax.all_gather(projection_weight, "fsdp", axis=0, tiled=True),
        lax.all_gather(query_value_bias, "fsdp", axis=0, tiled=True),
        lax.all_gather(output_weight, "fsdp", axis=0, tiled=True),
        lax.all_gather(output_bias, "fsdp", axis=0, tiled=True),
        lax.all_gather(up_weight, "fsdp", axis=0, tiled=True),
        lax.all_gather(up_bias, "fsdp", axis=0, tiled=True),
        lax.all_gather(down_weight, "fsdp", axis=0, tiled=True),
        lax.all_gather(down_bias, "fsdp", axis=0, tiled=True),
    )
    outputs = []
    input_grads = []
    cond_grads = []
    totals = None
    for micro_index in range(MICRO):
        start = micro_index * per_micro
        inputs = latents[start : start + per_micro].astype(jnp.float32)
        conditions = cond[start : start + per_micro].astype(jnp.float32)
        alive_mask = alive_all[start : start + per_micro]
        saved = forward_pass(kept, inputs, conditions)
        outputs.append((saved[0] * alive_mask[:, None, None]).astype(jnp.bfloat16))
        upstream = (
            cotangent[start : start + per_micro].astype(jnp.float32) * alive_mask[:, None, None]
        )
        weight_grads, grad_input, grad_conditions = backward_pass(
            kept, saved, inputs, conditions, upstream
        )
        input_grads.append(grad_input.astype(jnp.bfloat16))
        cond_grads.append(grad_conditions.astype(jnp.bfloat16))
        totals = (
            weight_grads
            if totals is None
            else tuple((left + right for left, right in zip(totals, weight_grads)))
        )
    totals = (
        lax.psum_scatter(totals[0], "fsdp", scatter_dimension=0, tiled=True),
        lax.psum_scatter(totals[1], "fsdp", scatter_dimension=0, tiled=True),
        lax.psum_scatter(totals[2], "fsdp", scatter_dimension=0, tiled=True),
        lax.psum_scatter(totals[3], "fsdp", scatter_dimension=0, tiled=True),
        lax.psum_scatter(totals[4], "fsdp", scatter_dimension=0, tiled=True),
        lax.psum_scatter(totals[5], "fsdp", scatter_dimension=0, tiled=True),
        lax.psum_scatter(totals[6], "fsdp", scatter_dimension=0, tiled=True),
        lax.psum_scatter(totals[7], "fsdp", scatter_dimension=0, tiled=True),
        lax.psum_scatter(totals[8], "fsdp", scatter_dimension=0, tiled=True),
        lax.psum_scatter(totals[9], "fsdp", scatter_dimension=0, tiled=True),
    )
    totals = (
        lax.psum(totals[0].astype(jnp.bfloat16), "dp").astype(jnp.float32),
        lax.psum(totals[1].astype(jnp.bfloat16), "dp").astype(jnp.float32),
        lax.psum(totals[2].astype(jnp.bfloat16), "dp").astype(jnp.float32),
        lax.psum(totals[3].astype(jnp.bfloat16), "dp").astype(jnp.float32),
        lax.psum(totals[4].astype(jnp.bfloat16), "dp").astype(jnp.float32),
        lax.psum(totals[5].astype(jnp.bfloat16), "dp").astype(jnp.float32),
        lax.psum(totals[6].astype(jnp.bfloat16), "dp").astype(jnp.float32),
        lax.psum(totals[7].astype(jnp.bfloat16), "dp").astype(jnp.float32),
        lax.psum(totals[8].astype(jnp.bfloat16), "dp").astype(jnp.float32),
        lax.psum(totals[9].astype(jnp.bfloat16), "dp").astype(jnp.float32),
    )
    return (
        jnp.concatenate(outputs, axis=0),
        jnp.concatenate(input_grads, axis=0),
        jnp.concatenate(cond_grads, axis=0),
        totals[0],
        totals[1],
        totals[2],
        totals[3],
        totals[4],
        totals[5],
        totals[6],
        totals[7],
        totals[8],
        totals[9],
    )


def solution(mesh):
    small = mesh.shape["dp"] == 4 and mesh.shape["fsdp"] == 8
    program = on_device_blocks if small else on_device
    placed = (
        P(("dp", "fsdp"), None, None),
        P(("dp", "fsdp"), None),
        P(("dp", "fsdp")),
        P(("dp", "fsdp"), None, None),
        P("fsdp", None),
        P("fsdp"),
        P("fsdp", None),
        P("fsdp"),
        P("fsdp", None),
        P("fsdp"),
        P("fsdp", None),
        P("fsdp"),
        P("fsdp", None),
        P("fsdp"),
    )
    return jax.shard_map(
        program,
        mesh=mesh,
        in_specs=placed,
        out_specs=(
            P(("dp", "fsdp"), None, None),
            P(("dp", "fsdp"), None, None),
            P(("dp", "fsdp"), None),
            P("fsdp", None),
            P("fsdp"),
            P("fsdp", None),
            P("fsdp"),
            P("fsdp", None),
            P("fsdp"),
            P("fsdp", None),
            P("fsdp"),
            P("fsdp", None),
            P("fsdp"),
        ),
        check_vma=False,
    )
```

```python
import functools

import jax
import jax.numpy as jnp
from jax import lax
from jax.experimental import pallas as pl
from jax.experimental.pallas import tpu as pltpu
from jax.sharding import PartitionSpec as P

HEADS = 6
HEAD_DIM = 64
MICRO = 2
F32 = jnp.float32
BF16 = jnp.bfloat16
BOTH = ("dp", "fsdp")
NN = (((1,), (0,)), ((), ()))
NT = (((1,), (1,)), ((), ()))
TN = (((0,), (0,)), ((), ()))
LEVELS = (0, 2, 1, 3)


def dot(left, right, dims=NN):
    return lax.dot_general(left, right, dims, preferred_element_type=F32)


def smem():
    return pl.BlockSpec(memory_space=pltpu.SMEM)


def vmem():
    return pl.BlockSpec(memory_space=pltpu.VMEM)


def hbm():
    return pl.BlockSpec(memory_space=pltpu.HBM)


def call(body, name, ids, ins, outs, scratch=(), flops=0, limit=48, far=()):
    fixed = [] if ids is None else [ids]
    moved = sum(a.size * a.dtype.itemsize for a in ins) + sum(
        jnp.dtype(t).itemsize * functools.reduce(lambda a, b: a * b, s, 1) for s, t in outs
    )
    return pl.pallas_call(
        body,
        out_shape=[jax.ShapeDtypeStruct(s, t) for s, t in outs],
        in_specs=[smem()] * len(fixed) + [hbm() if i in far else vmem() for i in range(len(ins))],
        out_specs=[vmem()] * len(outs),
        scratch_shapes=list(scratch),
        compiler_params=pltpu.CompilerParams(vmem_limit_bytes=limit * 1024 * 1024),
        cost_estimate=pl.CostEstimate(flops=flops, bytes_accessed=moved, transcendentals=0),
        name=name,
    )(*fixed, *ins)


def offsets(ids):
    d, f = ids[0], ids[1]
    core = lax.rem(f, 2)
    first = 1 + core
    second = 2 - core
    return d, f, (0, first, second, 3), (0, second, first, 3)


def flip(a, b):
    return lax.bitwise_xor(a, b)


def pick_body(proj, outw, up, down, cond, q_all, c_in, sems):
    d = lax.axis_index("dp")
    rows, width = outw.shape
    at = pl.ds(pl.multiple_of(d * width, 128), width)
    at_proj = pl.ds(pl.multiple_of(lax.min(d, 2) * width, 128), width)
    q_po = q_all.at[pl.ds(0, rows), :]
    copies = [
        pltpu.make_async_copy(cond, c_in, sems.at[0]),
        pltpu.make_async_copy(up.at[:, at], q_all.at[pl.ds(rows, rows), :], sems.at[1]),
        pltpu.make_async_copy(
            down.at[pl.ds(pl.multiple_of(d * rows, 16), rows), :],
            q_all.at[pl.ds(2 * rows, rows), :],
            sems.at[2],
        ),
    ]
    for copy in copies:
        copy.start()

    @pl.when(d < 3)
    def _():
        copy = pltpu.make_async_copy(proj.at[:, at_proj], q_po, sems.at[3])
        copy.start()
        copy.wait()

    @pl.when(d == 3)
    def _():
        copy = pltpu.make_async_copy(outw, q_po, sems.at[3])
        copy.start()
        copy.wait()

    for copy in copies:
        copy.wait()
    c = c_in[...].astype(F32)
    c = c / (1.0 + jnp.exp(-c))
    blank = jnp.zeros((16 - c.shape[0], width), F32)
    q_all[3 * rows :, :] = jnp.concatenate([c, blank], axis=0).astype(BF16)


def one_hot(shape, shift):
    r = lax.broadcasted_iota(jnp.int32, shape, 0)
    c = lax.broadcasted_iota(jnp.int32, shape, 1)
    return jnp.where(c == r + shift, 1.0, 0.0).astype(BF16)


def prepare_body(wmod_in, f0, f1, f2, f3, f4, wmod, placed):
    f = lax.axis_index("fsdp")
    wmod[...] = wmod_in[...]
    rows = []
    for ref in (f0, f1, f2, f3, f4):
        size = ref.shape[0]
        rows.append(dot(ref[...].reshape(1, size), one_hot((size, 8 * size), f * size)))
    bias, b_qv, b_out, b_up, b_down = rows
    feat = b_out.shape[1]
    placed[0:1, :] = bias
    placed[1:2, :] = jnp.concatenate([b_up, b_qv], axis=1)
    placed[2:3, :] = jnp.concatenate([b_out, b_down, jnp.zeros((1, 4 * feat), F32)], axis=1)


def mod_body(ids, c_own, c_other, wmod, placed, keep_lo, keep_hi, send):
    f = ids[1]
    rows, wide = wmod.shape
    feat = c_own.shape[1]
    slots = c_own.shape[0] // 4
    r = lax.broadcasted_iota(jnp.int32, (feat, rows), 0)
    c = lax.broadcasted_iota(jnp.int32, (feat, rows), 1)
    select = jnp.where(r == c + f * rows, 1.0, 0.0).astype(BF16)
    stacked = jnp.concatenate([c_own[...].astype(F32), c_other[...].astype(F32)], axis=0)
    own = dot(stacked.astype(BF16), select).astype(BF16)
    part = dot(own, wmod[...]) + placed[0:1, :]
    for n in range(4):
        keep = (keep_lo, keep_lo, keep_hi, keep_hi)[n]
        keep[n % 2, 0:slots, :] = part[slots * n : slots * (n + 1)]
        send[n, 0:slots, :] = part[slots * (n + 4) : slots * (n + 5)]
        keep[n % 2, 2:4, :] = placed[1:3, :]
        send[n, 2:4, :] = placed[1:3, :]


def norm_parts(x):
    mean = jnp.mean(x, axis=-1, keepdims=True)
    centered = x - mean
    rstd = lax.rsqrt(jnp.mean(centered * centered, axis=-1, keepdims=True) + 1e-06)
    return centered * rstd, rstd


def lane_masks(rows):
    lane = lax.broadcasted_iota(jnp.int32, (rows, 2 * HEAD_DIM), 1)
    return lane < HEAD_DIM


def attend_body(
    ids, *refs,
):
    d, f, mine, theirs = offsets(ids)
    pieces, (m_proj, m_out, o_proj, o_out, p0, p1, lat, wpo, mod, n1, proj, att) = refs[:16], refs[16:]
    rows, feat = m_out.shape
    whole = ((m_proj, m_out), (o_proj, o_out))
    split = (pieces[:8], mine, f), (pieces[8:], theirs, flip(f, 1))
    for (p_ref, o_ref), (found, flips, base) in zip(whole, split):
        at = pl.multiple_of(base * rows, 16)
        for block in range(3):
            wpo[block, pl.ds(at, rows), :] = p_ref[:, block * feat : (block + 1) * feat]
        wpo[3, pl.ds(at, rows), :] = o_ref[...]
        for n, how in enumerate(flips):
            block = flip(d, how)
            for zm, get in ((2, found[n]), (1, found[4 + n].at[0]), (3, found[4 + n].at[1])):
                at = pl.multiple_of(flip(base, 2 * zm) * rows, 16)
                wpo[block, pl.ds(at, rows), :] = get[0:rows, :]
    mod[...] = p0[0] + p1[...]
    length = lat.shape[1]
    low_half = lane_masks(length)
    qv = mod[2:3, 4 * feat :]

    def one(i, carry):
        at = pl.multiple_of(i * length, 256)
        x = lat[i].astype(F32)
        xhat, rstd = norm_parts(x)
        row = mod[pl.ds(i, 1), :]
        n = (xhat * (1.0 + row[:, feat : 2 * feat]) + row[:, :feat]).astype(BF16)
        n1[pl.ds(at, length), :] = n
        proj[pl.ds(at, length), 0:feat] = (dot(n, wpo[0]) + qv[:, :feat]).astype(BF16)
        proj[pl.ds(at, length), feat : 2 * feat] = dot(n, wpo[1]).astype(BF16)
        proj[pl.ds(at, length), 2 * feat :] = (dot(n, wpo[2]) + qv[:, feat:]).astype(BF16)
        for pair in range(HEADS // 2):
            lo = pair * 2 * HEAD_DIM
            hi = lo + 2 * HEAD_DIM
            q = proj[pl.ds(at, length), lo:hi]
            k = proj[pl.ds(at, length), feat + lo : feat + hi]
            v = proj[pl.ds(at, length), 2 * feat + lo : 2 * feat + hi]
            zero = jnp.zeros_like(q)
            outs = []
            for side in range(2):
                q_one = jnp.where(low_half, q, zero) if side == 0 else jnp.where(low_half, zero, q)
                s = dot(q_one, k, NT) * HEAD_DIM ** (-0.5)
                e = jnp.exp(s - jnp.max(s, axis=-1, keepdims=True))
                inv = 1.0 / jnp.sum(e, axis=-1, keepdims=True)
                outs.append(dot((e * inv).astype(BF16), v))
            att[pl.ds(at, length), lo:hi] = jnp.where(low_half, outs[0], outs[1]).astype(BF16)
        return carry

    lax.fori_loop(0, lat.shape[0], one, 0)


def spread(tmp, at_row, dm, pieces, rows, f, slot=None):
    keep_odd, keep_even, send_odd, send_even = pieces
    keep = (keep_even, keep_odd)[dm % 2]
    swapped = (0, 2, 1, 3)[dm]
    send = (send_even, send_odd)[swapped % 2]
    for place, zm in enumerate(LEVELS):
        for ref, at, owner in (
            (keep, dm // 2, flip(f, 2 * zm)),
            (send, swapped // 2, flip(f, 2 * zm + 1)),
        ):
            piece = tmp[pl.ds(pl.multiple_of(at_row(owner), 16), rows), :]
            if slot is None:
                ref[at, place] = piece
            else:
                ref[at, place, slot] = piece


def mlp_body(
    ids, *refs,
):
    mlp_steps(ids, refs[:16], *refs[16:])


def mlp_steps(
    ids, pieces, m_up, m_down, o_up, o_down, wout, mod, lat, cot, att,
    res, gmid, gbr, gatt, gsum, gmod, k_odd, k_even, s_odd, s_even,
    wu, wd, n2s, acts, dgs, gmlps, gpres, n2t, tmp, tmpd,
):
    d, f, mine, theirs = offsets(ids)
    count = ids[2]
    rows, feat = m_up.shape[0], m_down.shape[1]
    hidden = wd.shape[0]
    blocks = hidden // feat
    whole = ((m_up, m_down), (o_up, o_down))
    split = (pieces[:8], mine, f), (pieces[8:], theirs, flip(f, 1))
    for (u_ref, d_ref), (found, flips, base) in zip(whole, split):
        at = pl.multiple_of(base * rows, 16)
        for block in range(blocks):
            wu[block, pl.ds(at, rows), :] = u_ref[:, block * feat : (block + 1) * feat]
        wd[pl.ds(pl.multiple_of(base * 4 * rows, 16), 4 * rows), :] = d_ref[...]
        for n, how in enumerate(flips):
            block = flip(d, how)
            for zm, get in ((2, found[n]), (1, found[4 + n].at[0]), (3, found[4 + n].at[1])):
                owner = flip(base, 2 * zm)
                wu[block, pl.ds(pl.multiple_of(owner * rows, 16), rows), :] = get[
                    rows : 2 * rows, :
                ]
                at = pl.multiple_of((owner * 4 + block) * rows, 16)
                wd[pl.ds(at, rows), :] = get[2 * rows : 3 * rows, :]
    length = lat.shape[1]
    bup = mod[2:3, : 4 * feat]
    bout = mod[3:4, :feat]
    bdown = mod[3:4, feat : 2 * feat]
    gsum[...] = jnp.zeros_like(gsum)

    def one(i, carry):
        at = pl.multiple_of(i * length, 256)
        part = pl.ds(at, length)
        row = mod[pl.ds(i, 1), :]
        gate_one, shift, scale, gate_two = (row[:, j * feat : (j + 1) * feat] for j in (2, 3, 4, 5))
        alive = jnp.where(i < count, 1.0, 0.0).astype(F32)
        branch = dot(att[part, :], wout[0]) + bout
        middle = lat[i].astype(F32) + gate_one * branch
        xhat, rstd = norm_parts(middle)
        n2 = (xhat * (1.0 + scale) + shift).astype(BF16)
        n2s[part, :] = n2
        mlp = jnp.zeros((length, feat), F32) + bdown
        for j in range(blocks):
            cols = slice(j * feat, (j + 1) * feat)
            v = dot(n2, wu[j]) + bup[:, cols]
            t = jnp.tanh(0.7978845608028654 * (v + 0.044715 * v * v * v))
            half = 0.5 * (1.0 + t)
            act = (v * half).astype(BF16)
            dgs[:, cols] = half + 0.5 * v * (1.0 - t * t) * (
                0.7978845608028654 * (1.0 + 0.134145 * v * v)
            )
            acts[part, cols] = act
            mlp = mlp + dot(act, wd[cols, :])
        res[i] = (alive * (middle + gate_two * mlp)).astype(BF16)
        upstream = alive * cot[i].astype(F32)
        g_gate_two = jnp.sum(upstream * mlp, axis=0, keepdims=True)
        gmlp = (gate_two * upstream).astype(BF16)
        gmlps[part, :] = gmlp
        gn = jnp.zeros((length, feat), F32)
        for j in range(blocks):
            cols = slice(j * feat, (j + 1) * feat)
            gpre = (dot(gmlp, wd[cols, :], NT) * dgs[:, cols]).astype(BF16)
            gpres[part, cols] = gpre
            gn = gn + dot(gpre, wu[j], NT)
            gsum[:, feat + j * feat : 2 * feat + j * feat] += jnp.sum(
                gpre.astype(F32), axis=0, keepdims=True
            )
        g_shift = jnp.sum(gn, axis=0, keepdims=True)
        g_scale = jnp.sum(gn * xhat, axis=0, keepdims=True)
        gx = gn * (1.0 + scale)
        gmiddle = upstream + rstd * (
            gx
            - jnp.mean(gx, axis=-1, keepdims=True)
            - xhat * jnp.mean(gx * xhat, axis=-1, keepdims=True)
        )
        gmid[i] = gmiddle
        g_gate_one = jnp.sum(gmiddle * branch, axis=0, keepdims=True)
        gbranch = (gate_one * gmiddle).astype(BF16)
        gbr[part, :] = gbranch
        gatt[part, :] = dot(gbranch, wout[0], NT).astype(BF16)
        gsum[:, 0:feat] += jnp.sum(gbranch.astype(F32), axis=0, keepdims=True)
        gsum[:, 5 * feat : 6 * feat] += jnp.sum(gmlp.astype(F32), axis=0, keepdims=True)
        gmod[pl.ds(i, 1), :] = jnp.concatenate([g_gate_one, g_shift, g_scale, g_gate_two], axis=1)
        return carry

    lax.fori_loop(0, lat.shape[0], one, 0)
    pieces = (k_odd, k_even, s_odd, s_even)
    for j in range(blocks):
        cols = slice(j * feat, (j + 1) * feat)
        tmpd[cols, :] = dot(acts[:, cols], gmlps[...], TN).astype(BF16)
    n2t[...] = n2s[...].T
    for dm in (1, 3, 0, 2):
        block = flip(d, mine[dm])
        spread(tmpd, lambda o: (o * 4 + block) * rows, dm, pieces, rows, f, 1)
        tmp[...] = dot(
            n2t[...], gpres[:, pl.ds(pl.multiple_of(block * feat, 128), feat)]
        ).astype(BF16)
        spread(tmp, lambda o: o * rows, dm, pieces, rows, f, 0)


def attend_back_body(
    ids, proj, gatt, att, gbr, n1, gsum, gproj, bias, k_odd, k_even, s_odd, s_even,
    gall, xts, tmp, *, length,
):
    d, f, mine, _ = offsets(ids)
    feat = att.shape[1]
    rows = k_odd.shape[2]
    low_half = lane_masks(length)

    def one(i, carry):
        part = pl.ds(pl.multiple_of(i * length, 256), length)
        for pair in range(HEADS // 2):
            lo = pair * 2 * HEAD_DIM
            hi = lo + 2 * HEAD_DIM
            q = proj[part, lo:hi]
            k = proj[part, feat + lo : feat + hi]
            v = proj[part, 2 * feat + lo : 2 * feat + hi]
            ga = gatt[part, lo:hi]
            zero = jnp.zeros_like(q)
            gq = jnp.zeros(q.shape, F32)
            gk = jnp.zeros(q.shape, F32)
            gv = jnp.zeros(q.shape, F32)
            for side in range(2):
                own = lambda a: (
                    jnp.where(low_half, a, zero) if side == 0 else jnp.where(low_half, zero, a)
                )
                q_one, ga_one = own(q), own(ga)
                s = dot(k, q_one, NT) * HEAD_DIM ** (-0.5)
                e = jnp.exp(s - jnp.max(s, axis=0, keepdims=True))
                prob = e * (1.0 / jnp.sum(e, axis=0, keepdims=True))
                gv = gv + dot(prob.astype(BF16), ga_one)
                gp = dot(v, ga_one, NT)
                delta = jnp.sum(gp * prob, axis=0, keepdims=True)
                gs = (prob * (gp - delta)).astype(BF16)
                gk = gk + dot(gs, q_one)
                gq = gq + dot(gs, own(k), TN)
            gall[part, lo:hi] = (gq * HEAD_DIM ** (-0.5)).astype(BF16)
            gall[part, feat + lo : feat + hi] = (gk * HEAD_DIM ** (-0.5)).astype(BF16)
            gall[part, 2 * feat + lo : 2 * feat + hi] = gv.astype(BF16)
        return carry

    lax.fori_loop(0, proj.shape[0] // length, one, 0)
    gproj[...] = gall[:, : 3 * feat]
    gall[:, 3 * feat :] = gbr[...]
    xts[0] = n1[...].T
    xts[1] = att[...].T
    pieces = (k_odd, k_even, s_odd, s_even)
    for dm in (1, 3, 0, 2):
        block = flip(d, mine[dm])
        tmp[...] = dot(
            xts[jnp.where(block == 3, 1, 0)],
            gall[:, pl.ds(pl.multiple_of(block * feat, 128), feat)],
        ).astype(BF16)
        spread(tmp, lambda o: o * rows, dm, pieces, rows, f)
    bias[:, 0:feat] = jnp.sum(gall[:, 0:feat].astype(F32), axis=0, keepdims=True)
    bias[:, feat : 2 * feat] = jnp.sum(
        gall[:, 2 * feat : 3 * feat].astype(F32), axis=0, keepdims=True
    )
    bias[:, 2 * feat :] = gsum[...]


def input_back_body(ids, gproj, wpo, lat, gmid, mod, gmod, bias, lgrad, gm, full):
    length = lat.shape[1]
    feat = lat.shape[2]

    def one(i, carry):
        part = pl.ds(pl.multiple_of(i * length, 256), length)
        row = mod[pl.ds(i, 1), :]
        xhat, rstd = norm_parts(lat[i].astype(F32))
        gn = dot(gproj[part, 0:feat], wpo[0], NT)
        gn = gn + dot(gproj[part, feat : 2 * feat], wpo[1], NT)
        gn = gn + dot(gproj[part, 2 * feat :], wpo[2], NT)
        g_shift = jnp.sum(gn, axis=0, keepdims=True)
        g_scale = jnp.sum(gn * xhat, axis=0, keepdims=True)
        gx = gn * (1.0 + row[:, feat : 2 * feat])
        lgrad[i] = (
            gmid[i]
            + rstd
            * (
                gx
                - jnp.mean(gx, axis=-1, keepdims=True)
                - xhat * jnp.mean(gx * xhat, axis=-1, keepdims=True)
            )
        ).astype(BF16)
        full[pl.ds(i, 1), : 6 * feat] = jnp.concatenate(
            [g_shift, g_scale, gmod[pl.ds(i, 1), :]], axis=1
        )
        return carry

    lax.fori_loop(0, lat.shape[0], one, 0)
    full[0:1, 6 * feat :] = bias[:, : 4 * feat]
    full[1:2, 6 * feat :] = bias[:, 4 * feat :]
    gm[...] = full[...].astype(BF16)


def cond_back_body(ids, g0, g2, g1, g3, wmod, lo, hi):
    f = ids[1]
    rows, wide = wmod.shape
    place = one_hot((rows, lo.shape[2]), f * rows)
    lo[...] = jnp.zeros_like(lo)
    hi[...] = jnp.zeros_like(hi)
    for ref, out, at in ((g0, lo, 0), (g2, lo, 1), (g1, hi, 0), (g3, hi, 1)):
        part = dot(ref[:, :wide], wmod[...], NT).astype(BF16)
        out[at, 0 : part.shape[0], :] = dot(part, place).astype(BF16)


def mod_weight_body(ids, e0, e1, e2, e3, wgrad, bgrad):
    f = ids[1]
    rows, wide = wgrad.shape
    feat = wide // 6
    grad_wide = e0.shape[1] - feat
    select = one_hot((rows, feat), f * rows)
    total = None
    sums = None
    for ref in (e0, e1, e2, e3):
        own = dot(select, ref[:, grad_wide:], NT).astype(BF16)
        term = dot(own, ref[:, :wide])
        total = term if total is None else total + term
        low = ref[:, :grad_wide].astype(F32)
        sums = low if sums is None else sums + low
    wgrad[...] = total
    low = sums[:, wide:]
    odd = lax.broadcasted_iota(jnp.int32, low.shape, 0) % 2 == 1
    bgrad[:, :wide] = jnp.sum(sums[:, :wide], axis=0, keepdims=True)
    bgrad[:, wide : wide + 4 * feat] = jnp.sum(jnp.where(odd, 0.0, low), axis=0, keepdims=True)
    bgrad[:, wide + 4 * feat :] = jnp.sum(jnp.where(odd, low, 0.0), axis=0, keepdims=True)


def merge_body(ids, keep_ud, got_ud, keep_po, got_po, out):
    rows = keep_po.shape[2]
    for at in range(out.shape[0]):
        for place in range(out.shape[1]):
            out[at, place, 0:rows] = add_low(keep_po[at, place], got_po[at, place])
            for slot in range(2):
                out[at, place, (1 + slot) * rows : (2 + slot) * rows] = add_low(
                    keep_ud[at, place, slot], got_ud[at, place, slot]
                )


def join_far_body(ids, base, part, back, out):
    size = base.shape[1]
    for at in range(2):
        out[at, 0:size] = add_low(base[2 + at], part[2 + at])
        out[at, size:] = back[at]


def join_near_body(ids, base, part, back, got, out):
    size = base.shape[1]
    for at in range(2):
        out[at, 0:size] = add_low(base[at], part[at], got[at, 0:size])
        out[at, size:] = add_low(back[at], got[at, size:])


def final_body(ids, g0, g1, g2, g3, gp, go, gu, gd):
    d, _, mine, _ = offsets(ids)
    rows, feat = go.shape
    for ref, how in zip((g0, g1, g2, g3), mine):
        block = flip(d, how)

        @pl.when(block < 3)
        def _():
            at = pl.multiple_of(lax.min(block, 2) * feat, 128)
            gp[:, pl.ds(at, feat)] = ref[0:rows, :].astype(F32)

        @pl.when(block == 3)
        def _():
            go[...] = ref[0:rows, :].astype(F32)

        gu[:, pl.ds(pl.multiple_of(block * feat, 128), feat)] = ref[rows : 2 * rows, :].astype(F32)
        gd[pl.ds(pl.multiple_of(block * rows, 16), rows), :] = ref[2 * rows : 3 * rows, :].astype(F32)


def routes():
    core, first, second = [], [], []
    levels = {1: [], 2: []}
    for d in range(4):
        for f in range(8):
            i = d * 8 + f
            core.append((i, i ^ 1))
            a = 1 if f % 2 == 0 else 2
            first.append((i, (d ^ a) * 8 + f))
            second.append((i, (d ^ (3 - a)) * 8 + f))
            for m in levels:
                levels[m].append((i, d * 8 + (f ^ (2 * m))))
    return core, first, second, levels


def add_low(*parts):
    total = parts[0].astype(F32)
    for part in parts[1:]:
        total = total + part.astype(F32)
    return total.astype(BF16)


def on_device_blocks(
    latents, cond, counts, cotangent, modulation_weight, modulation_bias, projection_weight,
    query_value_bias, output_weight, output_bias, up_weight, up_bias, down_weight, down_bias,
):
    core, first, second, levels = routes()

    def move(x, route):
        return lax.ppermute(x, BOTH, route)

    slots, length, feat = latents.shape
    rows = projection_weight.shape[0]
    hidden = up_weight.shape[1]
    wide = modulation_weight.shape[1]
    tokens = slots * length
    d = lax.axis_index("dp")
    f = lax.axis_index("fsdp")
    ids = jnp.stack([d, f, counts[0]]).astype(jnp.int32)

    def after(x, *earlier):
        return lax.optimization_barrier((x,) + earlier)[0]

    (q_all,) = call(
        pick_body, "pick", None,
        [projection_weight, output_weight, up_weight, down_weight, cond],
        [((3 * rows + 16, feat), BF16)],
        [pltpu.VMEM((slots, feat), BF16), pltpu.SemaphoreType.DMA((4,))],
        far=(0, 1, 2, 3, 4), limit=60,
    )

    def over_dp(own):
        a = move(own, first)
        b = move(own, second)
        return [own, a, b, move(a, second)]

    whole = [projection_weight, output_weight, up_weight, down_weight]
    w_whole = whole + [move(x, core) for x in whole]
    biases = [modulation_bias, query_value_bias, output_bias, up_bias, down_bias]
    wmod, placed = call(
        prepare_body, "prepare", None, [modulation_weight] + biases,
        [((rows, wide), BF16), ((3, wide), F32)],
    )
    q_far = move(q_all, levels[2])
    ready = (placed, *w_whole[4:])
    q_near = move(after(q_all, q_far, *ready), levels[1])
    q_both = move(after(q_far, *ready), levels[1])
    a_far, b_far = move(q_far, first), move(q_far, second)
    c_own = [x[3 * rows : 3 * rows + slots] for x in (q_all, q_far, q_near, q_both)]
    c_own = after(jnp.concatenate(c_own), a_far, b_far)
    c_other = move(c_own, core)
    near = jnp.stack([q_near[: 3 * rows], q_both[: 3 * rows]])
    keep_lo, keep_hi, sent = call(
        mod_body, "modulation", ids, [c_own, c_other, wmod, placed],
        [((2, 4, wide), F32)] * 2 + [((4, 4, wide), F32)],
    )
    ab_far = move(a_far, second)
    got = after(move(sent, core), ab_far)
    paid_hi = keep_hi + got[2:]
    paid_lo = keep_lo + got[:2]
    paid_lo = paid_lo + move(paid_hi, levels[1])
    paid_far = move(paid_lo[1], levels[2])
    a_near, b_near = move(near, first), move(near, second)
    ab_near = move(after(a_near, paid_far), second)
    w_all = [q_far, a_far, b_far, ab_far, near, a_near, b_near, ab_near]
    w_all = w_all + [move(x, core) for x in w_all]

    wpo, mod, n1, proj, att = call(
        attend_body, "attention", ids,
        w_all + [w_whole[k] for k in (0, 1, 4, 5)] + [paid_lo, paid_far, latents],
        [((4, feat, feat), BF16), ((4, wide), F32), ((tokens, feat), BF16),
         ((tokens, 3 * feat), BF16), ((tokens, feat), BF16)],
        flops=2 * tokens * feat * (3 * feat + 4 * length),
    )
    wout = wpo[3:4]
    ud_shape = ((2, 4, 2, rows, feat), BF16)
    po_shape = ((2, 4, rows, feat), BF16)
    res, gmid, gbr, gatt, gsum, gmod, ud_odd, ud_even, ud_odd_out, ud_even_out = call(
        mlp_body, "mlp", ids,
        w_all + [w_whole[k] for k in (2, 3, 6, 7)] + [wout, mod, latents, cotangent, att],
        [((slots, length, feat), BF16), ((slots, length, feat), F32), ((tokens, feat), BF16),
         ((tokens, feat), BF16), ((1, 6 * feat), F32), ((slots, 4 * feat), F32)] + [ud_shape] * 4,
        [
            pltpu.VMEM((4, feat, feat), BF16), pltpu.VMEM((hidden, feat), BF16),
            pltpu.VMEM((tokens, feat), BF16), pltpu.VMEM((tokens, hidden), BF16),
            pltpu.VMEM((length, hidden), F32), pltpu.VMEM((tokens, feat), BF16),
            pltpu.VMEM((tokens, hidden), BF16), pltpu.VMEM((feat, tokens), BF16),
            pltpu.VMEM((feat, feat), BF16), pltpu.VMEM((hidden, feat), BF16),
        ],
        flops=2 * tokens * feat * (6 * hidden + 2 * feat),
    )
    ud_odd_in = move(ud_odd_out, core)
    ud_even_in = move(ud_even_out, core)
    gproj, bias, po_odd, po_even, po_odd_out, po_even_out = call(
        functools.partial(attend_back_body, length=length), "attention_back", ids,
        [proj, gatt, att, gbr, n1, gsum],
        [((tokens, 3 * feat), BF16), ((1, 8 * feat), F32)] + [po_shape] * 4,
        [pltpu.VMEM((tokens, 4 * feat), BF16), pltpu.VMEM((2, feat, tokens), BF16),
         pltpu.VMEM((feat, feat), BF16)],
        flops=2 * tokens * feat * (4 * feat + 10 * length),
    )
    po_odd_in = move(po_odd_out, core)
    po_even_in = move(po_even_out, core)
    all_shape = ((2, 4, 3 * rows, feat), BF16)
    (odd,) = call(merge_body, "merge_odd", ids, [ud_odd, ud_odd_in, po_odd, po_odd_in], [all_shape])
    got = move(odd, first)
    (even,) = call(
        merge_body, "merge_even", ids, [ud_even, ud_even_in, po_even, po_even_in], [all_shape]
    )
    lgrad, gm = call(
        input_back_body, "input_back", ids, [after(gproj, even), wpo, latents, gmid, mod, gmod, bias],
        [((slots, length, feat), BF16), ((slots, 10 * feat), BF16)],
        [pltpu.VMEM((slots, 10 * feat), F32)],
        flops=2 * tokens * feat * 3 * feat,
    )

    gm_pair = jnp.concatenate([gm, move(gm, core)], axis=0)
    gm_far = move(gm_pair, levels[2])
    turned = add_low(even[1], after(got[1], gm_far))
    gm_all = [
        gm_pair, gm_far,
        move(after(gm_pair, turned), levels[1]), move(after(gm_far, turned), levels[1]),
    ]
    part = move(turned, second)
    base = add_low(even[0], got[0])
    every = jnp.concatenate(
        [
            jnp.concatenate(gm_all, axis=0),
            jnp.concatenate(
                [x[slots * n : slots * (n + 1)] for n in range(4) for x in (c_own, c_other)]
            ),
        ],
        axis=1,
    )
    back_lo, back_hi = call(
        cond_back_body, "cond_back", ids, gm_all + [modulation_weight],
        [((2, 16, feat), BF16)] * 2,
    )

    pair_shape = ((2, 3 * rows + 16, feat), BF16)
    (turned,) = call(join_far_body, "join_far", ids, [base, part, back_hi], [pair_shape])
    got = move(turned, levels[1])
    every = after(every, turned)
    e_first, e_second = move(every, first), move(every, second)
    (base,) = call(join_near_body, "join_near", ids, [base, part, back_lo, got], [pair_shape])
    e_both = move(after(e_first, base), second)
    g_mod_weight, sums = call(
        mod_weight_body, "mod_weight", ids, [every, e_first, e_second, e_both],
        [((rows, wide), F32), ((1, wide + 8 * feat), F32)],
    )
    total = add_low(base[0], after(move(base[1], levels[2]), g_mod_weight))
    a_total, b_total = move(total, first), move(total, second)
    sums = after(sums[0], total)

    def share(at, size):
        size = size // 8
        return lax.dynamic_slice_in_dim(sums, at + f * size, size)

    g_biases = [
        share(0, wide), share(wide, 2 * feat), share(wide + 2 * feat, feat),
        share(wide + 3 * feat, hidden), share(wide + 7 * feat, feat),
    ]
    shares = [total, a_total, b_total, move(after(a_total, *g_biases), second)]
    silu_pair = total[3 * rows : 3 * rows + 2 * slots].astype(F32)
    silu_other = after(total, a_total, b_total)[3 * rows + slots : 3 * rows + 2 * slots]
    grad_silu = silu_pair[:slots] + move(silu_other, core).astype(F32)
    cond_full = cond.astype(F32)
    sig = 1.0 / (1.0 + jnp.exp(-cond_full))
    cond_grad = (grad_silu * (sig * (1.0 + cond_full * (1.0 - sig)))).astype(BF16)
    g_proj, g_out, g_up, g_down = call(
        final_body, "final", ids, shares,
        [((rows, 3 * feat), F32), ((rows, feat), F32), ((rows, hidden), F32),
         ((4 * rows, feat), F32)],
    )
    return (
        res, lgrad, cond_grad, g_mod_weight, g_biases[0], g_proj, g_biases[1],
        g_out, g_biases[2], g_up, g_biases[3], g_down, g_biases[4],
    )


def layer_norm(vector):
    row_mean = jnp.mean(vector, axis=-1, keepdims=True)
    centered = vector - row_mean
    variance = jnp.mean(centered * centered, axis=-1, keepdims=True)
    return centered * lax.rsqrt(variance + 1e-06)


def modulate(vector, offset, stretch):
    return layer_norm(vector) * (1.0 + stretch[:, None, :]) + offset[:, None, :]


def forward_pass(gathered, inputs, conditions):
    (
        modulation_weight,
        modulation_bias,
        projection_weight,
        query_value_bias,
        output_weight,
        output_bias,
        up_weight,
        up_bias,
        down_weight,
        down_bias,
    ) = gathered
    members, length, features = inputs.shape
    flat_rows = members * length
    cond_low = jax.nn.silu(conditions).astype(jnp.bfloat16)
    modulation = jnp.dot(cond_low, modulation_weight, preferred_element_type=jnp.float32)
    modulation = modulation + modulation_bias.astype(jnp.float32)
    pieces = jnp.split(modulation, 6, axis=-1)
    normed_one = (
        modulate(inputs, pieces[0], pieces[1]).astype(jnp.bfloat16).reshape(flat_rows, features)
    )
    bias_full = query_value_bias.astype(jnp.float32)
    joined_bias = jnp.concatenate(
        [bias_full[:features], jnp.zeros((features,), jnp.float32), bias_full[features:]]
    )
    projected = (
        jnp.dot(normed_one, projection_weight, preferred_element_type=jnp.float32) + joined_bias
    )
    projected = projected.astype(jnp.bfloat16).reshape(members, length, 3, HEADS, HEAD_DIM)
    queries = projected[:, :, 0]
    key_rows = projected[:, :, 1]
    values = projected[:, :, 2]
    scores = jnp.einsum(
        "bqhd,bkhd->bhqk", queries, key_rows, preferred_element_type=jnp.float32
    ) * HEAD_DIM ** (-0.5)
    row_max = jnp.max(scores, axis=-1, keepdims=True)
    exponent = jnp.exp(scores - row_max)
    row_total = jnp.sum(exponent, axis=-1, keepdims=True)
    probability = exponent / row_total
    log_total = row_max + jnp.log(row_total)
    attended = jnp.einsum(
        "bhqk,bkhd->bqhd",
        probability.astype(jnp.bfloat16),
        values,
        preferred_element_type=jnp.float32,
    )
    attended = attended.astype(jnp.bfloat16).reshape(flat_rows, features)
    branch = jnp.dot(
        attended, output_weight, preferred_element_type=jnp.float32
    ) + output_bias.astype(jnp.float32)
    branch = branch.reshape(members, length, features)
    middle = inputs + pieces[2][:, None, :] * branch
    normed_two = (
        modulate(middle, pieces[3], pieces[4]).astype(jnp.bfloat16).reshape(flat_rows, features)
    )
    pre_act = jnp.dot(normed_two, up_weight, preferred_element_type=jnp.float32) + up_bias.astype(
        jnp.float32
    )
    activated = jax.nn.gelu(pre_act, approximate=True).astype(jnp.bfloat16)
    mlp_out = jnp.dot(
        activated, down_weight, preferred_element_type=jnp.float32
    ) + down_bias.astype(jnp.float32)
    mlp_out = mlp_out.reshape(members, length, features)
    output = middle + pieces[5][:, None, :] * mlp_out
    return (
        output,
        cond_low,
        pieces,
        normed_one,
        queries,
        key_rows,
        values,
        log_total,
        attended,
        branch,
        middle,
        normed_two,
        pre_act,
        activated,
        mlp_out,
    )


def backward_pass(gathered, saved, inputs, conditions, upstream):
    (
        modulation_weight,
        modulation_bias,
        projection_weight,
        query_value_bias,
        output_weight,
        output_bias,
        up_weight,
        up_bias,
        down_weight,
        down_bias,
    ) = gathered
    (
        output,
        cond_low,
        pieces,
        normed_one,
        queries,
        key_rows,
        values,
        log_total,
        attended,
        branch,
        middle,
        normed_two,
        pre_act,
        activated,
        mlp_out,
    ) = saved
    members, length, features = inputs.shape
    flat_rows = members * length
    grad_gate_two = jnp.sum(upstream * mlp_out, axis=1)
    grad_mlp = (pieces[5][:, None, :] * upstream).astype(jnp.bfloat16).reshape(flat_rows, features)
    grad_down = jnp.einsum("nf,nd->fd", activated, grad_mlp, preferred_element_type=jnp.float32)
    grad_down_b = jnp.sum(grad_mlp.astype(jnp.float32), axis=0)
    grad_activated = jnp.einsum(
        "nd,fd->nf", grad_mlp, down_weight, preferred_element_type=jnp.float32
    )
    gelu_out, gelu_pull = jax.vjp(lambda vector: jax.nn.gelu(vector, approximate=True), pre_act)
    grad_pre = gelu_pull(grad_activated)[0].astype(jnp.bfloat16)
    grad_up = jnp.einsum("nd,nf->df", normed_two, grad_pre, preferred_element_type=jnp.float32)
    grad_up_b = jnp.sum(grad_pre.astype(jnp.float32), axis=0)
    grad_normed_two = jnp.einsum(
        "nf,df->nd", grad_pre, up_weight, preferred_element_type=jnp.float32
    )
    second_out, second_pull = jax.vjp(modulate, middle, pieces[3], pieces[4])
    grad_middle, grad_shift_two, grad_scale_two = second_pull(
        grad_normed_two.reshape(members, length, features)
    )
    grad_middle = grad_middle + upstream
    grad_gate_one = jnp.sum(grad_middle * branch, axis=1)
    grad_branch = (
        (pieces[2][:, None, :] * grad_middle).astype(jnp.bfloat16).reshape(flat_rows, features)
    )
    grad_output = jnp.einsum("nd,ne->de", attended, grad_branch, preferred_element_type=jnp.float32)
    grad_output_b = jnp.sum(grad_branch.astype(jnp.float32), axis=0)
    grad_attended = jnp.einsum(
        "ne,de->nd", grad_branch, output_weight, preferred_element_type=jnp.float32
    )
    grad_attended = grad_attended.astype(jnp.bfloat16).reshape(members, length, HEADS, HEAD_DIM)
    scale_factor = HEAD_DIM ** (-0.5)
    scores = (
        jnp.einsum("bqhd,bkhd->bhqk", queries, key_rows, preferred_element_type=jnp.float32)
        * scale_factor
    )
    probability = jnp.exp(scores - log_total)
    grad_values = jnp.einsum(
        "bhqk,bqhd->bkhd",
        probability.astype(jnp.bfloat16),
        grad_attended,
        preferred_element_type=jnp.float32,
    )
    grad_prob = jnp.einsum(
        "bqhd,bkhd->bhqk", grad_attended, values, preferred_element_type=jnp.float32
    )
    row_delta = jnp.sum(grad_prob * probability, axis=-1, keepdims=True)
    grad_scores = (probability * (grad_prob - row_delta)).astype(jnp.bfloat16)
    grad_queries = (
        jnp.einsum("bhqk,bkhd->bqhd", grad_scores, key_rows, preferred_element_type=jnp.float32)
        * scale_factor
    )
    grad_keys = (
        jnp.einsum("bhqk,bqhd->bkhd", grad_scores, queries, preferred_element_type=jnp.float32)
        * scale_factor
    )
    grad_projected = jnp.stack([grad_queries, grad_keys, grad_values], axis=2)
    grad_projected = grad_projected.astype(jnp.bfloat16).reshape(flat_rows, 3 * features)
    grad_projection = jnp.einsum(
        "nd,ne->de", normed_one, grad_projected, preferred_element_type=jnp.float32
    )
    column_sums = jnp.sum(grad_projected.astype(jnp.float32), axis=0)
    grad_query_value = jnp.concatenate([column_sums[:features], column_sums[2 * features :]])
    grad_normed_one = jnp.einsum(
        "ne,de->nd", grad_projected, projection_weight, preferred_element_type=jnp.float32
    )
    first_out, first_pull = jax.vjp(modulate, inputs, pieces[0], pieces[1])
    grad_input, grad_shift_one, grad_scale_one = first_pull(
        grad_normed_one.reshape(members, length, features)
    )
    grad_input = grad_input + grad_middle
    grad_modulation = jnp.concatenate(
        [
            grad_shift_one,
            grad_scale_one,
            grad_gate_one,
            grad_shift_two,
            grad_scale_two,
            grad_gate_two,
        ],
        axis=-1,
    ).astype(jnp.bfloat16)
    grad_mod_weight = jnp.einsum(
        "bc,be->ce", cond_low, grad_modulation, preferred_element_type=jnp.float32
    )
    grad_mod_bias = jnp.sum(grad_modulation.astype(jnp.float32), axis=0)
    grad_silu = jnp.einsum(
        "be,ce->bc", grad_modulation, modulation_weight, preferred_element_type=jnp.float32
    )
    silu_out, silu_pull = jax.vjp(jax.nn.silu, conditions)
    grad_conditions = silu_pull(grad_silu)[0]
    weight_grads = (
        grad_mod_weight,
        grad_mod_bias,
        grad_projection,
        grad_query_value,
        grad_output,
        grad_output_b,
        grad_up,
        grad_up_b,
        grad_down,
        grad_down_b,
    )
    return (weight_grads, grad_input, grad_conditions)


def on_device(
    latents,
    cond,
    counts,
    cotangent,
    modulation_weight,
    modulation_bias,
    projection_weight,
    query_value_bias,
    output_weight,
    output_bias,
    up_weight,
    up_bias,
    down_weight,
    down_bias,
):
    lat_slots = latents.shape[0]
    per_micro = lat_slots // MICRO
    alive_all = (jnp.arange(lat_slots) < counts[0]).astype(jnp.float32)
    kept = (
        lax.all_gather(modulation_weight, "fsdp", axis=0, tiled=True),
        lax.all_gather(modulation_bias, "fsdp", axis=0, tiled=True),
        lax.all_gather(projection_weight, "fsdp", axis=0, tiled=True),
        lax.all_gather(query_value_bias, "fsdp", axis=0, tiled=True),
        lax.all_gather(output_weight, "fsdp", axis=0, tiled=True),
        lax.all_gather(output_bias, "fsdp", axis=0, tiled=True),
        lax.all_gather(up_weight, "fsdp", axis=0, tiled=True),
        lax.all_gather(up_bias, "fsdp", axis=0, tiled=True),
        lax.all_gather(down_weight, "fsdp", axis=0, tiled=True),
        lax.all_gather(down_bias, "fsdp", axis=0, tiled=True),
    )
    outputs = []
    input_grads = []
    cond_grads = []
    totals = None
    for micro_index in range(MICRO):
        start = micro_index * per_micro
        inputs = latents[start : start + per_micro].astype(jnp.float32)
        conditions = cond[start : start + per_micro].astype(jnp.float32)
        alive_mask = alive_all[start : start + per_micro]
        saved = forward_pass(kept, inputs, conditions)
        outputs.append((saved[0] * alive_mask[:, None, None]).astype(jnp.bfloat16))
        upstream = (
            cotangent[start : start + per_micro].astype(jnp.float32) * alive_mask[:, None, None]
        )
        weight_grads, grad_input, grad_conditions = backward_pass(
            kept, saved, inputs, conditions, upstream
        )
        input_grads.append(grad_input.astype(jnp.bfloat16))
        cond_grads.append(grad_conditions.astype(jnp.bfloat16))
        totals = (
            weight_grads
            if totals is None
            else tuple((left + right for left, right in zip(totals, weight_grads)))
        )
    totals = (
        lax.psum_scatter(totals[0], "fsdp", scatter_dimension=0, tiled=True),
        lax.psum_scatter(totals[1], "fsdp", scatter_dimension=0, tiled=True),
        lax.psum_scatter(totals[2], "fsdp", scatter_dimension=0, tiled=True),
        lax.psum_scatter(totals[3], "fsdp", scatter_dimension=0, tiled=True),
        lax.psum_scatter(totals[4], "fsdp", scatter_dimension=0, tiled=True),
        lax.psum_scatter(totals[5], "fsdp", scatter_dimension=0, tiled=True),
        lax.psum_scatter(totals[6], "fsdp", scatter_dimension=0, tiled=True),
        lax.psum_scatter(totals[7], "fsdp", scatter_dimension=0, tiled=True),
        lax.psum_scatter(totals[8], "fsdp", scatter_dimension=0, tiled=True),
        lax.psum_scatter(totals[9], "fsdp", scatter_dimension=0, tiled=True),
    )
    totals = (
        lax.psum(totals[0].astype(jnp.bfloat16), "dp").astype(jnp.float32),
        lax.psum(totals[1].astype(jnp.bfloat16), "dp").astype(jnp.float32),
        lax.psum(totals[2].astype(jnp.bfloat16), "dp").astype(jnp.float32),
        lax.psum(totals[3].astype(jnp.bfloat16), "dp").astype(jnp.float32),
        lax.psum(totals[4].astype(jnp.bfloat16), "dp").astype(jnp.float32),
        lax.psum(totals[5].astype(jnp.bfloat16), "dp").astype(jnp.float32),
        lax.psum(totals[6].astype(jnp.bfloat16), "dp").astype(jnp.float32),
        lax.psum(totals[7].astype(jnp.bfloat16), "dp").astype(jnp.float32),
        lax.psum(totals[8].astype(jnp.bfloat16), "dp").astype(jnp.float32),
        lax.psum(totals[9].astype(jnp.bfloat16), "dp").astype(jnp.float32),
    )
    return (
        jnp.concatenate(outputs, axis=0),
        jnp.concatenate(input_grads, axis=0),
        jnp.concatenate(cond_grads, axis=0),
        totals[0],
        totals[1],
        totals[2],
        totals[3],
        totals[4],
        totals[5],
        totals[6],
        totals[7],
        totals[8],
        totals[9],
    )


def solution(mesh):
    small = mesh.shape["dp"] == 4 and mesh.shape["fsdp"] == 8
    program = on_device_blocks if small else on_device
    placed = (
        P(("dp", "fsdp"), None, None),
        P(("dp", "fsdp"), None),
        P(("dp", "fsdp")),
        P(("dp", "fsdp"), None, None),
        P("fsdp", None),
        P("fsdp"),
        P("fsdp", None),
        P("fsdp"),
        P("fsdp", None),
        P("fsdp"),
        P("fsdp", None),
        P("fsdp"),
        P("fsdp", None),
        P("fsdp"),
    )
    return jax.shard_map(
        program,
        mesh=mesh,
        in_specs=placed,
        out_specs=(
            P(("dp", "fsdp"), None, None),
            P(("dp", "fsdp"), None, None),
            P(("dp", "fsdp"), None),
            P("fsdp", None),
            P("fsdp"),
            P("fsdp", None),
            P("fsdp"),
            P("fsdp", None),
            P("fsdp"),
            P("fsdp", None),
            P("fsdp"),
            P("fsdp", None),
            P("fsdp"),
        ),
        check_vma=False,
    )
```

```python
import functools

import jax
import jax.numpy as jnp
from jax import lax
from jax.experimental import pallas as pl
from jax.experimental.pallas import tpu as pltpu
from jax.sharding import PartitionSpec as P

HEADS = 6
HEAD_DIM = 64
MICRO = 2
F32 = jnp.float32
BF16 = jnp.bfloat16
BOTH = ("dp", "fsdp")
NN = (((1,), (0,)), ((), ()))
NT = (((1,), (1,)), ((), ()))
TN = (((0,), (0,)), ((), ()))
LEVELS = (0, 2, 1, 3)


def dot(left, right, dims=NN):
    return lax.dot_general(left, right, dims, preferred_element_type=F32)


def smem():
    return pl.BlockSpec(memory_space=pltpu.SMEM)


def vmem():
    return pl.BlockSpec(memory_space=pltpu.VMEM)


def hbm():
    return pl.BlockSpec(memory_space=pltpu.HBM)


def call(body, name, ids, ins, outs, scratch=(), flops=0, limit=48, far=()):
    fixed = [] if ids is None else [ids]
    return pl.pallas_call(
        body,
        out_shape=[jax.ShapeDtypeStruct(s, t) for s, t in outs],
        in_specs=[smem()] * len(fixed) + [hbm() if i in far else vmem() for i in range(len(ins))],
        out_specs=[vmem()] * len(outs),
        scratch_shapes=list(scratch),
        compiler_params=pltpu.CompilerParams(vmem_limit_bytes=limit * 1024 * 1024),
        cost_estimate=pl.CostEstimate(flops=1, bytes_accessed=1, transcendentals=0),
        name=name,
    )(*fixed, *ins)


def offsets(ids):
    d, f = ids[0], ids[1]
    core = lax.rem(f, 2)
    first = 1 + core
    second = 2 - core
    return d, f, (0, first, second, 3), (0, second, first, 3)


def flip(a, b):
    return lax.bitwise_xor(a, b)


def pick_body(proj, outw, up, down, cond, q_all, c_in, sems):
    d = lax.axis_index("dp")
    rows, width = outw.shape
    at = pl.ds(pl.multiple_of(d * width, 128), width)
    at_proj = pl.ds(pl.multiple_of(lax.min(d, 2) * width, 128), width)
    q_po = q_all.at[pl.ds(0, rows), :]
    copies = [
        pltpu.make_async_copy(cond, c_in, sems.at[0]),
        pltpu.make_async_copy(up.at[:, at], q_all.at[pl.ds(rows, rows), :], sems.at[1]),
        pltpu.make_async_copy(
            down.at[pl.ds(pl.multiple_of(d * rows, 16), rows), :],
            q_all.at[pl.ds(2 * rows, rows), :],
            sems.at[2],
        ),
    ]
    for copy in copies:
        copy.start()

    @pl.when(d < 3)
    def _():
        copy = pltpu.make_async_copy(proj.at[:, at_proj], q_po, sems.at[3])
        copy.start()
        copy.wait()

    @pl.when(d == 3)
    def _():
        copy = pltpu.make_async_copy(outw, q_po, sems.at[3])
        copy.start()
        copy.wait()

    for copy in copies:
        copy.wait()
    c = c_in[...].astype(F32)
    c = c / (1.0 + jnp.exp(-c))
    blank = jnp.zeros((16 - c.shape[0], width), F32)
    q_all[3 * rows :, :] = jnp.concatenate([c, blank], axis=0).astype(BF16)


def one_hot(shape, shift):
    r = lax.broadcasted_iota(jnp.int32, shape, 0)
    c = lax.broadcasted_iota(jnp.int32, shape, 1)
    return jnp.where(c == r + shift, 1.0, 0.0).astype(BF16)


def prepare_body(wmod_own, wmod_other, f0, f1, f2, f3, f4, wmod, placed):
    f = lax.axis_index("fsdp")
    shard = wmod_own.shape[0]
    wmod[0:shard, :] = wmod_own[...]
    wmod[shard:, :] = wmod_other[...]
    rows = []
    for ref in (f0, f1, f2, f3, f4):
        size = ref.shape[0]
        rows.append(dot(ref[...].reshape(1, size), one_hot((size, 8 * size), f * size)))
    bias, b_qv, b_out, b_up, b_down = rows
    feat = b_out.shape[1]
    placed[0:1, :] = bias
    placed[1:2, :] = jnp.concatenate([b_up, b_qv], axis=1)
    placed[2:3, :] = jnp.concatenate([b_out, b_down, jnp.zeros((1, 4 * feat), F32)], axis=1)


def mod_body(ids, q0, q2, q1, q3, wmod, placed, placed_other, keep_lo, keep_hi, c_own):
    f = ids[1]
    rows, wide = wmod.shape
    slots, feat = c_own.shape[0] // 4, c_own.shape[1]
    shard = rows // 2
    at = q0.shape[0] - 16
    r = lax.broadcasted_iota(jnp.int32, (feat, rows), 0)
    c = lax.broadcasted_iota(jnp.int32, (feat, rows), 1)
    start = jnp.where(c < shard, f * shard, flip(f, 1) * shard - shard)
    select = jnp.where(r == c + start, 1.0, 0.0).astype(BF16)
    stacked = jnp.concatenate([ref[at : at + slots, :] for ref in (q0, q2, q1, q3)], axis=0)
    c_own[...] = stacked
    bias = placed[...] + placed_other[...]
    part = dot(dot(stacked, select).astype(BF16), wmod[...]) + bias[0:1]
    for n in range(4):
        keep = (keep_lo, keep_lo, keep_hi, keep_hi)[n]
        keep[n % 2, 0:slots, :] = part[slots * n : slots * (n + 1)]
        keep[n % 2, 2:4, :] = bias[1:3]


def norm_parts(x):
    mean = jnp.mean(x, axis=-1, keepdims=True)
    centered = x - mean
    rstd = lax.rsqrt(jnp.mean(centered * centered, axis=-1, keepdims=True) + 1e-06)
    return centered * rstd, rstd


def lane_masks(rows):
    lane = lax.broadcasted_iota(jnp.int32, (rows, 2 * HEAD_DIM), 1)
    return lane < HEAD_DIM


def attend_body(
    ids, *refs,
):
    d, f, mine, theirs = offsets(ids)
    pieces, (m_proj, m_out, o_proj, o_out, p0, p1, lat, wpo, mod, n1, proj, att) = refs[:8], refs[8:]
    rows, feat = m_out.shape
    whole = ((m_proj, m_out), (o_proj, o_out))
    split = (pieces[:4], mine, f), (pieces[4:], theirs, flip(f, 1))
    for (p_ref, o_ref), (found, flips, base) in zip(whole, split):
        at = pl.multiple_of(base * rows, 16)
        for block in range(3):
            wpo[block, pl.ds(at, rows), :] = p_ref[:, block * feat : (block + 1) * feat]
        wpo[3, pl.ds(at, rows), :] = o_ref[...]
        for n, how in enumerate(flips):
            block = flip(d, how)
            for place, zm in enumerate(LEVELS[1:]):
                get = found[n].at[place]
                at = pl.multiple_of(flip(base, 2 * zm) * rows, 16)
                wpo[block, pl.ds(at, rows), :] = get[0:rows, :]
    mod[...] = p0[0] + p1[...]
    length = lat.shape[1]
    low_half = lane_masks(length)
    qv = mod[2:3, 4 * feat :]

    def one(i, carry):
        at = pl.multiple_of(i * length, 256)
        x = lat[i].astype(F32)
        xhat, rstd = norm_parts(x)
        row = mod[pl.ds(i, 1), :]
        n = (xhat * (1.0 + row[:, feat : 2 * feat]) + row[:, :feat]).astype(BF16)
        n1[pl.ds(at, length), :] = n
        proj[pl.ds(at, length), 0:feat] = (dot(n, wpo[0]) + qv[:, :feat]).astype(BF16)
        proj[pl.ds(at, length), feat : 2 * feat] = dot(n, wpo[1]).astype(BF16)
        proj[pl.ds(at, length), 2 * feat :] = (dot(n, wpo[2]) + qv[:, feat:]).astype(BF16)
        for pair in range(HEADS // 2):
            lo = pair * 2 * HEAD_DIM
            hi = lo + 2 * HEAD_DIM
            q = proj[pl.ds(at, length), lo:hi]
            k = proj[pl.ds(at, length), feat + lo : feat + hi]
            v = proj[pl.ds(at, length), 2 * feat + lo : 2 * feat + hi]
            zero = jnp.zeros_like(q)
            outs = []
            for side in range(2):
                q_one = jnp.where(low_half, q, zero) if side == 0 else jnp.where(low_half, zero, q)
                s = dot(q_one, k, NT) * HEAD_DIM ** (-0.5)
                e = jnp.exp(s - jnp.max(s, axis=-1, keepdims=True))
                inv = 1.0 / jnp.sum(e, axis=-1, keepdims=True)
                outs.append(dot((e * inv).astype(BF16), v))
            att[pl.ds(at, length), lo:hi] = jnp.where(low_half, outs[0], outs[1]).astype(BF16)
        return carry

    lax.fori_loop(0, lat.shape[0], one, 0)


def spread(tmp, at_row, dm, pieces, rows, f, slot=None):
    keep_odd, keep_even, send_odd, send_even = pieces
    keep = (keep_even, keep_odd)[dm % 2]
    swapped = (0, 2, 1, 3)[dm]
    send = (send_even, send_odd)[swapped % 2]
    for place, zm in enumerate(LEVELS):
        for ref, at, owner in (
            (keep, dm // 2, flip(f, 2 * zm)),
            (send, swapped // 2, flip(f, 2 * zm + 1)),
        ):
            piece = tmp[pl.ds(pl.multiple_of(at_row(owner), 16), rows), :]
            if slot is None:
                ref[at, place] = piece
            else:
                ref[at, place, slot] = piece


def mlp_body(
    ids, *refs,
):
    mlp_steps(ids, refs[:8], *refs[8:])


def mlp_steps(
    ids, pieces, m_up, m_down, o_up, o_down, wout, mod, lat, cot, att,
    res, gmid, gbr, gatt, gsum, gmod, k_odd, k_even, s_odd, s_even,
    wu, wd, n2s, acts, dgs, gmlps, gpres, n2t, tmp, tmpd,
):
    d, f, mine, theirs = offsets(ids)
    count = ids[2]
    rows, feat = m_up.shape[0], m_down.shape[1]
    hidden = wd.shape[0]
    blocks = hidden // feat
    step = 512
    whole = ((m_up, m_down), (o_up, o_down))
    split = (pieces[:4], mine, f), (pieces[4:], theirs, flip(f, 1))
    for (u_ref, d_ref), (found, flips, base) in zip(whole, split):
        at = pl.multiple_of(base * rows, 16)
        wu[pl.ds(at, rows), :] = u_ref[...]
        wd[pl.ds(pl.multiple_of(base * 4 * rows, 16), 4 * rows), :] = d_ref[...]
        for n, how in enumerate(flips):
            block = flip(d, how)
            for place, zm in enumerate(LEVELS[1:]):
                get = found[n].at[place]
                owner = flip(base, 2 * zm)
                wu[
                    pl.ds(pl.multiple_of(owner * rows, 16), rows),
                    pl.ds(pl.multiple_of(block * feat, 128), feat),
                ] = get[rows : 2 * rows, :]
                at = pl.multiple_of((owner * 4 + block) * rows, 16)
                wd[pl.ds(at, rows), :] = get[2 * rows : 3 * rows, :]
    length = lat.shape[1]
    bup = mod[2:3, : 4 * feat]
    bout = mod[3:4, :feat]
    bdown = mod[3:4, feat : 2 * feat]
    gsum[...] = jnp.zeros_like(gsum)

    def one(i, carry):
        at = pl.multiple_of(i * length, 256)
        part = pl.ds(at, length)
        row = mod[pl.ds(i, 1), :]
        gate_one, shift, scale, gate_two = (row[:, j * feat : (j + 1) * feat] for j in (2, 3, 4, 5))
        alive = jnp.where(i < count, 1.0, 0.0).astype(F32)
        branch = dot(att[part, :], wout[0]) + bout
        middle = lat[i].astype(F32) + gate_one * branch
        xhat, rstd = norm_parts(middle)
        n2 = (xhat * (1.0 + scale) + shift).astype(BF16)
        n2s[part, :] = n2
        mlp = jnp.zeros((length, feat), F32) + bdown
        for j in range(0, hidden, step):
            cols = slice(j, j + step)
            v = dot(n2, wu[:, cols]) + bup[:, cols]
            square = v * v
            half = 0.5 + 0.5 * jnp.tanh(v * (0.7978845608028654 + 0.035677408136300125 * square))
            act = (v * half).astype(BF16)
            slope = v * (1.5957691216057308 + 0.21406444881780075 * square)
            dgs[:, cols] = half * (1.0 + (1.0 - half) * slope)
            acts[part, cols] = act
            mlp = mlp + dot(act, wd[cols, :])
        res[i] = (alive * (middle + gate_two * mlp)).astype(BF16)
        upstream = alive * cot[i].astype(F32)
        g_gate_two = jnp.sum(upstream * mlp, axis=0, keepdims=True)
        gmlp = (gate_two * upstream).astype(BF16)
        gmlps[part, :] = gmlp
        gn = jnp.zeros((length, feat), F32)
        for j in range(0, hidden, step):
            cols = slice(j, j + step)
            gpre = (dot(gmlp, wd[cols, :], NT) * dgs[:, cols]).astype(BF16)
            gpres[part, cols] = gpre
            gn = gn + dot(gpre, wu[:, cols], NT)
            gsum[:, feat + j : feat + j + step] += jnp.sum(gpre.astype(F32), axis=0, keepdims=True)
        g_shift = jnp.sum(gn, axis=0, keepdims=True)
        g_scale = jnp.sum(gn * xhat, axis=0, keepdims=True)
        gx = gn * (1.0 + scale)
        gmiddle = upstream + rstd * (
            gx
            - jnp.mean(gx, axis=-1, keepdims=True)
            - xhat * jnp.mean(gx * xhat, axis=-1, keepdims=True)
        )
        gmid[i] = gmiddle
        g_gate_one = jnp.sum(gmiddle * branch, axis=0, keepdims=True)
        gbranch = (gate_one * gmiddle).astype(BF16)
        gbr[part, :] = gbranch
        gatt[part, :] = dot(gbranch, wout[0], NT).astype(BF16)
        gsum[:, 0:feat] += jnp.sum(gbranch.astype(F32), axis=0, keepdims=True)
        gsum[:, 5 * feat : 6 * feat] += jnp.sum(gmlp.astype(F32), axis=0, keepdims=True)
        gmod[pl.ds(i, 1), :] = jnp.concatenate([g_gate_one, g_shift, g_scale, g_gate_two], axis=1)
        return carry

    lax.fori_loop(0, lat.shape[0], one, 0)
    pieces = (k_odd, k_even, s_odd, s_even)
    n2t[...] = n2s[...].T
    for j in range(0, hidden, step):
        cols = slice(j, j + step)
        tmpd[cols, :] = dot(acts[:, cols], gmlps[...], TN).astype(BF16)
        tmp[:, cols] = dot(n2t[...], gpres[:, cols]).astype(BF16)
    for dm in range(4):
        block = flip(d, mine[dm])
        spread(tmpd, lambda o: (o * 4 + block) * rows, dm, pieces, rows, f, 1)
        cut = pl.ds(pl.multiple_of(block * feat, 128), feat)
        spread(tmp.at[:, cut], lambda o: o * rows, dm, pieces, rows, f, 0)


def attend_back_one(proj, gatt, gall, i, length):
    feat = gatt.shape[1]
    low_half = lane_masks(length)

    def one(i, carry):
        part = slice(i * length, (i + 1) * length)
        for pair in range(HEADS // 2):
            lo = pair * 2 * HEAD_DIM
            hi = lo + 2 * HEAD_DIM
            q = proj[part, lo:hi]
            k = proj[part, feat + lo : feat + hi]
            v = proj[part, 2 * feat + lo : 2 * feat + hi]
            ga = gatt[part, lo:hi]
            zero = jnp.zeros_like(q)
            gq = jnp.zeros(q.shape, F32)
            gk = jnp.zeros(q.shape, F32)
            gv = jnp.zeros(q.shape, F32)
            for side in range(2):
                own = lambda a: (
                    jnp.where(low_half, a, zero) if side == 0 else jnp.where(low_half, zero, a)
                )
                q_one, ga_one = own(q), own(ga)
                s = dot(k, q_one, NT) * HEAD_DIM ** (-0.5)
                e = jnp.exp(s - jnp.max(s, axis=0, keepdims=True))
                prob = e * (1.0 / jnp.sum(e, axis=0, keepdims=True))
                gv = gv + dot(prob.astype(BF16), ga_one)
                gp = dot(v, ga_one, NT)
                delta = jnp.sum(gp * prob, axis=0, keepdims=True)
                gs = (prob * (gp - delta)).astype(BF16)
                gk = gk + dot(gs, q_one)
                gq = gq + dot(gs, own(k), TN)
            gall[part, lo:hi] = (gq * HEAD_DIM ** (-0.5)).astype(BF16)
            gall[part, feat + lo : feat + hi] = (gk * HEAD_DIM ** (-0.5)).astype(BF16)
            gall[part, 2 * feat + lo : 2 * feat + hi] = gv.astype(BF16)
        return carry

    one(i, 0)


def attend_back_first_body(proj, gatt, gproj, *, length):
    attend_back_one(proj, gatt, gproj, 0, length)


def attend_back_body(
    ids, proj, gatt, att, gbr, n1, gsum, g_first, gproj, bias, k_odd, k_even, s_odd, s_even,
    gall, xts, tmp, *, length,
):
    d, f, mine, _ = offsets(ids)
    feat = att.shape[1]
    rows = k_odd.shape[2]
    gall[0:length, : 3 * feat] = g_first[...]
    for i in range(1, proj.shape[0] // length):
        attend_back_one(proj, gatt, gall, i, length)
    gproj[...] = gall[:, : 3 * feat]
    gall[:, 3 * feat :] = gbr[...]
    xts[0] = n1[...].T
    xts[1] = att[...].T
    pieces = (k_odd, k_even, s_odd, s_even)
    for dm in (1, 3, 0, 2):
        block = flip(d, mine[dm])
        tmp[...] = dot(
            xts[jnp.where(block == 3, 1, 0)],
            gall[:, pl.ds(pl.multiple_of(block * feat, 128), feat)],
        ).astype(BF16)
        spread(tmp, lambda o: o * rows, dm, pieces, rows, f)
    bias[:, 0:feat] = jnp.sum(gall[:, 0:feat].astype(F32), axis=0, keepdims=True)
    bias[:, feat : 2 * feat] = jnp.sum(
        gall[:, 2 * feat : 3 * feat].astype(F32), axis=0, keepdims=True
    )
    bias[:, 2 * feat :] = gsum[...]


def input_back_body(ids, gproj, wpo, lat, gmid, mod, gmod, bias, lgrad, gm, full):
    length = lat.shape[1]
    feat = lat.shape[2]

    def one(i, carry):
        part = pl.ds(pl.multiple_of(i * length, 256), length)
        row = mod[pl.ds(i, 1), :]
        xhat, rstd = norm_parts(lat[i].astype(F32))
        gn = dot(gproj[part, 0:feat], wpo[0], NT)
        gn = gn + dot(gproj[part, feat : 2 * feat], wpo[1], NT)
        gn = gn + dot(gproj[part, 2 * feat :], wpo[2], NT)
        g_shift = jnp.sum(gn, axis=0, keepdims=True)
        g_scale = jnp.sum(gn * xhat, axis=0, keepdims=True)
        gx = gn * (1.0 + row[:, feat : 2 * feat])
        lgrad[i] = (
            gmid[i]
            + rstd
            * (
                gx
                - jnp.mean(gx, axis=-1, keepdims=True)
                - xhat * jnp.mean(gx * xhat, axis=-1, keepdims=True)
            )
        ).astype(BF16)
        full[pl.ds(i, 1), : 6 * feat] = jnp.concatenate(
            [g_shift, g_scale, gmod[pl.ds(i, 1), :]], axis=1
        )
        return carry

    lax.fori_loop(0, lat.shape[0], one, 0)
    full[0:1, 6 * feat :] = bias[:, : 4 * feat]
    full[1:2, 6 * feat :] = bias[:, 4 * feat :]
    gm[...] = full[...].astype(BF16)


def cond_back_body(ids, g0, g2, g1, g3, wmod, lo, hi):
    f = ids[1]
    rows, wide = wmod.shape
    place = one_hot((rows, lo.shape[2]), f * rows)
    lo[...] = jnp.zeros_like(lo)
    hi[...] = jnp.zeros_like(hi)
    for ref, out, at in ((g0, lo, 0), (g2, lo, 1), (g1, hi, 0), (g3, hi, 1)):
        part = dot(ref[:, :wide], wmod[...], NT).astype(BF16)
        out[at, 0 : part.shape[0], :] = dot(part, place).astype(BF16)


def mod_weight_body(ids, e0, e1, e2, e3, wgrad, b_mod, b_qv, b_out, b_up, b_down):
    f = ids[1]
    rows, wide = wgrad.shape
    feat = wide // 6
    grad_wide = e0.shape[1] - feat
    select = one_hot((rows, feat), f * rows)
    total = None
    sums = None
    for ref in (e0, e1, e2, e3):
        own = dot(select, ref[:, grad_wide:], NT).astype(BF16)
        term = dot(own, ref[:, :wide])
        total = term if total is None else total + term
        low = ref[:, :grad_wide].astype(F32)
        sums = low if sums is None else sums + low
    wgrad[...] = total
    low = sums[:, wide:]
    odd = lax.broadcasted_iota(jnp.int32, low.shape, 0) % 2 == 1
    even_sum = jnp.sum(jnp.where(odd, 0.0, low), axis=0, keepdims=True)
    odd_sum = jnp.sum(jnp.where(odd, low, 0.0), axis=0, keepdims=True)
    whole = jnp.concatenate([jnp.sum(sums[:, :wide], axis=0, keepdims=True), even_sum, odd_sum], axis=1)
    at = 0
    for out in (b_mod, b_qv, b_out, b_up, b_down):
        size = out.shape[0]
        vector = jnp.broadcast_to(whole[:, at : at + 8 * size], (8, 8 * size))
        out[...] = pltpu.roll(vector, lax.rem(8 - f, 8) * size, 1)[0, :size]
        at += 8 * size


def sum_body(keep, got, out):
    out[...] = add_low(keep[...], got[...])


def turn_body(keep_ud, in_ud, keep_po, in_po, got_ud, got_po, out, *, at):
    rows = keep_po.shape[2]
    for place in range(out.shape[0]):
        out[place, 0:rows] = add_low(keep_po[at, place], in_po[at, place], got_po[at, place])
        for slot in range(2):
            out[place, (1 + slot) * rows : (2 + slot) * rows] = add_low(
                keep_ud[at, place, slot], in_ud[at, place, slot], got_ud[at, place, slot]
            )


def pair_body(own, other, out):
    out[0 : own.shape[0], :] = own[...]
    out[own.shape[0] :, :] = other[...]


def pack_body(g0, g2, g1, g3, c_own, c_other, out):
    many, wide = g0.shape
    half = many // 2
    for n, ref in enumerate((g0, g2, g1, g3)):
        out[many * n : many * (n + 1), 0:wide] = ref[...]
        out[many * n : many * n + half, wide:] = c_own[half * n : half * (n + 1), :]
        out[many * n + half : many * (n + 1), wide:] = c_other[half * n : half * (n + 1), :]


def join_far_body(base, part, back, out):
    size = base.shape[1]
    out[:, 0:size] = add_low(base[2:], part[2:])
    out[:, size:] = back[...]


def join_near_body(base, part, back, got, out):
    size = base.shape[1]
    out[:, 0:size] = add_low(base[:2], part[:2], got[:, 0:size])
    out[:, size:] = add_low(back[...], got[:, size:])


def final_body(ids, g0, g1, g2, g3, gp, go, gu, gd):
    d, _, mine, _ = offsets(ids)
    rows, feat = go.shape
    for ref, how in zip((g0, g1, g2, g3), mine):
        block = flip(d, how)

        @pl.when(block < 3)
        def _():
            at = pl.multiple_of(lax.min(block, 2) * feat, 128)
            gp[:, pl.ds(at, feat)] = ref[0:rows, :].astype(F32)

        @pl.when(block == 3)
        def _():
            go[...] = ref[0:rows, :].astype(F32)

        gu[:, pl.ds(pl.multiple_of(block * feat, 128), feat)] = ref[rows : 2 * rows, :].astype(F32)
        gd[pl.ds(pl.multiple_of(block * rows, 16), rows), :] = ref[2 * rows : 3 * rows, :].astype(F32)


def routes():
    core, first, second, across = [], [], [], []
    levels = {1: [], 2: []}
    for d in range(4):
        for f in range(8):
            i = d * 8 + f
            core.append((i, i ^ 1))
            a = 1 if f % 2 == 0 else 2
            first.append((i, (d ^ a) * 8 + f))
            second.append((i, (d ^ (3 - a)) * 8 + f))
            across.append((i, (d ^ 3) * 8 + f))
            for m in levels:
                levels[m].append((i, d * 8 + (f ^ (2 * m))))
    return core, first, second, across, levels


def add_low(*parts):
    total = parts[0].astype(F32)
    for part in parts[1:]:
        total = total + part.astype(F32)
    return total.astype(BF16)


def on_device_blocks(
    latents, cond, counts, cotangent, modulation_weight, modulation_bias, projection_weight,
    query_value_bias, output_weight, output_bias, up_weight, up_bias, down_weight, down_bias,
):
    core, first, second, across, levels = routes()

    def move(x, route):
        return lax.ppermute(x, BOTH, route)

    slots, length, feat = latents.shape
    rows = projection_weight.shape[0]
    hidden = up_weight.shape[1]
    wide = modulation_weight.shape[1]
    tokens = slots * length
    d = lax.axis_index("dp")
    f = lax.axis_index("fsdp")
    ids = jnp.stack([d, f, counts[0]]).astype(jnp.int32)

    def after(x, *earlier):
        return lax.optimization_barrier((x,) + earlier)[0]

    (q_all,) = call(
        pick_body, "pick", None,
        [projection_weight, output_weight, up_weight, down_weight, cond],
        [((3 * rows + 16, feat), BF16)],
        [pltpu.VMEM((slots, feat), BF16), pltpu.SemaphoreType.DMA((4,))],
        far=(0, 1, 2, 3, 4), limit=60,
    )

    def over_dp(own):
        a = move(own, first)
        b = move(own, second)
        return [own, a, b, move(a, second)]

    whole = [projection_weight, output_weight, up_weight, down_weight]
    w_whole = whole + [move(x, core) for x in whole]
    biases = [modulation_bias, query_value_bias, output_bias, up_bias, down_bias]
    wmod, placed = call(
        prepare_body, "prepare", None, [modulation_weight, move(modulation_weight, core)] + biases,
        [((2 * rows, wide), BF16), ((3, wide), F32)],
    )
    q_far = move(q_all, levels[2])
    placed_other = move(placed, core)
    ready = (placed_other, *w_whole[4:])
    q_far = after(q_far, *ready)
    q_near, q_both = move(after(q_all, q_far), levels[1]), move(q_far, levels[1])
    own = jnp.stack([q_far, q_near, q_both])
    keep_lo, keep_hi, c_own = call(
        mod_body, "modulation", ids, [q_all, q_far, q_near, q_both, wmod, placed, placed_other],
        [((2, 4, wide), F32)] * 2 + [((4 * slots, feat), BF16)],
    )
    a_own, b_own = move(own, first), move(own, second)
    paid_lo = keep_lo + move(keep_hi, levels[1])
    a_own = after(a_own, paid_lo)
    paid_far = move(after(paid_lo[1], a_own), levels[2])
    ab_own = move(a_own, second)
    w_all = [own, a_own, b_own, ab_own]
    w_all = w_all + [move(x, core) for x in w_all[:3]] + [move(after(ab_own, paid_far), core)]

    wpo, mod, n1, proj, att = call(
        attend_body, "attention", ids,
        w_all + [w_whole[k] for k in (0, 1, 4, 5)] + [paid_lo, paid_far, latents],
        [((4, feat, feat), BF16), ((4, wide), F32), ((tokens, feat), BF16),
         ((tokens, 3 * feat), BF16), ((tokens, feat), BF16)],
        flops=2 * tokens * feat * (3 * feat + 4 * length),
    )
    wout = wpo[3:4]
    ud_shape = ((2, 4, 2, rows, feat), BF16)
    po_shape = ((2, 4, rows, feat), BF16)
    res, gmid, gbr, gatt, gsum, gmod, ud_odd, ud_even, ud_odd_out, ud_even_out = call(
        mlp_body, "mlp", ids,
        w_all + [w_whole[k] for k in (2, 3, 6, 7)] + [wout, mod, latents, cotangent, att],
        [((slots, length, feat), BF16), ((slots, length, feat), F32), ((tokens, feat), BF16),
         ((tokens, feat), BF16), ((1, 6 * feat), F32), ((slots, 4 * feat), F32)] + [ud_shape] * 4,
        [
            pltpu.VMEM((feat, hidden), BF16), pltpu.VMEM((hidden, feat), BF16),
            pltpu.VMEM((tokens, feat), BF16), pltpu.VMEM((tokens, hidden), BF16),
            pltpu.VMEM((length, hidden), F32), pltpu.VMEM((tokens, feat), BF16),
            pltpu.VMEM((tokens, hidden), BF16), pltpu.VMEM((feat, tokens), BF16),
            pltpu.VMEM((feat, hidden), BF16), pltpu.VMEM((hidden, feat), BF16),
        ],
        flops=2 * tokens * feat * (6 * hidden + 2 * feat),
    )
    ud_odd_in = move(ud_odd_out, core)
    ud_even_in = move(ud_even_out, core)
    (g_first,) = call(
        functools.partial(attend_back_first_body, length=length), "attention_back_first", None,
        [proj, gatt], [((length, 3 * feat), BF16)], flops=tokens * feat * 10 * length,
    )
    (odd_ud,) = call(sum_body, "sum_ud", None, [ud_odd, after(ud_odd_in, g_first)], [ud_shape])
    got_ud = move(odd_ud, first)
    gproj, bias, po_odd, po_even, po_odd_out, po_even_out = call(
        functools.partial(attend_back_body, length=length), "attention_back", ids,
        [proj, gatt, att, gbr, n1, gsum, after(g_first, odd_ud)],
        [((tokens, 3 * feat), BF16), ((1, 8 * feat), F32)] + [po_shape] * 4,
        [pltpu.VMEM((tokens, 4 * feat), BF16), pltpu.VMEM((2, feat, tokens), BF16),
         pltpu.VMEM((feat, feat), BF16)],
        flops=2 * tokens * feat * (4 * feat + 5 * length),
    )
    po_odd_in = move(po_odd_out, core)
    po_even_in = move(po_even_out, core)
    lgrad, gm = call(
        input_back_body, "input_back", ids,
        [gproj, wpo, latents, gmid, mod, gmod, bias],
        [((slots, length, feat), BF16), ((slots, 10 * feat), BF16)],
        [pltpu.VMEM((slots, 10 * feat), F32)],
        flops=2 * tokens * feat * 3 * feat,
    )
    (odd_po,) = call(sum_body, "sum_po", None, [po_odd, after(po_odd_in, gm, got_ud)], [po_shape])
    got_po = move(odd_po, first)
    c_other = move(c_own, core)

    (gm_pair,) = call(pair_body, "pair", None, [after(gm, c_other), move(gm, core)], [((2 * slots, 10 * feat), BF16)])
    gm_far = move(gm_pair, levels[2])

    halves = [ud_even, ud_even_in, po_even, po_even_in, got_ud, after(got_po, gm_far)]
    half_shape = ((4, 3 * rows, feat), BF16)
    (turned,) = call(functools.partial(turn_body, at=1), "turn", None, halves, [half_shape])
    part = move(turned, second)
    (base,) = call(
        functools.partial(turn_body, at=0), "base", None, halves[:5] + [after(got_po, turned)], [half_shape]
    )

    gm_all = [gm_pair, gm_far, move(after(gm_pair, gm_far), levels[1]), move(gm_far, levels[1])]
    (every,) = call(
        pack_body, "pack", None, gm_all + [c_own, c_other], [((8 * slots, 11 * feat), BF16)]
    )
    back_lo, back_hi = call(
        cond_back_body, "cond_back", ids, gm_all + [modulation_weight], [((2, 16, feat), BF16)] * 2
    )

    pair_shape = ((2, 3 * rows + 16, feat), BF16)
    (turned,) = call(join_far_body, "join_far", None, [base, part, back_hi], [pair_shape])
    got = move(turned, levels[1])
    every = after(every, turned)
    e_first, e_second, e_both = move(every, first), move(every, second), move(every, across)
    (base,) = call(join_near_body, "join_near", None, [base, part, back_lo, got], [pair_shape])
    g_mod_weight, *g_biases = call(
        mod_weight_body, "mod_weight", ids, [every, e_first, e_second, e_both],
        [((rows, wide), F32)] + [((size // 8,), F32) for size in (wide, 2 * feat, feat, hidden, feat)],
    )
    total = add_low(base[0], after(move(base[1], levels[2]), g_mod_weight))
    a_total, b_total = move(total, first), move(total, second)
    shares = [total, a_total, b_total, move(a_total, second)]
    silu_pair = total[3 * rows : 3 * rows + 2 * slots].astype(F32)
    silu_other = after(total, b_total)[3 * rows + slots : 3 * rows + 2 * slots]
    grad_silu = silu_pair[:slots] + move(silu_other, core).astype(F32)
    cond_full = cond.astype(F32)
    sig = 1.0 / (1.0 + jnp.exp(-cond_full))
    cond_grad = (grad_silu * (sig * (1.0 + cond_full * (1.0 - sig)))).astype(BF16)
    g_proj, g_out, g_up, g_down = call(
        final_body, "final", ids, shares,
        [((rows, 3 * feat), F32), ((rows, feat), F32), ((rows, hidden), F32),
         ((4 * rows, feat), F32)],
    )
    return (
        res, lgrad, cond_grad, g_mod_weight, g_biases[0], g_proj, g_biases[1],
        g_out, g_biases[2], g_up, g_biases[3], g_down, g_biases[4],
    )


def layer_norm(vector):
    row_mean = jnp.mean(vector, axis=-1, keepdims=True)
    centered = vector - row_mean
    variance = jnp.mean(centered * centered, axis=-1, keepdims=True)
    return centered * lax.rsqrt(variance + 1e-06)


def modulate(vector, offset, stretch):
    return layer_norm(vector) * (1.0 + stretch[:, None, :]) + offset[:, None, :]


def forward_pass(gathered, inputs, conditions):
    (
        modulation_weight,
        modulation_bias,
        projection_weight,
        query_value_bias,
        output_weight,
        output_bias,
        up_weight,
        up_bias,
        down_weight,
        down_bias,
    ) = gathered
    members, length, features = inputs.shape
    flat_rows = members * length
    cond_low = jax.nn.silu(conditions).astype(jnp.bfloat16)
    modulation = jnp.dot(cond_low, modulation_weight, preferred_element_type=jnp.float32)
    modulation = modulation + modulation_bias.astype(jnp.float32)
    pieces = jnp.split(modulation, 6, axis=-1)
    normed_one = (
        modulate(inputs, pieces[0], pieces[1]).astype(jnp.bfloat16).reshape(flat_rows, features)
    )
    bias_full = query_value_bias.astype(jnp.float32)
    joined_bias = jnp.concatenate(
        [bias_full[:features], jnp.zeros((features,), jnp.float32), bias_full[features:]]
    )
    projected = (
        jnp.dot(normed_one, projection_weight, preferred_element_type=jnp.float32) + joined_bias
    )
    projected = projected.astype(jnp.bfloat16).reshape(members, length, 3, HEADS, HEAD_DIM)
    queries = projected[:, :, 0]
    key_rows = projected[:, :, 1]
    values = projected[:, :, 2]
    scores = jnp.einsum(
        "bqhd,bkhd->bhqk", queries, key_rows, preferred_element_type=jnp.float32
    ) * HEAD_DIM ** (-0.5)
    row_max = jnp.max(scores, axis=-1, keepdims=True)
    exponent = jnp.exp(scores - row_max)
    row_total = jnp.sum(exponent, axis=-1, keepdims=True)
    probability = exponent / row_total
    log_total = row_max + jnp.log(row_total)
    attended = jnp.einsum(
        "bhqk,bkhd->bqhd",
        probability.astype(jnp.bfloat16),
        values,
        preferred_element_type=jnp.float32,
    )
    attended = attended.astype(jnp.bfloat16).reshape(flat_rows, features)
    branch = jnp.dot(
        attended, output_weight, preferred_element_type=jnp.float32
    ) + output_bias.astype(jnp.float32)
    branch = branch.reshape(members, length, features)
    middle = inputs + pieces[2][:, None, :] * branch
    normed_two = (
        modulate(middle, pieces[3], pieces[4]).astype(jnp.bfloat16).reshape(flat_rows, features)
    )
    pre_act = jnp.dot(normed_two, up_weight, preferred_element_type=jnp.float32) + up_bias.astype(
        jnp.float32
    )
    activated = jax.nn.gelu(pre_act, approximate=True).astype(jnp.bfloat16)
    mlp_out = jnp.dot(
        activated, down_weight, preferred_element_type=jnp.float32
    ) + down_bias.astype(jnp.float32)
    mlp_out = mlp_out.reshape(members, length, features)
    output = middle + pieces[5][:, None, :] * mlp_out
    return (
        output,
        cond_low,
        pieces,
        normed_one,
        queries,
        key_rows,
        values,
        log_total,
        attended,
        branch,
        middle,
        normed_two,
        pre_act,
        activated,
        mlp_out,
    )


def backward_pass(gathered, saved, inputs, conditions, upstream):
    (
        modulation_weight,
        modulation_bias,
        projection_weight,
        query_value_bias,
        output_weight,
        output_bias,
        up_weight,
        up_bias,
        down_weight,
        down_bias,
    ) = gathered
    (
        output,
        cond_low,
        pieces,
        normed_one,
        queries,
        key_rows,
        values,
        log_total,
        attended,
        branch,
        middle,
        normed_two,
        pre_act,
        activated,
        mlp_out,
    ) = saved
    members, length, features = inputs.shape
    flat_rows = members * length
    grad_gate_two = jnp.sum(upstream * mlp_out, axis=1)
    grad_mlp = (pieces[5][:, None, :] * upstream).astype(jnp.bfloat16).reshape(flat_rows, features)
    grad_down = jnp.einsum("nf,nd->fd", activated, grad_mlp, preferred_element_type=jnp.float32)
    grad_down_b = jnp.sum(grad_mlp.astype(jnp.float32), axis=0)
    grad_activated = jnp.einsum(
        "nd,fd->nf", grad_mlp, down_weight, preferred_element_type=jnp.float32
    )
    gelu_out, gelu_pull = jax.vjp(lambda vector: jax.nn.gelu(vector, approximate=True), pre_act)
    grad_pre = gelu_pull(grad_activated)[0].astype(jnp.bfloat16)
    grad_up = jnp.einsum("nd,nf->df", normed_two, grad_pre, preferred_element_type=jnp.float32)
    grad_up_b = jnp.sum(grad_pre.astype(jnp.float32), axis=0)
    grad_normed_two = jnp.einsum(
        "nf,df->nd", grad_pre, up_weight, preferred_element_type=jnp.float32
    )
    second_out, second_pull = jax.vjp(modulate, middle, pieces[3], pieces[4])
    grad_middle, grad_shift_two, grad_scale_two = second_pull(
        grad_normed_two.reshape(members, length, features)
    )
    grad_middle = grad_middle + upstream
    grad_gate_one = jnp.sum(grad_middle * branch, axis=1)
    grad_branch = (
        (pieces[2][:, None, :] * grad_middle).astype(jnp.bfloat16).reshape(flat_rows, features)
    )
    grad_output = jnp.einsum("nd,ne->de", attended, grad_branch, preferred_element_type=jnp.float32)
    grad_output_b = jnp.sum(grad_branch.astype(jnp.float32), axis=0)
    grad_attended = jnp.einsum(
        "ne,de->nd", grad_branch, output_weight, preferred_element_type=jnp.float32
    )
    grad_attended = grad_attended.astype(jnp.bfloat16).reshape(members, length, HEADS, HEAD_DIM)
    scale_factor = HEAD_DIM ** (-0.5)
    scores = (
        jnp.einsum("bqhd,bkhd->bhqk", queries, key_rows, preferred_element_type=jnp.float32)
        * scale_factor
    )
    probability = jnp.exp(scores - log_total)
    grad_values = jnp.einsum(
        "bhqk,bqhd->bkhd",
        probability.astype(jnp.bfloat16),
        grad_attended,
        preferred_element_type=jnp.float32,
    )
    grad_prob = jnp.einsum(
        "bqhd,bkhd->bhqk", grad_attended, values, preferred_element_type=jnp.float32
    )
    row_delta = jnp.sum(grad_prob * probability, axis=-1, keepdims=True)
    grad_scores = (probability * (grad_prob - row_delta)).astype(jnp.bfloat16)
    grad_queries = (
        jnp.einsum("bhqk,bkhd->bqhd", grad_scores, key_rows, preferred_element_type=jnp.float32)
        * scale_factor
    )
    grad_keys = (
        jnp.einsum("bhqk,bqhd->bkhd", grad_scores, queries, preferred_element_type=jnp.float32)
        * scale_factor
    )
    grad_projected = jnp.stack([grad_queries, grad_keys, grad_values], axis=2)
    grad_projected = grad_projected.astype(jnp.bfloat16).reshape(flat_rows, 3 * features)
    grad_projection = jnp.einsum(
        "nd,ne->de", normed_one, grad_projected, preferred_element_type=jnp.float32
    )
    column_sums = jnp.sum(grad_projected.astype(jnp.float32), axis=0)
    grad_query_value = jnp.concatenate([column_sums[:features], column_sums[2 * features :]])
    grad_normed_one = jnp.einsum(
        "ne,de->nd", grad_projected, projection_weight, preferred_element_type=jnp.float32
    )
    first_out, first_pull = jax.vjp(modulate, inputs, pieces[0], pieces[1])
    grad_input, grad_shift_one, grad_scale_one = first_pull(
        grad_normed_one.reshape(members, length, features)
    )
    grad_input = grad_input + grad_middle
    grad_modulation = jnp.concatenate(
        [
            grad_shift_one,
            grad_scale_one,
            grad_gate_one,
            grad_shift_two,
            grad_scale_two,
            grad_gate_two,
        ],
        axis=-1,
    ).astype(jnp.bfloat16)
    grad_mod_weight = jnp.einsum(
        "bc,be->ce", cond_low, grad_modulation, preferred_element_type=jnp.float32
    )
    grad_mod_bias = jnp.sum(grad_modulation.astype(jnp.float32), axis=0)
    grad_silu = jnp.einsum(
        "be,ce->bc", grad_modulation, modulation_weight, preferred_element_type=jnp.float32
    )
    silu_out, silu_pull = jax.vjp(jax.nn.silu, conditions)
    grad_conditions = silu_pull(grad_silu)[0]
    weight_grads = (
        grad_mod_weight,
        grad_mod_bias,
        grad_projection,
        grad_query_value,
        grad_output,
        grad_output_b,
        grad_up,
        grad_up_b,
        grad_down,
        grad_down_b,
    )
    return (weight_grads, grad_input, grad_conditions)


def on_device(
    latents,
    cond,
    counts,
    cotangent,
    modulation_weight,
    modulation_bias,
    projection_weight,
    query_value_bias,
    output_weight,
    output_bias,
    up_weight,
    up_bias,
    down_weight,
    down_bias,
):
    lat_slots = latents.shape[0]
    per_micro = lat_slots // MICRO
    alive_all = (jnp.arange(lat_slots) < counts[0]).astype(jnp.float32)
    kept = (
        lax.all_gather(modulation_weight, "fsdp", axis=0, tiled=True),
        lax.all_gather(modulation_bias, "fsdp", axis=0, tiled=True),
        lax.all_gather(projection_weight, "fsdp", axis=0, tiled=True),
        lax.all_gather(query_value_bias, "fsdp", axis=0, tiled=True),
        lax.all_gather(output_weight, "fsdp", axis=0, tiled=True),
        lax.all_gather(output_bias, "fsdp", axis=0, tiled=True),
        lax.all_gather(up_weight, "fsdp", axis=0, tiled=True),
        lax.all_gather(up_bias, "fsdp", axis=0, tiled=True),
        lax.all_gather(down_weight, "fsdp", axis=0, tiled=True),
        lax.all_gather(down_bias, "fsdp", axis=0, tiled=True),
    )
    outputs = []
    input_grads = []
    cond_grads = []
    totals = None
    for micro_index in range(MICRO):
        start = micro_index * per_micro
        inputs = latents[start : start + per_micro].astype(jnp.float32)
        conditions = cond[start : start + per_micro].astype(jnp.float32)
        alive_mask = alive_all[start : start + per_micro]
        saved = forward_pass(kept, inputs, conditions)
        outputs.append((saved[0] * alive_mask[:, None, None]).astype(jnp.bfloat16))
        upstream = (
            cotangent[start : start + per_micro].astype(jnp.float32) * alive_mask[:, None, None]
        )
        weight_grads, grad_input, grad_conditions = backward_pass(
            kept, saved, inputs, conditions, upstream
        )
        input_grads.append(grad_input.astype(jnp.bfloat16))
        cond_grads.append(grad_conditions.astype(jnp.bfloat16))
        totals = (
            weight_grads
            if totals is None
            else tuple((left + right for left, right in zip(totals, weight_grads)))
        )
    totals = (
        lax.psum_scatter(totals[0], "fsdp", scatter_dimension=0, tiled=True),
        lax.psum_scatter(totals[1], "fsdp", scatter_dimension=0, tiled=True),
        lax.psum_scatter(totals[2], "fsdp", scatter_dimension=0, tiled=True),
        lax.psum_scatter(totals[3], "fsdp", scatter_dimension=0, tiled=True),
        lax.psum_scatter(totals[4], "fsdp", scatter_dimension=0, tiled=True),
        lax.psum_scatter(totals[5], "fsdp", scatter_dimension=0, tiled=True),
        lax.psum_scatter(totals[6], "fsdp", scatter_dimension=0, tiled=True),
        lax.psum_scatter(totals[7], "fsdp", scatter_dimension=0, tiled=True),
        lax.psum_scatter(totals[8], "fsdp", scatter_dimension=0, tiled=True),
        lax.psum_scatter(totals[9], "fsdp", scatter_dimension=0, tiled=True),
    )
    totals = (
        lax.psum(totals[0].astype(jnp.bfloat16), "dp").astype(jnp.float32),
        lax.psum(totals[1].astype(jnp.bfloat16), "dp").astype(jnp.float32),
        lax.psum(totals[2].astype(jnp.bfloat16), "dp").astype(jnp.float32),
        lax.psum(totals[3].astype(jnp.bfloat16), "dp").astype(jnp.float32),
        lax.psum(totals[4].astype(jnp.bfloat16), "dp").astype(jnp.float32),
        lax.psum(totals[5].astype(jnp.bfloat16), "dp").astype(jnp.float32),
        lax.psum(totals[6].astype(jnp.bfloat16), "dp").astype(jnp.float32),
        lax.psum(totals[7].astype(jnp.bfloat16), "dp").astype(jnp.float32),
        lax.psum(totals[8].astype(jnp.bfloat16), "dp").astype(jnp.float32),
        lax.psum(totals[9].astype(jnp.bfloat16), "dp").astype(jnp.float32),
    )
    return (
        jnp.concatenate(outputs, axis=0),
        jnp.concatenate(input_grads, axis=0),
        jnp.concatenate(cond_grads, axis=0),
        totals[0],
        totals[1],
        totals[2],
        totals[3],
        totals[4],
        totals[5],
        totals[6],
        totals[7],
        totals[8],
        totals[9],
    )


def solution(mesh):
    small = mesh.shape["dp"] == 4 and mesh.shape["fsdp"] == 8
    program = on_device_blocks if small else on_device
    placed = (
        P(("dp", "fsdp"), None, None),
        P(("dp", "fsdp"), None),
        P(("dp", "fsdp")),
        P(("dp", "fsdp"), None, None),
        P("fsdp", None),
        P("fsdp"),
        P("fsdp", None),
        P("fsdp"),
        P("fsdp", None),
        P("fsdp"),
        P("fsdp", None),
        P("fsdp"),
        P("fsdp", None),
        P("fsdp"),
    )
    return jax.shard_map(
        program,
        mesh=mesh,
        in_specs=placed,
        out_specs=(
            P(("dp", "fsdp"), None, None),
            P(("dp", "fsdp"), None, None),
            P(("dp", "fsdp"), None),
            P("fsdp", None),
            P("fsdp"),
            P("fsdp", None),
            P("fsdp"),
            P("fsdp", None),
            P("fsdp"),
            P("fsdp", None),
            P("fsdp"),
            P("fsdp", None),
            P("fsdp"),
        ),
        check_vma=False,
    )
```

```python
import functools

import jax
import jax.numpy as jnp
from jax import lax
from jax.experimental import pallas as pl
from jax.experimental.pallas import tpu as pltpu
from jax.sharding import PartitionSpec as P

HEADS = 6
HEAD_DIM = 64
MICRO = 2
F32 = jnp.float32
BF16 = jnp.bfloat16
BOTH = ("dp", "fsdp")
NN = (((1,), (0,)), ((), ()))
NT = (((1,), (1,)), ((), ()))
TN = (((0,), (0,)), ((), ()))
LEVELS = (0, 2, 1, 3)


def dot(left, right, dims=NN):
    return lax.dot_general(left, right, dims, preferred_element_type=F32)


def smem():
    return pl.BlockSpec(memory_space=pltpu.SMEM)


def vmem():
    return pl.BlockSpec(memory_space=pltpu.VMEM)


def hbm():
    return pl.BlockSpec(memory_space=pltpu.HBM)


def call(body, name, ids, ins, outs, scratch=(), flops=0, limit=48, far=()):
    fixed = [] if ids is None else [ids]
    return pl.pallas_call(
        body,
        out_shape=[jax.ShapeDtypeStruct(s, t) for s, t in outs],
        in_specs=[smem()] * len(fixed) + [hbm() if i in far else vmem() for i in range(len(ins))],
        out_specs=[vmem()] * len(outs),
        scratch_shapes=list(scratch),
        compiler_params=pltpu.CompilerParams(vmem_limit_bytes=limit * 1024 * 1024),
        cost_estimate=pl.CostEstimate(flops=1, bytes_accessed=1, transcendentals=0),
        name=name,
    )(*fixed, *ins)


def offsets(ids):
    d, f = ids[0], ids[1]
    core = lax.rem(f, 2)
    first = 1 + core
    second = 2 - core
    return d, f, (0, first, second, 3), (0, second, first, 3)


def flip(a, b):
    return lax.bitwise_xor(a, b)


def pick_body(proj, outw, up, down, cond, q_all, c_in, sems):
    d = lax.axis_index("dp")
    rows, width = outw.shape
    at = pl.ds(pl.multiple_of(d * width, 128), width)
    at_proj = pl.ds(pl.multiple_of(lax.min(d, 2) * width, 128), width)
    q_po = q_all.at[pl.ds(0, rows), :]
    copies = [
        pltpu.make_async_copy(cond, c_in, sems.at[0]),
        pltpu.make_async_copy(up.at[:, at], q_all.at[pl.ds(rows, rows), :], sems.at[1]),
        pltpu.make_async_copy(
            down.at[pl.ds(pl.multiple_of(d * rows, 16), rows), :],
            q_all.at[pl.ds(2 * rows, rows), :],
            sems.at[2],
        ),
    ]
    for copy in copies:
        copy.start()

    @pl.when(d < 3)
    def _():
        copy = pltpu.make_async_copy(proj.at[:, at_proj], q_po, sems.at[3])
        copy.start()
        copy.wait()

    @pl.when(d == 3)
    def _():
        copy = pltpu.make_async_copy(outw, q_po, sems.at[3])
        copy.start()
        copy.wait()

    for copy in copies:
        copy.wait()
    c = c_in[...].astype(F32)
    c = c / (1.0 + jnp.exp(-c))
    blank = jnp.zeros((16 - c.shape[0], width), F32)
    q_all[3 * rows :, :] = jnp.concatenate([c, blank], axis=0).astype(BF16)


def one_hot(shape, shift):
    r = lax.broadcasted_iota(jnp.int32, shape, 0)
    c = lax.broadcasted_iota(jnp.int32, shape, 1)
    return jnp.where(c == r + shift, 1.0, 0.0).astype(BF16)


def prepare_body(wmod_own, wmod_other, f0, f1, f2, f3, f4, wmod, placed):
    f = lax.axis_index("fsdp")
    shard = wmod_own.shape[0]
    wmod[0:shard, :] = wmod_own[...]
    wmod[shard:, :] = wmod_other[...]
    rows = []
    for ref in (f0, f1, f2, f3, f4):
        size = ref.shape[0]
        rows.append(dot(ref[...].reshape(1, size), one_hot((size, 8 * size), f * size)))
    bias, b_qv, b_out, b_up, b_down = rows
    feat = b_out.shape[1]
    placed[0:1, :] = bias
    placed[1:2, :] = jnp.concatenate([b_up, b_qv], axis=1)
    placed[2:3, :] = jnp.concatenate([b_out, b_down, jnp.zeros((1, 4 * feat), F32)], axis=1)


def mod_body(ids, q0, q2, q1, q3, wmod, placed, placed_other, keep_lo, keep_hi, c_own):
    f = ids[1]
    rows, wide = wmod.shape
    slots, feat = c_own.shape[0] // 4, c_own.shape[1]
    shard = rows // 2
    at = q0.shape[0] - 16
    r = lax.broadcasted_iota(jnp.int32, (feat, rows), 0)
    c = lax.broadcasted_iota(jnp.int32, (feat, rows), 1)
    start = jnp.where(c < shard, f * shard, flip(f, 1) * shard - shard)
    select = jnp.where(r == c + start, 1.0, 0.0).astype(BF16)
    stacked = jnp.concatenate([ref[at : at + slots, :] for ref in (q0, q2, q1, q3)], axis=0)
    c_own[...] = stacked
    bias = placed[...] + placed_other[...]
    part = dot(dot(stacked, select).astype(BF16), wmod[...]) + bias[0:1]
    for n in range(4):
        keep = (keep_lo, keep_lo, keep_hi, keep_hi)[n]
        keep[n % 2, 0:slots, :] = part[slots * n : slots * (n + 1)]
        keep[n % 2, 2:4, :] = bias[1:3]


def norm_parts(x):
    mean = jnp.mean(x, axis=-1, keepdims=True)
    centered = x - mean
    rstd = lax.rsqrt(jnp.mean(centered * centered, axis=-1, keepdims=True) + 1e-06)
    return centered * rstd, rstd


def lane_masks(rows):
    lane = lax.broadcasted_iota(jnp.int32, (rows, 2 * HEAD_DIM), 1)
    return lane < HEAD_DIM


def attend_body(
    ids, *refs,
):
    d, f, mine, theirs = offsets(ids)
    pieces, (m_proj, m_out, o_proj, o_out, p0, p1, lat, wpo, mod, n1, proj, att) = refs[:8], refs[8:]
    rows, feat = m_out.shape
    whole = ((m_proj, m_out), (o_proj, o_out))
    split = (pieces[:4], mine, f), (pieces[4:], theirs, flip(f, 1))
    for (p_ref, o_ref), (found, flips, base) in zip(whole, split):
        at = pl.multiple_of(base * rows, 16)
        for block in range(3):
            wpo[block, pl.ds(at, rows), :] = p_ref[:, block * feat : (block + 1) * feat]
        wpo[3, pl.ds(at, rows), :] = o_ref[...]
        for n, how in enumerate(flips):
            block = flip(d, how)
            for place, zm in enumerate(LEVELS[1:]):
                get = found[n].at[place]
                at = pl.multiple_of(flip(base, 2 * zm) * rows, 16)
                wpo[block, pl.ds(at, rows), :] = get[0:rows, :]
    mod[...] = p0[0] + p1[...]
    length = lat.shape[1]
    low_half = lane_masks(length)
    qv = mod[2:3, 4 * feat :]

    for i in range(lat.shape[0]):
        xhat, rstd = norm_parts(lat[i].astype(F32))
        row = mod[i : i + 1, :]
        n1[i * length : (i + 1) * length, :] = (
            xhat * (1.0 + row[:, feat : 2 * feat]) + row[:, :feat]
        ).astype(BF16)
    proj[:, 0:feat] = (dot(n1[...], wpo[0]) + qv[:, :feat]).astype(BF16)
    proj[:, feat : 2 * feat] = dot(n1[...], wpo[1]).astype(BF16)
    proj[:, 2 * feat :] = (dot(n1[...], wpo[2]) + qv[:, feat:]).astype(BF16)

    def one(i, carry):
        at = i * length
        for pair in range(HEADS // 2):
            lo = pair * 2 * HEAD_DIM
            hi = lo + 2 * HEAD_DIM
            q = proj[pl.ds(at, length), lo:hi]
            k = proj[pl.ds(at, length), feat + lo : feat + hi]
            v = proj[pl.ds(at, length), 2 * feat + lo : 2 * feat + hi]
            zero = jnp.zeros_like(q)
            outs = []
            for side in range(2):
                q_one = jnp.where(low_half, q, zero) if side == 0 else jnp.where(low_half, zero, q)
                s = dot(q_one, k, NT) * HEAD_DIM ** (-0.5)
                e = jnp.exp(s - jnp.max(s, axis=-1, keepdims=True))
                inv = 1.0 / jnp.sum(e, axis=-1, keepdims=True)
                outs.append(dot((e * inv).astype(BF16), v))
            att[pl.ds(at, length), lo:hi] = jnp.where(low_half, outs[0], outs[1]).astype(BF16)
        return carry

    for i in range(lat.shape[0]):
        one(i, 0)


def spread(tmp, at_row, dm, pieces, rows, f, slot=None):
    keep_odd, keep_even, send_odd, send_even = pieces
    keep = (keep_even, keep_odd)[dm % 2]
    swapped = (0, 2, 1, 3)[dm]
    send = (send_even, send_odd)[swapped % 2]
    for place, zm in enumerate(LEVELS):
        for ref, at, owner in (
            (keep, dm // 2, flip(f, 2 * zm)),
            (send, swapped // 2, flip(f, 2 * zm + 1)),
        ):
            piece = tmp[pl.ds(pl.multiple_of(at_row(owner), 16), rows), :]
            if slot is None:
                ref[at, place] = piece
            else:
                ref[at, place, slot] = piece


def mlp_body(
    ids, *refs,
):
    mlp_steps(ids, refs[:8], *refs[8:])


def mlp_steps(
    ids, pieces, m_up, m_down, o_up, o_down, wout, mod, lat, cot, att,
    res, gmid, gbr, gatt, gsum, gmod, k_odd, k_even, s_odd, s_even,
    wu, wd, n2s, acts, dgs, gmlps, gpres, n2t, tmp, tmpd, brs, xhats, rstds, mlps,
):
    d, f, mine, theirs = offsets(ids)
    count = ids[2]
    rows, feat = m_up.shape[0], m_down.shape[1]
    hidden = wd.shape[0]
    blocks = hidden // feat
    step = 512
    whole = ((m_up, m_down), (o_up, o_down))
    split = (pieces[:4], mine, f), (pieces[4:], theirs, flip(f, 1))
    for (u_ref, d_ref), (found, flips, base) in zip(whole, split):
        at = pl.multiple_of(base * rows, 16)
        wu[pl.ds(at, rows), :] = u_ref[...]
        wd[pl.ds(pl.multiple_of(base * 4 * rows, 16), 4 * rows), :] = d_ref[...]
        for n, how in enumerate(flips):
            block = flip(d, how)
            for place, zm in enumerate(LEVELS[1:]):
                get = found[n].at[place]
                owner = flip(base, 2 * zm)
                wu[
                    pl.ds(pl.multiple_of(owner * rows, 16), rows),
                    pl.ds(pl.multiple_of(block * feat, 128), feat),
                ] = get[rows : 2 * rows, :]
                at = pl.multiple_of((owner * 4 + block) * rows, 16)
                wd[pl.ds(at, rows), :] = get[2 * rows : 3 * rows, :]
    length = lat.shape[1]
    bup = mod[2:3, : 4 * feat]
    bout = mod[3:4, :feat]
    bdown = mod[3:4, feat : 2 * feat]
    members = lat.shape[0]

    def rows_of(i):
        row = mod[i : i + 1, :]
        return (row[:, j * feat : (j + 1) * feat] for j in (2, 3, 4, 5))

    brs[...] = dot(att[...], wout[0]) + bout
    for i in range(members):
        part = slice(i * length, (i + 1) * length)
        gate_one, shift, scale, _ = rows_of(i)
        middle = lat[i].astype(F32) + gate_one * brs[part, :]
        xhat, rstd = norm_parts(middle)
        gmid[i] = middle
        xhats[part, :] = xhat
        rstds[part, :] = jnp.broadcast_to(rstd, (length, 128))
        n2s[part, :] = (xhat * (1.0 + scale) + shift).astype(BF16)
    mlp = None
    for j in range(0, hidden, step):
        cols = slice(j, j + step)
        v = dot(n2s[...], wu[:, cols]) + bup[:, cols]
        square = v * v
        half = 0.5 + 0.5 * jnp.tanh(v * (0.7978845608028654 + 0.035677408136300125 * square))
        act = (v * half).astype(BF16)
        slope = v * (1.5957691216057308 + 0.21406444881780075 * square)
        dgs[:, cols] = half * (1.0 + (1.0 - half) * slope)
        acts[:, cols] = act
        term = dot(act, wd[cols, :])
        mlp = term if mlp is None else mlp + term
    mlps[...] = mlp + bdown
    g_gate_two = []
    for i in range(members):
        part = slice(i * length, (i + 1) * length)
        gate_two = list(rows_of(i))[3]
        alive = jnp.where(i < count, 1.0, 0.0).astype(F32)
        mlp = mlps[part, :]
        res[i] = (alive * (gmid[i] + gate_two * mlp)).astype(BF16)
        upstream = alive * cot[i].astype(F32)
        g_gate_two.append(jnp.sum(upstream * mlp, axis=0, keepdims=True))
        gmlps[part, :] = (gate_two * upstream).astype(BF16)
    gn = None
    for j in range(0, hidden, step):
        cols = slice(j, j + step)
        gpre = (dot(gmlps[...], wd[cols, :], NT) * dgs[:, cols]).astype(BF16)
        gpres[:, cols] = gpre
        term = dot(gpre, wu[:, cols], NT)
        gn = term if gn is None else gn + term
        gsum[:, feat + j : feat + j + step] = jnp.sum(gpre.astype(F32), axis=0, keepdims=True)
    mlps[...] = gn
    for i in range(members):
        part = slice(i * length, (i + 1) * length)
        gate_one, _, scale, _ = rows_of(i)
        alive = jnp.where(i < count, 1.0, 0.0).astype(F32)
        gn, xhat = mlps[part, :], xhats[part, :]
        g_shift = jnp.sum(gn, axis=0, keepdims=True)
        g_scale = jnp.sum(gn * xhat, axis=0, keepdims=True)
        gx = gn * (1.0 + scale)
        gmiddle = alive * cot[i].astype(F32) + rstds[part, 0:1] * (
            gx
            - jnp.mean(gx, axis=-1, keepdims=True)
            - xhat * jnp.mean(gx * xhat, axis=-1, keepdims=True)
        )
        gmid[i] = gmiddle
        g_gate_one = jnp.sum(gmiddle * brs[part, :], axis=0, keepdims=True)
        gbr[part, :] = (gate_one * gmiddle).astype(BF16)
        gmod[i : i + 1, :] = jnp.concatenate([g_gate_one, g_shift, g_scale, g_gate_two[i]], axis=1)
    gatt[...] = dot(gbr[...], wout[0], NT).astype(BF16)
    gsum[:, 0:feat] = jnp.sum(gbr[...].astype(F32), axis=0, keepdims=True)
    gsum[:, 5 * feat : 6 * feat] = jnp.sum(gmlps[...].astype(F32), axis=0, keepdims=True)
    pieces = (k_odd, k_even, s_odd, s_even)
    n2t[...] = n2s[...].T
    for j in range(0, hidden, step):
        cols = slice(j, j + step)
        tmpd[cols, :] = dot(acts[:, cols], gmlps[...], TN).astype(BF16)
        tmp[:, cols] = dot(n2t[...], gpres[:, cols]).astype(BF16)
    for dm in range(4):
        block = flip(d, mine[dm])
        spread(tmpd, lambda o: (o * 4 + block) * rows, dm, pieces, rows, f, 1)
        cut = pl.ds(pl.multiple_of(block * feat, 128), feat)
        spread(tmp.at[:, cut], lambda o: o * rows, dm, pieces, rows, f, 0)


def attend_back_one(proj, gatt, gall, i, length):
    feat = gatt.shape[1]
    low_half = lane_masks(length)

    def one(i, carry):
        part = slice(i * length, (i + 1) * length)
        for pair in range(HEADS // 2):
            lo = pair * 2 * HEAD_DIM
            hi = lo + 2 * HEAD_DIM
            q = proj[part, lo:hi]
            k = proj[part, feat + lo : feat + hi]
            v = proj[part, 2 * feat + lo : 2 * feat + hi]
            ga = gatt[part, lo:hi]
            zero = jnp.zeros_like(q)
            gq = jnp.zeros(q.shape, F32)
            gk = jnp.zeros(q.shape, F32)
            gv = jnp.zeros(q.shape, F32)
            for side in range(2):
                own = lambda a: (
                    jnp.where(low_half, a, zero) if side == 0 else jnp.where(low_half, zero, a)
                )
                q_one, ga_one = own(q), own(ga)
                s = dot(k, q_one, NT) * HEAD_DIM ** (-0.5)
                e = jnp.exp(s - jnp.max(s, axis=0, keepdims=True))
                prob = e * (1.0 / jnp.sum(e, axis=0, keepdims=True))
                gv = gv + dot(prob.astype(BF16), ga_one)
                gp = dot(v, ga_one, NT)
                delta = jnp.sum(gp * prob, axis=0, keepdims=True)
                gs = (prob * (gp - delta)).astype(BF16)
                gk = gk + dot(gs, q_one)
                gq = gq + dot(gs, own(k), TN)
            gall[part, lo:hi] = (gq * HEAD_DIM ** (-0.5)).astype(BF16)
            gall[part, feat + lo : feat + hi] = (gk * HEAD_DIM ** (-0.5)).astype(BF16)
            gall[part, 2 * feat + lo : 2 * feat + hi] = gv.astype(BF16)
        return carry

    one(i, 0)


def attend_back_first_body(proj, gatt, gproj, *, length):
    attend_back_one(proj, gatt, gproj, 0, length)


def attend_back_body(
    ids, proj, gatt, att, gbr, n1, gsum, g_first, gproj, bias, k_odd, k_even, s_odd, s_even,
    gall, xts, tmp, *, length,
):
    d, f, mine, _ = offsets(ids)
    feat = att.shape[1]
    rows = k_odd.shape[2]
    gall[0:length, : 3 * feat] = g_first[...]
    for i in range(1, proj.shape[0] // length):
        attend_back_one(proj, gatt, gall, i, length)
    gproj[...] = gall[:, : 3 * feat]
    gall[:, 3 * feat :] = gbr[...]
    xts[0] = n1[...].T
    xts[1] = att[...].T
    pieces = (k_odd, k_even, s_odd, s_even)
    for dm in (1, 3, 0, 2):
        block = flip(d, mine[dm])
        tmp[...] = dot(
            xts[jnp.where(block == 3, 1, 0)],
            gall[:, pl.ds(pl.multiple_of(block * feat, 128), feat)],
        ).astype(BF16)
        spread(tmp, lambda o: o * rows, dm, pieces, rows, f)
    bias[:, 0:feat] = jnp.sum(gall[:, 0:feat].astype(F32), axis=0, keepdims=True)
    bias[:, feat : 2 * feat] = jnp.sum(
        gall[:, 2 * feat : 3 * feat].astype(F32), axis=0, keepdims=True
    )
    bias[:, 2 * feat :] = gsum[...]


def input_back_body(ids, gproj, wpo, lat, gmid, mod, gmod, bias, lgrad, gm, full):
    length = lat.shape[1]
    feat = lat.shape[2]

    def one(i, carry):
        part = pl.ds(i * length, length)
        row = mod[pl.ds(i, 1), :]
        xhat, rstd = norm_parts(lat[i].astype(F32))
        gn = dot(gproj[part, 0:feat], wpo[0], NT)
        gn = gn + dot(gproj[part, feat : 2 * feat], wpo[1], NT)
        gn = gn + dot(gproj[part, 2 * feat :], wpo[2], NT)
        g_shift = jnp.sum(gn, axis=0, keepdims=True)
        g_scale = jnp.sum(gn * xhat, axis=0, keepdims=True)
        gx = gn * (1.0 + row[:, feat : 2 * feat])
        lgrad[i] = (
            gmid[i]
            + rstd
            * (
                gx
                - jnp.mean(gx, axis=-1, keepdims=True)
                - xhat * jnp.mean(gx * xhat, axis=-1, keepdims=True)
            )
        ).astype(BF16)
        full[pl.ds(i, 1), : 6 * feat] = jnp.concatenate(
            [g_shift, g_scale, gmod[pl.ds(i, 1), :]], axis=1
        )
        return carry

    for i in range(lat.shape[0]):
        one(i, 0)
    full[0:1, 6 * feat :] = bias[:, : 4 * feat]
    full[1:2, 6 * feat :] = bias[:, 4 * feat :]
    gm[...] = full[...].astype(BF16)


def cond_back_body(ids, g0, g2, g1, g3, wmod, lo, hi):
    f = ids[1]
    rows, wide = wmod.shape
    many = g0.shape[0]
    place = one_hot((rows, lo.shape[2]), f * rows)
    grads = jnp.concatenate([ref[:, :wide] for ref in (g0, g2, g1, g3)], axis=0)
    whole = dot(dot(grads, wmod[...], NT).astype(BF16), place).astype(BF16)
    for n, (out, at) in enumerate(((lo, 0), (lo, 1), (hi, 0), (hi, 1))):
        out[at] = jnp.zeros(out.shape[1:], BF16)
        out[at, 0:many, :] = whole[many * n : many * (n + 1)]


def mod_weight_body(ids, e0, e1, e2, e3, wgrad, b_mod, b_qv, b_out, b_up, b_down):
    f = ids[1]
    rows, wide = wgrad.shape
    feat = wide // 6
    grad_wide = e0.shape[1] - feat
    select = one_hot((rows, feat), f * rows)
    total = None
    sums = None
    for ref in (e0, e1, e2, e3):
        own = dot(select, ref[:, grad_wide:], NT).astype(BF16)
        term = dot(own, ref[:, :wide])
        total = term if total is None else total + term
        low = ref[:, :grad_wide].astype(F32)
        sums = low if sums is None else sums + low
    wgrad[...] = total
    low = sums[:, wide:]
    odd = lax.broadcasted_iota(jnp.int32, low.shape, 0) % 2 == 1
    even_sum = jnp.sum(jnp.where(odd, 0.0, low), axis=0, keepdims=True)
    odd_sum = jnp.sum(jnp.where(odd, low, 0.0), axis=0, keepdims=True)
    whole = jnp.concatenate([jnp.sum(sums[:, :wide], axis=0, keepdims=True), even_sum, odd_sum], axis=1)
    at = 0
    for out in (b_mod, b_qv, b_out, b_up, b_down):
        size = out.shape[0]
        vector = jnp.broadcast_to(whole[:, at : at + 8 * size], (8, 8 * size))
        out[...] = pltpu.roll(vector, lax.rem(8 - f, 8) * size, 1)[0, :size]
        at += 8 * size


def sum_body(keep, got, out):
    out[...] = add_low(keep[...], got[...])


def turn_body(keep_ud, in_ud, keep_po, in_po, got_ud, got_po, out, *, at):
    rows = keep_po.shape[2]
    for place in range(out.shape[0]):
        out[place, 0:rows] = add_low(keep_po[at, place], in_po[at, place], got_po[at, place])
        for slot in range(2):
            out[place, (1 + slot) * rows : (2 + slot) * rows] = add_low(
                keep_ud[at, place, slot], in_ud[at, place, slot], got_ud[at, place, slot]
            )


def stack_body(q2, q1, q3, out):
    for n, ref in enumerate((q2, q1, q3)):
        out[n] = ref[0 : out.shape[1], :]


def pair_body(own, other, out):
    out[0 : own.shape[0], :] = own[...]
    out[own.shape[0] :, :] = other[...]


def pack_body(g0, g2, g1, g3, c_own, c_other, out):
    many, wide = g0.shape
    half = many // 2
    for n, ref in enumerate((g0, g2, g1, g3)):
        out[many * n : many * (n + 1), 0:wide] = ref[...]
        out[many * n : many * n + half, wide:] = c_own[half * n : half * (n + 1), :]
        out[many * n + half : many * (n + 1), wide:] = c_other[half * n : half * (n + 1), :]


def join_far_body(base, part, back, out):
    size = base.shape[1]
    out[:, 0:size] = add_low(base[2:], part[2:])
    out[:, size:] = back[...]


def join_near_body(base, part, back, got, out, far):
    size = base.shape[1]
    for at, ref in enumerate((out, far)):
        ref[0:size, :] = add_low(base[at], part[at], got[at, 0:size])
        ref[size:, :] = add_low(back[at], got[at, size:])


def total_body(base, got, out, back):
    size = out.shape[0]
    out[...] = add_low(base[0:size, :], got[0:size, :])
    back[...] = base[size:, :].astype(F32) + got[size:, :].astype(F32)


def final_body(ids, g0, g1, g2, g3, gp, go, gu, gd):
    d, _, mine, _ = offsets(ids)
    rows, feat = go.shape
    for ref, how in zip((g0, g1, g2, g3), mine):
        block = flip(d, how)

        @pl.when(block < 3)
        def _():
            at = pl.multiple_of(lax.min(block, 2) * feat, 128)
            gp[:, pl.ds(at, feat)] = ref[0:rows, :].astype(F32)

        @pl.when(block == 3)
        def _():
            go[...] = ref[0:rows, :].astype(F32)

        gu[:, pl.ds(pl.multiple_of(block * feat, 128), feat)] = ref[rows : 2 * rows, :].astype(F32)
        gd[pl.ds(pl.multiple_of(block * rows, 16), rows), :] = ref[2 * rows : 3 * rows, :].astype(F32)


def routes():
    core, first, second, across = [], [], [], []
    levels = {1: [], 2: []}
    for d in range(4):
        for f in range(8):
            i = d * 8 + f
            core.append((i, i ^ 1))
            a = 1 if f % 2 == 0 else 2
            first.append((i, (d ^ a) * 8 + f))
            second.append((i, (d ^ (3 - a)) * 8 + f))
            across.append((i, (d ^ 3) * 8 + f))
            for m in levels:
                levels[m].append((i, d * 8 + (f ^ (2 * m))))
    return core, first, second, across, levels


def add_low(*parts):
    total = parts[0].astype(F32)
    for part in parts[1:]:
        total = total + part.astype(F32)
    return total.astype(BF16)


def on_device_blocks(
    latents, cond, counts, cotangent, modulation_weight, modulation_bias, projection_weight,
    query_value_bias, output_weight, output_bias, up_weight, up_bias, down_weight, down_bias,
):
    core, first, second, across, levels = routes()

    def move(x, route):
        return lax.ppermute(x, BOTH, route)

    slots, length, feat = latents.shape
    rows = projection_weight.shape[0]
    hidden = up_weight.shape[1]
    wide = modulation_weight.shape[1]
    tokens = slots * length
    d = lax.axis_index("dp")
    f = lax.axis_index("fsdp")
    ids = jnp.stack([d, f, counts[0]]).astype(jnp.int32)

    def after(x, *earlier):
        return lax.optimization_barrier((x,) + earlier)[0]

    (q_all,) = call(
        pick_body, "pick", None,
        [projection_weight, output_weight, up_weight, down_weight, cond],
        [((3 * rows + 16, feat), BF16)],
        [pltpu.VMEM((slots, feat), BF16), pltpu.SemaphoreType.DMA((4,))],
        far=(0, 1, 2, 3, 4), limit=60,
    )

    def over_dp(own):
        a = move(own, first)
        b = move(own, second)
        return [own, a, b, move(a, second)]

    whole = [projection_weight, output_weight, up_weight, down_weight]
    w_whole = whole + [move(after(x, q_all), core) for x in whole]
    biases = [modulation_bias, query_value_bias, output_bias, up_bias, down_bias]
    wmod, placed = call(
        prepare_body, "prepare", None, [modulation_weight, move(after(modulation_weight, q_all), core)] + biases,
        [((2 * rows, wide), BF16), ((3, wide), F32)],
    )
    q_far = move(q_all, levels[2])
    placed_other = move(placed, core)
    ready = (placed_other, *w_whole[4:])
    q_far = after(q_far, *ready)
    q_near, q_both = move(after(q_all, q_far), levels[1]), move(q_far, levels[1])
    (own,) = call(stack_body, "stack", None, [q_far, q_near, q_both], [((3, 3 * rows, feat), BF16)])
    keep_lo, keep_hi, c_own = call(
        mod_body, "modulation", ids, [q_all, q_far, q_near, q_both, wmod, placed, placed_other],
        [((2, 4, wide), F32)] * 2 + [((4 * slots, feat), BF16)],
    )
    a_own, b_own = move(own, first), move(own, second)
    paid_lo = keep_lo + move(keep_hi, levels[1])
    a_own = after(a_own, paid_lo)
    paid_far = move(after(paid_lo[1], a_own), levels[2])
    ab_own = move(a_own, second)
    w_all = [own, a_own, b_own, ab_own]
    w_all = w_all + [move(x, core) for x in w_all[:3]] + [move(after(ab_own, paid_far), core)]

    wpo, mod, n1, proj, att = call(
        attend_body, "attention", ids,
        w_all + [w_whole[k] for k in (0, 1, 4, 5)] + [paid_lo, paid_far, latents],
        [((4, feat, feat), BF16), ((4, wide), F32), ((tokens, feat), BF16),
         ((tokens, 3 * feat), BF16), ((tokens, feat), BF16)],
        flops=2 * tokens * feat * (3 * feat + 4 * length),
    )
    wout = wpo[3:4]
    ud_shape = ((2, 4, 2, rows, feat), BF16)
    po_shape = ((2, 4, rows, feat), BF16)
    res, gmid, gbr, gatt, gsum, gmod, ud_odd, ud_even, ud_odd_out, ud_even_out = call(
        mlp_body, "mlp", ids,
        w_all + [w_whole[k] for k in (2, 3, 6, 7)] + [wout, mod, latents, cotangent, att],
        [((slots, length, feat), BF16), ((slots, length, feat), F32), ((tokens, feat), BF16),
         ((tokens, feat), BF16), ((1, 6 * feat), F32), ((slots, 4 * feat), F32)] + [ud_shape] * 4,
        [
            pltpu.VMEM((feat, hidden), BF16), pltpu.VMEM((hidden, feat), BF16),
            pltpu.VMEM((tokens, feat), BF16), pltpu.VMEM((tokens, hidden), BF16),
            pltpu.VMEM((tokens, hidden), F32), pltpu.VMEM((tokens, feat), BF16),
            pltpu.VMEM((tokens, hidden), BF16), pltpu.VMEM((feat, tokens), BF16),
            pltpu.VMEM((feat, hidden), BF16), pltpu.VMEM((hidden, feat), BF16),
            pltpu.VMEM((tokens, feat), F32), pltpu.VMEM((tokens, feat), F32),
            pltpu.VMEM((tokens, 128), F32), pltpu.VMEM((tokens, feat), F32),
        ],
        flops=2 * tokens * feat * (6 * hidden + 2 * feat),
    )
    ud_odd_in = move(ud_odd_out, core)
    ud_even_in = move(ud_even_out, core)
    (g_first,) = call(
        functools.partial(attend_back_first_body, length=length), "attention_back_first", None,
        [proj, gatt], [((length, 3 * feat), BF16)], flops=tokens * feat * 10 * length,
    )
    (odd_ud,) = call(sum_body, "sum_ud", None, [ud_odd, after(ud_odd_in, g_first)], [ud_shape])
    got_ud = move(odd_ud, first)
    gproj, bias, po_odd, po_even, po_odd_out, po_even_out = call(
        functools.partial(attend_back_body, length=length), "attention_back", ids,
        [proj, gatt, att, gbr, n1, gsum, after(g_first, odd_ud)],
        [((tokens, 3 * feat), BF16), ((1, 8 * feat), F32)] + [po_shape] * 4,
        [pltpu.VMEM((tokens, 4 * feat), BF16), pltpu.VMEM((2, feat, tokens), BF16),
         pltpu.VMEM((feat, feat), BF16)],
        flops=2 * tokens * feat * (4 * feat + 5 * length),
    )
    po_odd_in = move(po_odd_out, core)
    po_even_in = move(po_even_out, core)
    lgrad, gm = call(
        input_back_body, "input_back", ids,
        [gproj, wpo, latents, gmid, mod, gmod, bias],
        [((slots, length, feat), BF16), ((slots, 10 * feat), BF16)],
        [pltpu.VMEM((slots, 10 * feat), F32)],
        flops=2 * tokens * feat * 3 * feat,
    )
    (odd_po,) = call(sum_body, "sum_po", None, [po_odd, after(po_odd_in, gm, got_ud)], [po_shape])
    got_po = move(odd_po, first)
    c_other = move(c_own, core)

    (gm_pair,) = call(pair_body, "pair", None, [after(gm, c_other), move(gm, core)], [((2 * slots, 10 * feat), BF16)])
    gm_far = move(gm_pair, levels[2])

    halves = [ud_even, ud_even_in, po_even, po_even_in, got_ud, after(got_po, gm_far)]
    half_shape = ((4, 3 * rows, feat), BF16)
    (turned,) = call(functools.partial(turn_body, at=1), "turn", None, halves, [half_shape])
    part = move(turned, second)
    (base,) = call(
        functools.partial(turn_body, at=0), "base", None, halves[:5] + [after(got_po, turned)], [half_shape]
    )

    gm_all = [gm_pair, gm_far, move(after(gm_pair, gm_far), levels[1]), move(gm_far, levels[1])]
    (every,) = call(
        pack_body, "pack", None, gm_all + [c_own, c_other], [((8 * slots, 11 * feat), BF16)]
    )
    back_lo, back_hi = call(
        cond_back_body, "cond_back", ids, gm_all + [modulation_weight], [((2, 16, feat), BF16)] * 2
    )

    pair_shape = ((2, 3 * rows + 16, feat), BF16)
    (turned,) = call(join_far_body, "join_far", None, [base, part, back_hi], [pair_shape])
    got = move(turned, levels[1])
    every = after(every, turned)
    e_first, e_second, e_both = move(every, first), move(every, second), move(every, across)
    base, far = call(
        join_near_body, "join_near", None, [base, part, back_lo, got], [((3 * rows + 16, feat), BF16)] * 2
    )
    g_mod_weight, *g_biases = call(
        mod_weight_body, "mod_weight", ids, [every, e_first, e_second, e_both],
        [((rows, wide), F32)] + [((size // 8,), F32) for size in (wide, 2 * feat, feat, hidden, feat)],
    )
    total, back = call(
        total_body, "total", None, [base, after(move(far, levels[2]), g_mod_weight)],
        [((3 * rows, feat), BF16), ((16, feat), F32)],
    )
    a_total, b_total = move(total, first), move(total, second)
    shares = [total, a_total, b_total, move(total, across)]
    grad_silu = back[:slots] + move(back[slots : 2 * slots], core)
    cond_full = cond.astype(F32)
    sig = 1.0 / (1.0 + jnp.exp(-cond_full))
    cond_grad = (grad_silu * (sig * (1.0 + cond_full * (1.0 - sig)))).astype(BF16)
    g_proj, g_out, g_up, g_down = call(
        final_body, "final", ids, shares,
        [((rows, 3 * feat), F32), ((rows, feat), F32), ((rows, hidden), F32),
         ((4 * rows, feat), F32)],
    )
    return (
        res, lgrad, cond_grad, g_mod_weight, g_biases[0], g_proj, g_biases[1],
        g_out, g_biases[2], g_up, g_biases[3], g_down, g_biases[4],
    )


def layer_norm(vector):
    row_mean = jnp.mean(vector, axis=-1, keepdims=True)
    centered = vector - row_mean
    variance = jnp.mean(centered * centered, axis=-1, keepdims=True)
    return centered * lax.rsqrt(variance + 1e-06)


def modulate(vector, offset, stretch):
    return layer_norm(vector) * (1.0 + stretch[:, None, :]) + offset[:, None, :]


def forward_pass(gathered, inputs, conditions):
    (
        modulation_weight,
        modulation_bias,
        projection_weight,
        query_value_bias,
        output_weight,
        output_bias,
        up_weight,
        up_bias,
        down_weight,
        down_bias,
    ) = gathered
    members, length, features = inputs.shape
    flat_rows = members * length
    cond_low = jax.nn.silu(conditions).astype(jnp.bfloat16)
    modulation = jnp.dot(cond_low, modulation_weight, preferred_element_type=jnp.float32)
    modulation = modulation + modulation_bias.astype(jnp.float32)
    pieces = jnp.split(modulation, 6, axis=-1)
    normed_one = (
        modulate(inputs, pieces[0], pieces[1]).astype(jnp.bfloat16).reshape(flat_rows, features)
    )
    bias_full = query_value_bias.astype(jnp.float32)
    joined_bias = jnp.concatenate(
        [bias_full[:features], jnp.zeros((features,), jnp.float32), bias_full[features:]]
    )
    projected = (
        jnp.dot(normed_one, projection_weight, preferred_element_type=jnp.float32) + joined_bias
    )
    projected = projected.astype(jnp.bfloat16).reshape(members, length, 3, HEADS, HEAD_DIM)
    queries = projected[:, :, 0]
    key_rows = projected[:, :, 1]
    values = projected[:, :, 2]
    scores = jnp.einsum(
        "bqhd,bkhd->bhqk", queries, key_rows, preferred_element_type=jnp.float32
    ) * HEAD_DIM ** (-0.5)
    row_max = jnp.max(scores, axis=-1, keepdims=True)
    exponent = jnp.exp(scores - row_max)
    row_total = jnp.sum(exponent, axis=-1, keepdims=True)
    probability = exponent / row_total
    log_total = row_max + jnp.log(row_total)
    attended = jnp.einsum(
        "bhqk,bkhd->bqhd",
        probability.astype(jnp.bfloat16),
        values,
        preferred_element_type=jnp.float32,
    )
    attended = attended.astype(jnp.bfloat16).reshape(flat_rows, features)
    branch = jnp.dot(
        attended, output_weight, preferred_element_type=jnp.float32
    ) + output_bias.astype(jnp.float32)
    branch = branch.reshape(members, length, features)
    middle = inputs + pieces[2][:, None, :] * branch
    normed_two = (
        modulate(middle, pieces[3], pieces[4]).astype(jnp.bfloat16).reshape(flat_rows, features)
    )
    pre_act = jnp.dot(normed_two, up_weight, preferred_element_type=jnp.float32) + up_bias.astype(
        jnp.float32
    )
    activated = jax.nn.gelu(pre_act, approximate=True).astype(jnp.bfloat16)
    mlp_out = jnp.dot(
        activated, down_weight, preferred_element_type=jnp.float32
    ) + down_bias.astype(jnp.float32)
    mlp_out = mlp_out.reshape(members, length, features)
    output = middle + pieces[5][:, None, :] * mlp_out
    return (
        output,
        cond_low,
        pieces,
        normed_one,
        queries,
        key_rows,
        values,
        log_total,
        attended,
        branch,
        middle,
        normed_two,
        pre_act,
        activated,
        mlp_out,
    )


def backward_pass(gathered, saved, inputs, conditions, upstream):
    (
        modulation_weight,
        modulation_bias,
        projection_weight,
        query_value_bias,
        output_weight,
        output_bias,
        up_weight,
        up_bias,
        down_weight,
        down_bias,
    ) = gathered
    (
        output,
        cond_low,
        pieces,
        normed_one,
        queries,
        key_rows,
        values,
        log_total,
        attended,
        branch,
        middle,
        normed_two,
        pre_act,
        activated,
        mlp_out,
    ) = saved
    members, length, features = inputs.shape
    flat_rows = members * length
    grad_gate_two = jnp.sum(upstream * mlp_out, axis=1)
    grad_mlp = (pieces[5][:, None, :] * upstream).astype(jnp.bfloat16).reshape(flat_rows, features)
    grad_down = jnp.einsum("nf,nd->fd", activated, grad_mlp, preferred_element_type=jnp.float32)
    grad_down_b = jnp.sum(grad_mlp.astype(jnp.float32), axis=0)
    grad_activated = jnp.einsum(
        "nd,fd->nf", grad_mlp, down_weight, preferred_element_type=jnp.float32
    )
    gelu_out, gelu_pull = jax.vjp(lambda vector: jax.nn.gelu(vector, approximate=True), pre_act)
    grad_pre = gelu_pull(grad_activated)[0].astype(jnp.bfloat16)
    grad_up = jnp.einsum("nd,nf->df", normed_two, grad_pre, preferred_element_type=jnp.float32)
    grad_up_b = jnp.sum(grad_pre.astype(jnp.float32), axis=0)
    grad_normed_two = jnp.einsum(
        "nf,df->nd", grad_pre, up_weight, preferred_element_type=jnp.float32
    )
    second_out, second_pull = jax.vjp(modulate, middle, pieces[3], pieces[4])
    grad_middle, grad_shift_two, grad_scale_two = second_pull(
        grad_normed_two.reshape(members, length, features)
    )
    grad_middle = grad_middle + upstream
    grad_gate_one = jnp.sum(grad_middle * branch, axis=1)
    grad_branch = (
        (pieces[2][:, None, :] * grad_middle).astype(jnp.bfloat16).reshape(flat_rows, features)
    )
    grad_output = jnp.einsum("nd,ne->de", attended, grad_branch, preferred_element_type=jnp.float32)
    grad_output_b = jnp.sum(grad_branch.astype(jnp.float32), axis=0)
    grad_attended = jnp.einsum(
        "ne,de->nd", grad_branch, output_weight, preferred_element_type=jnp.float32
    )
    grad_attended = grad_attended.astype(jnp.bfloat16).reshape(members, length, HEADS, HEAD_DIM)
    scale_factor = HEAD_DIM ** (-0.5)
    scores = (
        jnp.einsum("bqhd,bkhd->bhqk", queries, key_rows, preferred_element_type=jnp.float32)
        * scale_factor
    )
    probability = jnp.exp(scores - log_total)
    grad_values = jnp.einsum(
        "bhqk,bqhd->bkhd",
        probability.astype(jnp.bfloat16),
        grad_attended,
        preferred_element_type=jnp.float32,
    )
    grad_prob = jnp.einsum(
        "bqhd,bkhd->bhqk", grad_attended, values, preferred_element_type=jnp.float32
    )
    row_delta = jnp.sum(grad_prob * probability, axis=-1, keepdims=True)
    grad_scores = (probability * (grad_prob - row_delta)).astype(jnp.bfloat16)
    grad_queries = (
        jnp.einsum("bhqk,bkhd->bqhd", grad_scores, key_rows, preferred_element_type=jnp.float32)
        * scale_factor
    )
    grad_keys = (
        jnp.einsum("bhqk,bqhd->bkhd", grad_scores, queries, preferred_element_type=jnp.float32)
        * scale_factor
    )
    grad_projected = jnp.stack([grad_queries, grad_keys, grad_values], axis=2)
    grad_projected = grad_projected.astype(jnp.bfloat16).reshape(flat_rows, 3 * features)
    grad_projection = jnp.einsum(
        "nd,ne->de", normed_one, grad_projected, preferred_element_type=jnp.float32
    )
    column_sums = jnp.sum(grad_projected.astype(jnp.float32), axis=0)
    grad_query_value = jnp.concatenate([column_sums[:features], column_sums[2 * features :]])
    grad_normed_one = jnp.einsum(
        "ne,de->nd", grad_projected, projection_weight, preferred_element_type=jnp.float32
    )
    first_out, first_pull = jax.vjp(modulate, inputs, pieces[0], pieces[1])
    grad_input, grad_shift_one, grad_scale_one = first_pull(
        grad_normed_one.reshape(members, length, features)
    )
    grad_input = grad_input + grad_middle
    grad_modulation = jnp.concatenate(
        [
            grad_shift_one,
            grad_scale_one,
            grad_gate_one,
            grad_shift_two,
            grad_scale_two,
            grad_gate_two,
        ],
        axis=-1,
    ).astype(jnp.bfloat16)
    grad_mod_weight = jnp.einsum(
        "bc,be->ce", cond_low, grad_modulation, preferred_element_type=jnp.float32
    )
    grad_mod_bias = jnp.sum(grad_modulation.astype(jnp.float32), axis=0)
    grad_silu = jnp.einsum(
        "be,ce->bc", grad_modulation, modulation_weight, preferred_element_type=jnp.float32
    )
    silu_out, silu_pull = jax.vjp(jax.nn.silu, conditions)
    grad_conditions = silu_pull(grad_silu)[0]
    weight_grads = (
        grad_mod_weight,
        grad_mod_bias,
        grad_projection,
        grad_query_value,
        grad_output,
        grad_output_b,
        grad_up,
        grad_up_b,
        grad_down,
        grad_down_b,
    )
    return (weight_grads, grad_input, grad_conditions)


def on_device(
    latents,
    cond,
    counts,
    cotangent,
    modulation_weight,
    modulation_bias,
    projection_weight,
    query_value_bias,
    output_weight,
    output_bias,
    up_weight,
    up_bias,
    down_weight,
    down_bias,
):
    lat_slots = latents.shape[0]
    per_micro = lat_slots // MICRO
    alive_all = (jnp.arange(lat_slots) < counts[0]).astype(jnp.float32)
    kept = (
        lax.all_gather(modulation_weight, "fsdp", axis=0, tiled=True),
        lax.all_gather(modulation_bias, "fsdp", axis=0, tiled=True),
        lax.all_gather(projection_weight, "fsdp", axis=0, tiled=True),
        lax.all_gather(query_value_bias, "fsdp", axis=0, tiled=True),
        lax.all_gather(output_weight, "fsdp", axis=0, tiled=True),
        lax.all_gather(output_bias, "fsdp", axis=0, tiled=True),
        lax.all_gather(up_weight, "fsdp", axis=0, tiled=True),
        lax.all_gather(up_bias, "fsdp", axis=0, tiled=True),
        lax.all_gather(down_weight, "fsdp", axis=0, tiled=True),
        lax.all_gather(down_bias, "fsdp", axis=0, tiled=True),
    )
    outputs = []
    input_grads = []
    cond_grads = []
    totals = None
    for micro_index in range(MICRO):
        start = micro_index * per_micro
        inputs = latents[start : start + per_micro].astype(jnp.float32)
        conditions = cond[start : start + per_micro].astype(jnp.float32)
        alive_mask = alive_all[start : start + per_micro]
        saved = forward_pass(kept, inputs, conditions)
        outputs.append((saved[0] * alive_mask[:, None, None]).astype(jnp.bfloat16))
        upstream = (
            cotangent[start : start + per_micro].astype(jnp.float32) * alive_mask[:, None, None]
        )
        weight_grads, grad_input, grad_conditions = backward_pass(
            kept, saved, inputs, conditions, upstream
        )
        input_grads.append(grad_input.astype(jnp.bfloat16))
        cond_grads.append(grad_conditions.astype(jnp.bfloat16))
        totals = (
            weight_grads
            if totals is None
            else tuple((left + right for left, right in zip(totals, weight_grads)))
        )
    totals = (
        lax.psum_scatter(totals[0], "fsdp", scatter_dimension=0, tiled=True),
        lax.psum_scatter(totals[1], "fsdp", scatter_dimension=0, tiled=True),
        lax.psum_scatter(totals[2], "fsdp", scatter_dimension=0, tiled=True),
        lax.psum_scatter(totals[3], "fsdp", scatter_dimension=0, tiled=True),
        lax.psum_scatter(totals[4], "fsdp", scatter_dimension=0, tiled=True),
        lax.psum_scatter(totals[5], "fsdp", scatter_dimension=0, tiled=True),
        lax.psum_scatter(totals[6], "fsdp", scatter_dimension=0, tiled=True),
        lax.psum_scatter(totals[7], "fsdp", scatter_dimension=0, tiled=True),
        lax.psum_scatter(totals[8], "fsdp", scatter_dimension=0, tiled=True),
        lax.psum_scatter(totals[9], "fsdp", scatter_dimension=0, tiled=True),
    )
    totals = (
        lax.psum(totals[0].astype(jnp.bfloat16), "dp").astype(jnp.float32),
        lax.psum(totals[1].astype(jnp.bfloat16), "dp").astype(jnp.float32),
        lax.psum(totals[2].astype(jnp.bfloat16), "dp").astype(jnp.float32),
        lax.psum(totals[3].astype(jnp.bfloat16), "dp").astype(jnp.float32),
        lax.psum(totals[4].astype(jnp.bfloat16), "dp").astype(jnp.float32),
        lax.psum(totals[5].astype(jnp.bfloat16), "dp").astype(jnp.float32),
        lax.psum(totals[6].astype(jnp.bfloat16), "dp").astype(jnp.float32),
        lax.psum(totals[7].astype(jnp.bfloat16), "dp").astype(jnp.float32),
        lax.psum(totals[8].astype(jnp.bfloat16), "dp").astype(jnp.float32),
        lax.psum(totals[9].astype(jnp.bfloat16), "dp").astype(jnp.float32),
    )
    return (
        jnp.concatenate(outputs, axis=0),
        jnp.concatenate(input_grads, axis=0),
        jnp.concatenate(cond_grads, axis=0),
        totals[0],
        totals[1],
        totals[2],
        totals[3],
        totals[4],
        totals[5],
        totals[6],
        totals[7],
        totals[8],
        totals[9],
    )


def solution(mesh):
    small = mesh.shape["dp"] == 4 and mesh.shape["fsdp"] == 8
    program = on_device_blocks if small else on_device
    placed = (
        P(("dp", "fsdp"), None, None),
        P(("dp", "fsdp"), None),
        P(("dp", "fsdp")),
        P(("dp", "fsdp"), None, None),
        P("fsdp", None),
        P("fsdp"),
        P("fsdp", None),
        P("fsdp"),
        P("fsdp", None),
        P("fsdp"),
        P("fsdp", None),
        P("fsdp"),
        P("fsdp", None),
        P("fsdp"),
    )
    return jax.shard_map(
        program,
        mesh=mesh,
        in_specs=placed,
        out_specs=(
            P(("dp", "fsdp"), None, None),
            P(("dp", "fsdp"), None, None),
            P(("dp", "fsdp"), None),
            P("fsdp", None),
            P("fsdp"),
            P("fsdp", None),
            P("fsdp"),
            P("fsdp", None),
            P("fsdp"),
            P("fsdp", None),
            P("fsdp"),
            P("fsdp", None),
            P("fsdp"),
        ),
        check_vma=False,
    )
```

```python
import functools

import jax
import jax.numpy as jnp
from jax import lax
from jax.experimental import pallas as pl
from jax.experimental.pallas import tpu as pltpu
from jax.sharding import PartitionSpec as P

HEADS = 6
HEAD_DIM = 64
MICRO = 2
F32 = jnp.float32
BF16 = jnp.bfloat16
BOTH = ("dp", "fsdp")
NN = (((1,), (0,)), ((), ()))
NT = (((1,), (1,)), ((), ()))
TN = (((0,), (0,)), ((), ()))
LEVELS = (0, 2, 1, 3)


def dot(left, right, dims=NN):
    return lax.dot_general(left, right, dims, preferred_element_type=F32)


def smem():
    return pl.BlockSpec(memory_space=pltpu.SMEM)


def vmem():
    return pl.BlockSpec(memory_space=pltpu.VMEM)


def hbm():
    return pl.BlockSpec(memory_space=pltpu.HBM)


def call(body, name, ids, ins, outs, scratch=(), flops=0, limit=48, far=()):
    fixed = [] if ids is None else [ids]
    return pl.pallas_call(
        body,
        out_shape=[jax.ShapeDtypeStruct(s, t) for s, t in outs],
        in_specs=[smem()] * len(fixed) + [hbm() if i in far else vmem() for i in range(len(ins))],
        out_specs=[vmem()] * len(outs),
        scratch_shapes=list(scratch),
        compiler_params=pltpu.CompilerParams(vmem_limit_bytes=limit * 1024 * 1024),
        cost_estimate=pl.CostEstimate(flops=1, bytes_accessed=1, transcendentals=0),
        name=name,
    )(*fixed, *ins)


def offsets(ids):
    d, f = ids[0], ids[1]
    core = lax.rem(f, 2)
    first = 1 + core
    second = 2 - core
    return d, f, (0, first, second, 3), (0, second, first, 3)


def flip(a, b):
    return lax.bitwise_xor(a, b)


def pick_body(proj, outw, up, down, cond, q_all, c_in, sems):
    d = lax.axis_index("dp")
    rows, width = outw.shape
    at = pl.ds(pl.multiple_of(d * width, 128), width)
    at_proj = pl.ds(pl.multiple_of(lax.min(d, 2) * width, 128), width)
    q_po = q_all.at[pl.ds(0, rows), :]
    copies = [
        pltpu.make_async_copy(cond, c_in, sems.at[0]),
        pltpu.make_async_copy(up.at[:, at], q_all.at[pl.ds(rows, rows), :], sems.at[1]),
        pltpu.make_async_copy(
            down.at[pl.ds(pl.multiple_of(d * rows, 16), rows), :],
            q_all.at[pl.ds(2 * rows, rows), :],
            sems.at[2],
        ),
    ]
    for copy in copies:
        copy.start()

    @pl.when(d < 3)
    def _():
        copy = pltpu.make_async_copy(proj.at[:, at_proj], q_po, sems.at[3])
        copy.start()
        copy.wait()

    @pl.when(d == 3)
    def _():
        copy = pltpu.make_async_copy(outw, q_po, sems.at[3])
        copy.start()
        copy.wait()

    for copy in copies:
        copy.wait()
    c = c_in[...].astype(F32)
    c = c / (1.0 + jnp.exp(-c))
    blank = jnp.zeros((16 - c.shape[0], width), F32)
    q_all[3 * rows :, :] = jnp.concatenate([c, blank], axis=0).astype(BF16)


def one_hot(shape, shift):
    r = lax.broadcasted_iota(jnp.int32, shape, 0)
    c = lax.broadcasted_iota(jnp.int32, shape, 1)
    return jnp.where(c == r + shift, 1.0, 0.0).astype(BF16)


def prepare_body(wmod_own, wmod_other, f0, f1, f2, f3, f4, wmod, placed):
    f = lax.axis_index("fsdp")
    shard = wmod_own.shape[0]
    wmod[0:shard, :] = wmod_own[...]
    wmod[shard:, :] = wmod_other[...]
    rows = []
    for ref in (f0, f1, f2, f3, f4):
        size = ref.shape[0]
        rows.append(dot(ref[...].reshape(1, size), one_hot((size, 8 * size), f * size)))
    bias, b_qv, b_out, b_up, b_down = rows
    feat = b_out.shape[1]
    placed[0:1, :] = bias
    placed[1:2, :] = jnp.concatenate([b_up, b_qv], axis=1)
    placed[2:3, :] = jnp.concatenate([b_out, b_down, jnp.zeros((1, 4 * feat), F32)], axis=1)


def mod_body(ids, q0, q2, q1, q3, wmod, placed, placed_other, keep_lo, keep_hi, c_own):
    f = ids[1]
    rows, wide = wmod.shape
    slots, feat = c_own.shape[0] // 4, c_own.shape[1]
    shard = rows // 2
    at = q0.shape[0] - 16
    r = lax.broadcasted_iota(jnp.int32, (feat, rows), 0)
    c = lax.broadcasted_iota(jnp.int32, (feat, rows), 1)
    start = jnp.where(c < shard, f * shard, flip(f, 1) * shard - shard)
    select = jnp.where(r == c + start, 1.0, 0.0).astype(BF16)
    stacked = jnp.concatenate([ref[at : at + slots, :] for ref in (q0, q2, q1, q3)], axis=0)
    c_own[...] = stacked
    bias = placed[...] + placed_other[...]
    part = dot(dot(stacked, select).astype(BF16), wmod[...]) + bias[0:1]
    for n in range(4):
        keep = (keep_lo, keep_lo, keep_hi, keep_hi)[n]
        keep[n % 2, 0:slots, :] = part[slots * n : slots * (n + 1)]
        keep[n % 2, 2:4, :] = bias[1:3]


def norm_parts(x):
    mean = jnp.mean(x, axis=-1, keepdims=True)
    centered = x - mean
    rstd = lax.rsqrt(jnp.mean(centered * centered, axis=-1, keepdims=True) + 1e-06)
    return centered * rstd, rstd


def lane_masks(rows):
    lane = lax.broadcasted_iota(jnp.int32, (rows, 2 * HEAD_DIM), 1)
    return lane < HEAD_DIM


def attend_body(
    ids, *refs,
):
    d, f, mine, theirs = offsets(ids)
    pieces, (m_proj, m_out, o_proj, o_out, p0, p1, lat, wpo, mod, n1, proj, att) = refs[:8], refs[8:]
    rows, feat = m_out.shape
    whole = ((m_proj, m_out), (o_proj, o_out))
    split = (pieces[:4], mine, f), (pieces[4:], theirs, flip(f, 1))
    for (p_ref, o_ref), (found, flips, base) in zip(whole, split):
        at = pl.multiple_of(base * rows, 16)
        for block in range(3):
            wpo[block, pl.ds(at, rows), :] = p_ref[:, block * feat : (block + 1) * feat]
        wpo[3, pl.ds(at, rows), :] = o_ref[...]
        for n, how in enumerate(flips):
            block = flip(d, how)
            for place, zm in enumerate(LEVELS[1:]):
                get = found[n].at[place]
                at = pl.multiple_of(flip(base, 2 * zm) * rows, 16)
                wpo[block, pl.ds(at, rows), :] = get[0:rows, :]
    mod[...] = p0[0] + p1[...]
    length = lat.shape[1]
    low_half = lane_masks(length)
    qv = mod[2:3, 4 * feat :]

    for i in range(lat.shape[0]):
        xhat, rstd = norm_parts(lat[i].astype(F32))
        row = mod[i : i + 1, :]
        n1[i * length : (i + 1) * length, :] = (
            xhat * (1.0 + row[:, feat : 2 * feat]) + row[:, :feat]
        ).astype(BF16)
    proj[:, 0:feat] = (dot(n1[...], wpo[0]) + qv[:, :feat]).astype(BF16)
    proj[:, feat : 2 * feat] = dot(n1[...], wpo[1]).astype(BF16)
    proj[:, 2 * feat :] = (dot(n1[...], wpo[2]) + qv[:, feat:]).astype(BF16)

    def one(i, carry):
        at = i * length
        for pair in range(HEADS // 2):
            lo = pair * 2 * HEAD_DIM
            hi = lo + 2 * HEAD_DIM
            q = proj[pl.ds(at, length), lo:hi]
            k = proj[pl.ds(at, length), feat + lo : feat + hi]
            v = proj[pl.ds(at, length), 2 * feat + lo : 2 * feat + hi]
            zero = jnp.zeros_like(q)
            outs = []
            for side in range(2):
                q_one = jnp.where(low_half, q, zero) if side == 0 else jnp.where(low_half, zero, q)
                s = dot(q_one, k, NT) * HEAD_DIM ** (-0.5)
                e = jnp.exp(s - jnp.max(s, axis=-1, keepdims=True))
                inv = 1.0 / jnp.sum(e, axis=-1, keepdims=True)
                outs.append(dot((e * inv).astype(BF16), v))
            att[pl.ds(at, length), lo:hi] = jnp.where(low_half, outs[0], outs[1]).astype(BF16)
        return carry

    for i in range(lat.shape[0]):
        one(i, 0)


def spread(tmp, at_row, dm, pieces, rows, f, slot=None):
    keep_odd, keep_even, send_odd, send_even = pieces
    keep = (keep_even, keep_odd)[dm % 2]
    swapped = (0, 2, 1, 3)[dm]
    send = (send_even, send_odd)[swapped % 2]
    for place, zm in enumerate(LEVELS):
        for ref, at, owner in (
            (keep, dm // 2, flip(f, 2 * zm)),
            (send, swapped // 2, flip(f, 2 * zm + 1)),
        ):
            piece = tmp[pl.ds(pl.multiple_of(at_row(owner), 16), rows), :]
            if slot is None:
                ref[at, place] = piece
            else:
                ref[at, place, slot] = piece


def mlp_body(
    ids, *refs,
):
    mlp_steps(ids, refs[:8], *refs[8:])


def mlp_steps(
    ids, pieces, m_up, m_down, o_up, o_down, wout, mod, lat, cot, att,
    res, gmid, gbr, gatt, gsum, gmod, k_odd, k_even, s_odd, s_even,
    wu, wd, n2s, acts, dgs, gmlps, gpres, n2t, tmp, tmpd, brs, xhats, rstds, mlps,
):
    d, f, mine, theirs = offsets(ids)
    count = ids[2]
    rows, feat = m_up.shape[0], m_down.shape[1]
    hidden = wd.shape[0]
    blocks = hidden // feat
    step = 512
    whole = ((m_up, m_down), (o_up, o_down))
    split = (pieces[:4], mine, f), (pieces[4:], theirs, flip(f, 1))
    for (u_ref, d_ref), (found, flips, base) in zip(whole, split):
        at = pl.multiple_of(base * rows, 16)
        wu[pl.ds(at, rows), :] = u_ref[...]
        wd[pl.ds(pl.multiple_of(base * 4 * rows, 16), 4 * rows), :] = d_ref[...]
        for n, how in enumerate(flips):
            block = flip(d, how)
            for place, zm in enumerate(LEVELS[1:]):
                get = found[n].at[place]
                owner = flip(base, 2 * zm)
                wu[
                    pl.ds(pl.multiple_of(owner * rows, 16), rows),
                    pl.ds(pl.multiple_of(block * feat, 128), feat),
                ] = get[rows : 2 * rows, :]
                at = pl.multiple_of((owner * 4 + block) * rows, 16)
                wd[pl.ds(at, rows), :] = get[2 * rows : 3 * rows, :]
    length = lat.shape[1]
    bup = mod[2:3, : 4 * feat]
    bout = mod[3:4, :feat]
    bdown = mod[3:4, feat : 2 * feat]
    members = lat.shape[0]

    def rows_of(i):
        row = mod[i : i + 1, :]
        return (row[:, j * feat : (j + 1) * feat] for j in (2, 3, 4, 5))

    brs[...] = dot(att[...], wout[0]) + bout
    for i in range(members):
        part = slice(i * length, (i + 1) * length)
        gate_one, shift, scale, _ = rows_of(i)
        middle = lat[i].astype(F32) + gate_one * brs[part, :]
        xhat, rstd = norm_parts(middle)
        gmid[i] = middle
        xhats[part, :] = xhat
        rstds[part, :] = jnp.broadcast_to(rstd, (length, 128))
        n2s[part, :] = (xhat * (1.0 + scale) + shift).astype(BF16)
    mlp = None
    for j in range(0, hidden, step):
        cols = slice(j, j + step)
        v = dot(n2s[...], wu[:, cols]) + bup[:, cols]
        square = v * v
        half = 0.5 + 0.5 * jnp.tanh(v * (0.7978845608028654 + 0.035677408136300125 * square))
        act = (v * half).astype(BF16)
        slope = v * (1.5957691216057308 + 0.21406444881780075 * square)
        dgs[:, cols] = half * (1.0 + (1.0 - half) * slope)
        acts[:, cols] = act
        term = dot(act, wd[cols, :])
        mlp = term if mlp is None else mlp + term
    mlps[...] = mlp + bdown
    g_gate_two = []
    for i in range(members):
        part = slice(i * length, (i + 1) * length)
        gate_two = list(rows_of(i))[3]
        alive = jnp.where(i < count, 1.0, 0.0).astype(F32)
        mlp = mlps[part, :]
        res[i] = (alive * (gmid[i] + gate_two * mlp)).astype(BF16)
        upstream = alive * cot[i].astype(F32)
        g_gate_two.append(jnp.sum(upstream * mlp, axis=0, keepdims=True))
        gmlps[part, :] = (gate_two * upstream).astype(BF16)
    gn = None
    for j in range(0, hidden, step):
        cols = slice(j, j + step)
        gpre = (dot(gmlps[...], wd[cols, :], NT) * dgs[:, cols]).astype(BF16)
        gpres[:, cols] = gpre
        term = dot(gpre, wu[:, cols], NT)
        gn = term if gn is None else gn + term
        gsum[:, feat + j : feat + j + step] = jnp.sum(gpre.astype(F32), axis=0, keepdims=True)
    mlps[...] = gn
    for i in range(members):
        part = slice(i * length, (i + 1) * length)
        gate_one, _, scale, _ = rows_of(i)
        alive = jnp.where(i < count, 1.0, 0.0).astype(F32)
        gn, xhat = mlps[part, :], xhats[part, :]
        g_shift = jnp.sum(gn, axis=0, keepdims=True)
        g_scale = jnp.sum(gn * xhat, axis=0, keepdims=True)
        gx = gn * (1.0 + scale)
        gmiddle = alive * cot[i].astype(F32) + rstds[part, 0:1] * (
            gx
            - jnp.mean(gx, axis=-1, keepdims=True)
            - xhat * jnp.mean(gx * xhat, axis=-1, keepdims=True)
        )
        gmid[i] = gmiddle
        g_gate_one = jnp.sum(gmiddle * brs[part, :], axis=0, keepdims=True)
        gbr[part, :] = (gate_one * gmiddle).astype(BF16)
        gmod[i : i + 1, :] = jnp.concatenate([g_gate_one, g_shift, g_scale, g_gate_two[i]], axis=1)
    gatt[...] = dot(gbr[...], wout[0], NT).astype(BF16)
    gsum[:, 0:feat] = jnp.sum(gbr[...].astype(F32), axis=0, keepdims=True)
    gsum[:, 5 * feat : 6 * feat] = jnp.sum(gmlps[...].astype(F32), axis=0, keepdims=True)
    pieces = (k_odd, k_even, s_odd, s_even)
    n2t[...] = n2s[...].T
    for j in range(0, hidden, step):
        cols = slice(j, j + step)
        tmpd[cols, :] = dot(acts[:, cols], gmlps[...], TN).astype(BF16)
        tmp[:, cols] = dot(n2t[...], gpres[:, cols]).astype(BF16)
    for dm in range(4):
        block = flip(d, mine[dm])
        spread(tmpd, lambda o: (o * 4 + block) * rows, dm, pieces, rows, f, 1)
        cut = pl.ds(pl.multiple_of(block * feat, 128), feat)
        spread(tmp.at[:, cut], lambda o: o * rows, dm, pieces, rows, f, 0)


def attend_back_one(proj, gatt, gall, i, length):
    feat = gatt.shape[1]
    low_half = lane_masks(length)

    def one(i, carry):
        part = slice(i * length, (i + 1) * length)
        for pair in range(HEADS // 2):
            lo = pair * 2 * HEAD_DIM
            hi = lo + 2 * HEAD_DIM
            q = proj[part, lo:hi]
            k = proj[part, feat + lo : feat + hi]
            v = proj[part, 2 * feat + lo : 2 * feat + hi]
            ga = gatt[part, lo:hi]
            zero = jnp.zeros_like(q)
            gq = jnp.zeros(q.shape, F32)
            gk = jnp.zeros(q.shape, F32)
            gv = jnp.zeros(q.shape, F32)
            for side in range(2):
                own = lambda a: (
                    jnp.where(low_half, a, zero) if side == 0 else jnp.where(low_half, zero, a)
                )
                q_one, ga_one = own(q), own(ga)
                s = dot(k, q_one, NT) * HEAD_DIM ** (-0.5)
                e = jnp.exp(s - jnp.max(s, axis=0, keepdims=True))
                prob = e * (1.0 / jnp.sum(e, axis=0, keepdims=True))
                gv = gv + dot(prob.astype(BF16), ga_one)
                gp = dot(v, ga_one, NT)
                delta = jnp.sum(gp * prob, axis=0, keepdims=True)
                gs = (prob * (gp - delta)).astype(BF16)
                gk = gk + dot(gs, q_one)
                gq = gq + dot(gs, own(k), TN)
            gall[part, lo:hi] = (gq * HEAD_DIM ** (-0.5)).astype(BF16)
            gall[part, feat + lo : feat + hi] = (gk * HEAD_DIM ** (-0.5)).astype(BF16)
            gall[part, 2 * feat + lo : 2 * feat + hi] = gv.astype(BF16)
        return carry

    one(i, 0)


def attend_back_first_body(proj, gatt, gproj, *, length):
    attend_back_one(proj, gatt, gproj, 0, length)


def attend_back_body(
    ids, proj, gatt, att, gbr, n1, gsum, g_first, gproj, bias, k_odd, k_even, s_odd, s_even,
    gall, xts, tmp, *, length,
):
    d, f, mine, _ = offsets(ids)
    feat = att.shape[1]
    rows = k_odd.shape[2]
    gall[0:length, : 3 * feat] = g_first[...]
    for i in range(1, proj.shape[0] // length):
        attend_back_one(proj, gatt, gall, i, length)
    gproj[...] = gall[:, : 3 * feat]
    gall[:, 3 * feat :] = gbr[...]
    xts[0] = n1[...].T
    xts[1] = att[...].T
    pieces = (k_odd, k_even, s_odd, s_even)
    for dm in (1, 3, 0, 2):
        block = flip(d, mine[dm])
        tmp[...] = dot(
            xts[jnp.where(block == 3, 1, 0)],
            gall[:, pl.ds(pl.multiple_of(block * feat, 128), feat)],
        ).astype(BF16)
        spread(tmp, lambda o: o * rows, dm, pieces, rows, f)
    bias[:, 0:feat] = jnp.sum(gall[:, 0:feat].astype(F32), axis=0, keepdims=True)
    bias[:, feat : 2 * feat] = jnp.sum(
        gall[:, 2 * feat : 3 * feat].astype(F32), axis=0, keepdims=True
    )
    bias[:, 2 * feat :] = gsum[...]


def input_back_body(ids, gproj, wpo, lat, gmid, mod, gmod, bias, lgrad, gm, full):
    length = lat.shape[1]
    feat = lat.shape[2]

    def one(i, carry):
        part = pl.ds(i * length, length)
        row = mod[pl.ds(i, 1), :]
        xhat, rstd = norm_parts(lat[i].astype(F32))
        gn = dot(gproj[part, 0:feat], wpo[0], NT)
        gn = gn + dot(gproj[part, feat : 2 * feat], wpo[1], NT)
        gn = gn + dot(gproj[part, 2 * feat :], wpo[2], NT)
        g_shift = jnp.sum(gn, axis=0, keepdims=True)
        g_scale = jnp.sum(gn * xhat, axis=0, keepdims=True)
        gx = gn * (1.0 + row[:, feat : 2 * feat])
        lgrad[i] = (
            gmid[i]
            + rstd
            * (
                gx
                - jnp.mean(gx, axis=-1, keepdims=True)
                - xhat * jnp.mean(gx * xhat, axis=-1, keepdims=True)
            )
        ).astype(BF16)
        full[pl.ds(i, 1), : 6 * feat] = jnp.concatenate(
            [g_shift, g_scale, gmod[pl.ds(i, 1), :]], axis=1
        )
        return carry

    for i in range(lat.shape[0]):
        one(i, 0)
    full[0:1, 6 * feat :] = bias[:, : 4 * feat]
    full[1:2, 6 * feat :] = bias[:, 4 * feat :]
    gm[...] = full[...].astype(BF16)


def cond_back_body(ids, g0, g2, g1, g3, wmod, lo, hi):
    f = ids[1]
    rows, wide = wmod.shape
    many = g0.shape[0]
    place = one_hot((rows, lo.shape[2]), f * rows)
    grads = jnp.concatenate([ref[:, :wide] for ref in (g0, g2, g1, g3)], axis=0)
    whole = dot(dot(grads, wmod[...], NT).astype(BF16), place).astype(BF16)
    for n, (out, at) in enumerate(((lo, 0), (lo, 1), (hi, 0), (hi, 1))):
        out[at] = jnp.zeros(out.shape[1:], BF16)
        out[at, 0:many, :] = whole[many * n : many * (n + 1)]


def mod_weight_body(ids, e0, e1, e2, e3, wgrad, b_mod, b_qv, b_out, b_up, b_down):
    f = ids[1]
    rows, wide = wgrad.shape
    feat = wide // 6
    grad_wide = e0.shape[1] - feat
    select = one_hot((rows, feat), f * rows)
    total = None
    sums = None
    for ref in (e0, e1, e2, e3):
        own = dot(select, ref[:, grad_wide:], NT).astype(BF16)
        term = dot(own, ref[:, :wide])
        total = term if total is None else total + term
        low = ref[:, :grad_wide].astype(F32)
        sums = low if sums is None else sums + low
    wgrad[...] = total
    low = sums[:, wide:]
    odd = lax.broadcasted_iota(jnp.int32, low.shape, 0) % 2 == 1
    even_sum = jnp.sum(jnp.where(odd, 0.0, low), axis=0, keepdims=True)
    odd_sum = jnp.sum(jnp.where(odd, low, 0.0), axis=0, keepdims=True)
    whole = jnp.concatenate([jnp.sum(sums[:, :wide], axis=0, keepdims=True), even_sum, odd_sum], axis=1)
    at = 0
    for out in (b_mod, b_qv, b_out, b_up, b_down):
        size = out.shape[0]
        vector = jnp.broadcast_to(whole[:, at : at + 8 * size], (8, 8 * size))
        out[...] = pltpu.roll(vector, lax.rem(8 - f, 8) * size, 1)[0, :size]
        at += 8 * size


def sum_body(keep, got, out):
    out[...] = add_low(keep[...], got[...])


def turn_body(keep_ud, in_ud, keep_po, in_po, got_ud, got_po, out, *, at):
    rows = keep_po.shape[2]
    for place in range(out.shape[0]):
        out[place, 0:rows] = add_low(keep_po[at, place], in_po[at, place], got_po[at, place])
        for slot in range(2):
            out[place, (1 + slot) * rows : (2 + slot) * rows] = add_low(
                keep_ud[at, place, slot], in_ud[at, place, slot], got_ud[at, place, slot]
            )


def stack_body(q2, q1, q3, out):
    for n, ref in enumerate((q2, q1, q3)):
        out[n] = ref[0 : out.shape[1], :]


def pair_body(own, other, out):
    out[0 : own.shape[0], :] = own[...]
    out[own.shape[0] :, :] = other[...]


def pack_body(g0, g2, g1, g3, c_own, c_other, out):
    many, wide = g0.shape
    half = many // 2
    for n, ref in enumerate((g0, g2, g1, g3)):
        out[many * n : many * (n + 1), 0:wide] = ref[...]
        out[many * n : many * n + half, wide:] = c_own[half * n : half * (n + 1), :]
        out[many * n + half : many * (n + 1), wide:] = c_other[half * n : half * (n + 1), :]


def join_far_body(base, part, back, out):
    size = base.shape[1]
    out[:, 0:size] = add_low(base[2:], part[2:])
    out[:, size:] = back[...]


def join_near_body(base, part, back, got, out, far):
    size = base.shape[1]
    for at, ref in enumerate((out, far)):
        ref[0:size, :] = add_low(base[at], part[at], got[at, 0:size])
        ref[size:, :] = add_low(back[at], got[at, size:])


def total_body(base, got, out, back):
    size = out.shape[0]
    out[...] = add_low(base[0:size, :], got[0:size, :])
    back[...] = base[size:, :].astype(F32) + got[size:, :].astype(F32)


def final_body(ids, g0, g1, g2, g3, gp, go, gu, gd):
    d, _, mine, _ = offsets(ids)
    rows, feat = go.shape
    for ref, how in zip((g0, g1, g2, g3), mine):
        block = flip(d, how)

        @pl.when(block < 3)
        def _():
            at = pl.multiple_of(lax.min(block, 2) * feat, 128)
            gp[:, pl.ds(at, feat)] = ref[0:rows, :].astype(F32)

        @pl.when(block == 3)
        def _():
            go[...] = ref[0:rows, :].astype(F32)

        gu[:, pl.ds(pl.multiple_of(block * feat, 128), feat)] = ref[rows : 2 * rows, :].astype(F32)
        gd[pl.ds(pl.multiple_of(block * rows, 16), rows), :] = ref[2 * rows : 3 * rows, :].astype(F32)


def routes():
    core, first, second, across = [], [], [], []
    levels = {1: [], 2: []}
    for d in range(4):
        for f in range(8):
            i = d * 8 + f
            core.append((i, i ^ 1))
            a = 1 if f % 2 == 0 else 2
            first.append((i, (d ^ a) * 8 + f))
            second.append((i, (d ^ (3 - a)) * 8 + f))
            across.append((i, (d ^ 3) * 8 + f))
            for m in levels:
                levels[m].append((i, d * 8 + (f ^ (2 * m))))
    return core, first, second, across, levels


def add_low(*parts):
    total = parts[0].astype(F32)
    for part in parts[1:]:
        total = total + part.astype(F32)
    return total.astype(BF16)


def on_device_blocks(
    latents, cond, counts, cotangent, modulation_weight, modulation_bias, projection_weight,
    query_value_bias, output_weight, output_bias, up_weight, up_bias, down_weight, down_bias,
):
    core, first, second, across, levels = routes()

    def move(x, route):
        return lax.ppermute(x, BOTH, route)

    slots, length, feat = latents.shape
    rows = projection_weight.shape[0]
    hidden = up_weight.shape[1]
    wide = modulation_weight.shape[1]
    tokens = slots * length
    d = lax.axis_index("dp")
    f = lax.axis_index("fsdp")
    ids = jnp.stack([d, f, counts[0]]).astype(jnp.int32)

    def after(x, *earlier):
        return lax.optimization_barrier((x,) + earlier)[0]

    (q_all,) = call(
        pick_body, "pick", None,
        [projection_weight, output_weight, up_weight, down_weight, cond],
        [((3 * rows + 16, feat), BF16)],
        [pltpu.VMEM((slots, feat), BF16), pltpu.SemaphoreType.DMA((4,))],
        far=(0, 1, 2, 3, 4), limit=60,
    )

    def over_dp(own):
        a = move(own, first)
        b = move(own, second)
        return [own, a, b, move(a, second)]

    whole = [projection_weight, output_weight, up_weight, down_weight]
    w_whole = whole + [move(after(x, q_all), core) for x in whole]
    wmod_other = move(after(modulation_weight, q_all), core)
    biases = [modulation_bias, query_value_bias, output_bias, up_bias, down_bias]
    wmod, placed = call(
        prepare_body, "prepare", None, [modulation_weight, wmod_other] + biases,
        [((2 * rows, wide), BF16), ((3, wide), F32)],
    )
    q_far = move(q_all, levels[2])
    placed_other = move(placed, core)
    ready = (placed_other, *w_whole[4:])
    q_far = after(q_far, *ready)
    q_near, q_both = move(after(q_all, wmod_other), levels[1]), move(q_far, levels[1])
    (own,) = call(stack_body, "stack", None, [q_far, q_near, q_both], [((3, 3 * rows, feat), BF16)])
    keep_lo, keep_hi, c_own = call(
        mod_body, "modulation", ids, [q_all, q_far, q_near, q_both, wmod, placed, placed_other],
        [((2, 4, wide), F32)] * 2 + [((4 * slots, feat), BF16)],
    )
    a_own, b_own = move(own, first), move(own, second)
    paid_lo = keep_lo + move(keep_hi, levels[1])
    a_own = after(a_own, paid_lo)
    paid_far = move(after(paid_lo[1], a_own), levels[2])
    ab_own = move(a_own, second)
    w_all = [own, a_own, b_own, ab_own]
    w_all = w_all + [move(x, core) for x in w_all[:3]] + [move(after(ab_own, paid_far), core)]

    wpo, mod, n1, proj, att = call(
        attend_body, "attention", ids,
        w_all + [w_whole[k] for k in (0, 1, 4, 5)] + [paid_lo, paid_far, latents],
        [((4, feat, feat), BF16), ((4, wide), F32), ((tokens, feat), BF16),
         ((tokens, 3 * feat), BF16), ((tokens, feat), BF16)],
        flops=2 * tokens * feat * (3 * feat + 4 * length),
    )
    wout = wpo[3:4]
    ud_shape = ((2, 4, 2, rows, feat), BF16)
    po_shape = ((2, 4, rows, feat), BF16)
    res, gmid, gbr, gatt, gsum, gmod, ud_odd, ud_even, ud_odd_out, ud_even_out = call(
        mlp_body, "mlp", ids,
        w_all + [w_whole[k] for k in (2, 3, 6, 7)] + [wout, mod, latents, cotangent, att],
        [((slots, length, feat), BF16), ((slots, length, feat), F32), ((tokens, feat), BF16),
         ((tokens, feat), BF16), ((1, 6 * feat), F32), ((slots, 4 * feat), F32)] + [ud_shape] * 4,
        [
            pltpu.VMEM((feat, hidden), BF16), pltpu.VMEM((hidden, feat), BF16),
            pltpu.VMEM((tokens, feat), BF16), pltpu.VMEM((tokens, hidden), BF16),
            pltpu.VMEM((tokens, hidden), F32), pltpu.VMEM((tokens, feat), BF16),
            pltpu.VMEM((tokens, hidden), BF16), pltpu.VMEM((feat, tokens), BF16),
            pltpu.VMEM((feat, hidden), BF16), pltpu.VMEM((hidden, feat), BF16),
            pltpu.VMEM((tokens, feat), F32), pltpu.VMEM((tokens, feat), F32),
            pltpu.VMEM((tokens, 128), F32), pltpu.VMEM((tokens, feat), F32),
        ],
        flops=2 * tokens * feat * (6 * hidden + 2 * feat),
    )
    ud_odd_in = move(ud_odd_out, core)
    ud_even_in = move(ud_even_out, core)
    (g_first,) = call(
        functools.partial(attend_back_first_body, length=length), "attention_back_first", None,
        [proj, gatt], [((length, 3 * feat), BF16)], flops=tokens * feat * 10 * length,
    )
    (odd_ud,) = call(sum_body, "sum_ud", None, [ud_odd, after(ud_odd_in, g_first)], [ud_shape])
    got_ud = move(odd_ud, first)
    gproj, bias, po_odd, po_even, po_odd_out, po_even_out = call(
        functools.partial(attend_back_body, length=length), "attention_back", ids,
        [proj, gatt, att, gbr, n1, gsum, after(g_first, odd_ud)],
        [((tokens, 3 * feat), BF16), ((1, 8 * feat), F32)] + [po_shape] * 4,
        [pltpu.VMEM((tokens, 4 * feat), BF16), pltpu.VMEM((2, feat, tokens), BF16),
         pltpu.VMEM((feat, feat), BF16)],
        flops=2 * tokens * feat * (4 * feat + 5 * length),
    )
    po_odd_in = move(po_odd_out, core)
    po_even_in = move(po_even_out, core)
    lgrad, gm = call(
        input_back_body, "input_back", ids,
        [gproj, wpo, latents, gmid, mod, gmod, bias],
        [((slots, length, feat), BF16), ((slots, 10 * feat), BF16)],
        [pltpu.VMEM((slots, 10 * feat), F32)],
        flops=2 * tokens * feat * 3 * feat,
    )
    (odd_po,) = call(sum_body, "sum_po", None, [po_odd, after(po_odd_in, gm, got_ud)], [po_shape])
    got_po = move(odd_po, first)
    c_other = move(c_own, core)

    (gm_pair,) = call(pair_body, "pair", None, [after(gm, c_other), move(gm, core)], [((2 * slots, 10 * feat), BF16)])
    gm_far = move(gm_pair, levels[2])

    halves = [ud_even, ud_even_in, po_even, po_even_in, got_ud, after(got_po, gm_far)]
    half_shape = ((4, 3 * rows, feat), BF16)
    (turned,) = call(functools.partial(turn_body, at=1), "turn", None, halves, [half_shape])
    part = move(turned, second)
    (base,) = call(
        functools.partial(turn_body, at=0), "base", None, halves[:5] + [after(got_po, turned)], [half_shape]
    )

    gm_all = [gm_pair, gm_far, move(gm_pair, levels[1]), move(gm_far, levels[1])]
    (every,) = call(
        pack_body, "pack", None, gm_all + [c_own, c_other], [((8 * slots, 11 * feat), BF16)]
    )
    back_lo, back_hi = call(
        cond_back_body, "cond_back", ids, gm_all + [modulation_weight], [((2, 16, feat), BF16)] * 2
    )

    pair_shape = ((2, 3 * rows + 16, feat), BF16)
    (turned,) = call(join_far_body, "join_far", None, [base, part, back_hi], [pair_shape])
    got = move(turned, levels[1])
    every = after(every, turned)
    e_first, e_second, e_both = move(every, first), move(every, second), move(every, across)
    base, far = call(
        join_near_body, "join_near", None, [base, part, back_lo, got], [((3 * rows + 16, feat), BF16)] * 2
    )
    g_mod_weight, *g_biases = call(
        mod_weight_body, "mod_weight", ids, [every, e_first, e_second, e_both],
        [((rows, wide), F32)] + [((size // 8,), F32) for size in (wide, 2 * feat, feat, hidden, feat)],
    )
    total, back = call(
        total_body, "total", None, [base, after(move(far, levels[2]), g_mod_weight)],
        [((3 * rows, feat), BF16), ((16, feat), F32)],
    )
    a_total, b_total = move(total, first), move(total, second)
    shares = [total, a_total, b_total, move(total, across)]
    grad_silu = back[:slots] + move(back[slots : 2 * slots], core)
    cond_full = cond.astype(F32)
    sig = 1.0 / (1.0 + jnp.exp(-cond_full))
    cond_grad = (grad_silu * (sig * (1.0 + cond_full * (1.0 - sig)))).astype(BF16)
    g_proj, g_out, g_up, g_down = call(
        final_body, "final", ids, shares,
        [((rows, 3 * feat), F32), ((rows, feat), F32), ((rows, hidden), F32),
         ((4 * rows, feat), F32)],
    )
    return (
        res, lgrad, cond_grad, g_mod_weight, g_biases[0], g_proj, g_biases[1],
        g_out, g_biases[2], g_up, g_biases[3], g_down, g_biases[4],
    )


def layer_norm(vector):
    row_mean = jnp.mean(vector, axis=-1, keepdims=True)
    centered = vector - row_mean
    variance = jnp.mean(centered * centered, axis=-1, keepdims=True)
    return centered * lax.rsqrt(variance + 1e-06)


def modulate(vector, offset, stretch):
    return layer_norm(vector) * (1.0 + stretch[:, None, :]) + offset[:, None, :]


def forward_pass(gathered, inputs, conditions):
    (
        modulation_weight,
        modulation_bias,
        projection_weight,
        query_value_bias,
        output_weight,
        output_bias,
        up_weight,
        up_bias,
        down_weight,
        down_bias,
    ) = gathered
    members, length, features = inputs.shape
    flat_rows = members * length
    cond_low = jax.nn.silu(conditions).astype(jnp.bfloat16)
    modulation = jnp.dot(cond_low, modulation_weight, preferred_element_type=jnp.float32)
    modulation = modulation + modulation_bias.astype(jnp.float32)
    pieces = jnp.split(modulation, 6, axis=-1)
    normed_one = (
        modulate(inputs, pieces[0], pieces[1]).astype(jnp.bfloat16).reshape(flat_rows, features)
    )
    bias_full = query_value_bias.astype(jnp.float32)
    joined_bias = jnp.concatenate(
        [bias_full[:features], jnp.zeros((features,), jnp.float32), bias_full[features:]]
    )
    projected = (
        jnp.dot(normed_one, projection_weight, preferred_element_type=jnp.float32) + joined_bias
    )
    projected = projected.astype(jnp.bfloat16).reshape(members, length, 3, HEADS, HEAD_DIM)
    queries = projected[:, :, 0]
    key_rows = projected[:, :, 1]
    values = projected[:, :, 2]
    scores = jnp.einsum(
        "bqhd,bkhd->bhqk", queries, key_rows, preferred_element_type=jnp.float32
    ) * HEAD_DIM ** (-0.5)
    row_max = jnp.max(scores, axis=-1, keepdims=True)
    exponent = jnp.exp(scores - row_max)
    row_total = jnp.sum(exponent, axis=-1, keepdims=True)
    probability = exponent / row_total
    log_total = row_max + jnp.log(row_total)
    attended = jnp.einsum(
        "bhqk,bkhd->bqhd",
        probability.astype(jnp.bfloat16),
        values,
        preferred_element_type=jnp.float32,
    )
    attended = attended.astype(jnp.bfloat16).reshape(flat_rows, features)
    branch = jnp.dot(
        attended, output_weight, preferred_element_type=jnp.float32
    ) + output_bias.astype(jnp.float32)
    branch = branch.reshape(members, length, features)
    middle = inputs + pieces[2][:, None, :] * branch
    normed_two = (
        modulate(middle, pieces[3], pieces[4]).astype(jnp.bfloat16).reshape(flat_rows, features)
    )
    pre_act = jnp.dot(normed_two, up_weight, preferred_element_type=jnp.float32) + up_bias.astype(
        jnp.float32
    )
    activated = jax.nn.gelu(pre_act, approximate=True).astype(jnp.bfloat16)
    mlp_out = jnp.dot(
        activated, down_weight, preferred_element_type=jnp.float32
    ) + down_bias.astype(jnp.float32)
    mlp_out = mlp_out.reshape(members, length, features)
    output = middle + pieces[5][:, None, :] * mlp_out
    return (
        output,
        cond_low,
        pieces,
        normed_one,
        queries,
        key_rows,
        values,
        log_total,
        attended,
        branch,
        middle,
        normed_two,
        pre_act,
        activated,
        mlp_out,
    )


def backward_pass(gathered, saved, inputs, conditions, upstream):
    (
        modulation_weight,
        modulation_bias,
        projection_weight,
        query_value_bias,
        output_weight,
        output_bias,
        up_weight,
        up_bias,
        down_weight,
        down_bias,
    ) = gathered
    (
        output,
        cond_low,
        pieces,
        normed_one,
        queries,
        key_rows,
        values,
        log_total,
        attended,
        branch,
        middle,
        normed_two,
        pre_act,
        activated,
        mlp_out,
    ) = saved
    members, length, features = inputs.shape
    flat_rows = members * length
    grad_gate_two = jnp.sum(upstream * mlp_out, axis=1)
    grad_mlp = (pieces[5][:, None, :] * upstream).astype(jnp.bfloat16).reshape(flat_rows, features)
    grad_down = jnp.einsum("nf,nd->fd", activated, grad_mlp, preferred_element_type=jnp.float32)
    grad_down_b = jnp.sum(grad_mlp.astype(jnp.float32), axis=0)
    grad_activated = jnp.einsum(
        "nd,fd->nf", grad_mlp, down_weight, preferred_element_type=jnp.float32
    )
    gelu_out, gelu_pull = jax.vjp(lambda vector: jax.nn.gelu(vector, approximate=True), pre_act)
    grad_pre = gelu_pull(grad_activated)[0].astype(jnp.bfloat16)
    grad_up = jnp.einsum("nd,nf->df", normed_two, grad_pre, preferred_element_type=jnp.float32)
    grad_up_b = jnp.sum(grad_pre.astype(jnp.float32), axis=0)
    grad_normed_two = jnp.einsum(
        "nf,df->nd", grad_pre, up_weight, preferred_element_type=jnp.float32
    )
    second_out, second_pull = jax.vjp(modulate, middle, pieces[3], pieces[4])
    grad_middle, grad_shift_two, grad_scale_two = second_pull(
        grad_normed_two.reshape(members, length, features)
    )
    grad_middle = grad_middle + upstream
    grad_gate_one = jnp.sum(grad_middle * branch, axis=1)
    grad_branch = (
        (pieces[2][:, None, :] * grad_middle).astype(jnp.bfloat16).reshape(flat_rows, features)
    )
    grad_output = jnp.einsum("nd,ne->de", attended, grad_branch, preferred_element_type=jnp.float32)
    grad_output_b = jnp.sum(grad_branch.astype(jnp.float32), axis=0)
    grad_attended = jnp.einsum(
        "ne,de->nd", grad_branch, output_weight, preferred_element_type=jnp.float32
    )
    grad_attended = grad_attended.astype(jnp.bfloat16).reshape(members, length, HEADS, HEAD_DIM)
    scale_factor = HEAD_DIM ** (-0.5)
    scores = (
        jnp.einsum("bqhd,bkhd->bhqk", queries, key_rows, preferred_element_type=jnp.float32)
        * scale_factor
    )
    probability = jnp.exp(scores - log_total)
    grad_values = jnp.einsum(
        "bhqk,bqhd->bkhd",
        probability.astype(jnp.bfloat16),
        grad_attended,
        preferred_element_type=jnp.float32,
    )
    grad_prob = jnp.einsum(
        "bqhd,bkhd->bhqk", grad_attended, values, preferred_element_type=jnp.float32
    )
    row_delta = jnp.sum(grad_prob * probability, axis=-1, keepdims=True)
    grad_scores = (probability * (grad_prob - row_delta)).astype(jnp.bfloat16)
    grad_queries = (
        jnp.einsum("bhqk,bkhd->bqhd", grad_scores, key_rows, preferred_element_type=jnp.float32)
        * scale_factor
    )
    grad_keys = (
        jnp.einsum("bhqk,bqhd->bkhd", grad_scores, queries, preferred_element_type=jnp.float32)
        * scale_factor
    )
    grad_projected = jnp.stack([grad_queries, grad_keys, grad_values], axis=2)
    grad_projected = grad_projected.astype(jnp.bfloat16).reshape(flat_rows, 3 * features)
    grad_projection = jnp.einsum(
        "nd,ne->de", normed_one, grad_projected, preferred_element_type=jnp.float32
    )
    column_sums = jnp.sum(grad_projected.astype(jnp.float32), axis=0)
    grad_query_value = jnp.concatenate([column_sums[:features], column_sums[2 * features :]])
    grad_normed_one = jnp.einsum(
        "ne,de->nd", grad_projected, projection_weight, preferred_element_type=jnp.float32
    )
    first_out, first_pull = jax.vjp(modulate, inputs, pieces[0], pieces[1])
    grad_input, grad_shift_one, grad_scale_one = first_pull(
        grad_normed_one.reshape(members, length, features)
    )
    grad_input = grad_input + grad_middle
    grad_modulation = jnp.concatenate(
        [
            grad_shift_one,
            grad_scale_one,
            grad_gate_one,
            grad_shift_two,
            grad_scale_two,
            grad_gate_two,
        ],
        axis=-1,
    ).astype(jnp.bfloat16)
    grad_mod_weight = jnp.einsum(
        "bc,be->ce", cond_low, grad_modulation, preferred_element_type=jnp.float32
    )
    grad_mod_bias = jnp.sum(grad_modulation.astype(jnp.float32), axis=0)
    grad_silu = jnp.einsum(
        "be,ce->bc", grad_modulation, modulation_weight, preferred_element_type=jnp.float32
    )
    silu_out, silu_pull = jax.vjp(jax.nn.silu, conditions)
    grad_conditions = silu_pull(grad_silu)[0]
    weight_grads = (
        grad_mod_weight,
        grad_mod_bias,
        grad_projection,
        grad_query_value,
        grad_output,
        grad_output_b,
        grad_up,
        grad_up_b,
        grad_down,
        grad_down_b,
    )
    return (weight_grads, grad_input, grad_conditions)


def on_device(
    latents,
    cond,
    counts,
    cotangent,
    modulation_weight,
    modulation_bias,
    projection_weight,
    query_value_bias,
    output_weight,
    output_bias,
    up_weight,
    up_bias,
    down_weight,
    down_bias,
):
    lat_slots = latents.shape[0]
    per_micro = lat_slots // MICRO
    alive_all = (jnp.arange(lat_slots) < counts[0]).astype(jnp.float32)
    kept = (
        lax.all_gather(modulation_weight, "fsdp", axis=0, tiled=True),
        lax.all_gather(modulation_bias, "fsdp", axis=0, tiled=True),
        lax.all_gather(projection_weight, "fsdp", axis=0, tiled=True),
        lax.all_gather(query_value_bias, "fsdp", axis=0, tiled=True),
        lax.all_gather(output_weight, "fsdp", axis=0, tiled=True),
        lax.all_gather(output_bias, "fsdp", axis=0, tiled=True),
        lax.all_gather(up_weight, "fsdp", axis=0, tiled=True),
        lax.all_gather(up_bias, "fsdp", axis=0, tiled=True),
        lax.all_gather(down_weight, "fsdp", axis=0, tiled=True),
        lax.all_gather(down_bias, "fsdp", axis=0, tiled=True),
    )
    outputs = []
    input_grads = []
    cond_grads = []
    totals = None
    for micro_index in range(MICRO):
        start = micro_index * per_micro
        inputs = latents[start : start + per_micro].astype(jnp.float32)
        conditions = cond[start : start + per_micro].astype(jnp.float32)
        alive_mask = alive_all[start : start + per_micro]
        saved = forward_pass(kept, inputs, conditions)
        outputs.append((saved[0] * alive_mask[:, None, None]).astype(jnp.bfloat16))
        upstream = (
            cotangent[start : start + per_micro].astype(jnp.float32) * alive_mask[:, None, None]
        )
        weight_grads, grad_input, grad_conditions = backward_pass(
            kept, saved, inputs, conditions, upstream
        )
        input_grads.append(grad_input.astype(jnp.bfloat16))
        cond_grads.append(grad_conditions.astype(jnp.bfloat16))
        totals = (
            weight_grads
            if totals is None
            else tuple((left + right for left, right in zip(totals, weight_grads)))
        )
    totals = (
        lax.psum_scatter(totals[0], "fsdp", scatter_dimension=0, tiled=True),
        lax.psum_scatter(totals[1], "fsdp", scatter_dimension=0, tiled=True),
        lax.psum_scatter(totals[2], "fsdp", scatter_dimension=0, tiled=True),
        lax.psum_scatter(totals[3], "fsdp", scatter_dimension=0, tiled=True),
        lax.psum_scatter(totals[4], "fsdp", scatter_dimension=0, tiled=True),
        lax.psum_scatter(totals[5], "fsdp", scatter_dimension=0, tiled=True),
        lax.psum_scatter(totals[6], "fsdp", scatter_dimension=0, tiled=True),
        lax.psum_scatter(totals[7], "fsdp", scatter_dimension=0, tiled=True),
        lax.psum_scatter(totals[8], "fsdp", scatter_dimension=0, tiled=True),
        lax.psum_scatter(totals[9], "fsdp", scatter_dimension=0, tiled=True),
    )
    totals = (
        lax.psum(totals[0].astype(jnp.bfloat16), "dp").astype(jnp.float32),
        lax.psum(totals[1].astype(jnp.bfloat16), "dp").astype(jnp.float32),
        lax.psum(totals[2].astype(jnp.bfloat16), "dp").astype(jnp.float32),
        lax.psum(totals[3].astype(jnp.bfloat16), "dp").astype(jnp.float32),
        lax.psum(totals[4].astype(jnp.bfloat16), "dp").astype(jnp.float32),
        lax.psum(totals[5].astype(jnp.bfloat16), "dp").astype(jnp.float32),
        lax.psum(totals[6].astype(jnp.bfloat16), "dp").astype(jnp.float32),
        lax.psum(totals[7].astype(jnp.bfloat16), "dp").astype(jnp.float32),
        lax.psum(totals[8].astype(jnp.bfloat16), "dp").astype(jnp.float32),
        lax.psum(totals[9].astype(jnp.bfloat16), "dp").astype(jnp.float32),
    )
    return (
        jnp.concatenate(outputs, axis=0),
        jnp.concatenate(input_grads, axis=0),
        jnp.concatenate(cond_grads, axis=0),
        totals[0],
        totals[1],
        totals[2],
        totals[3],
        totals[4],
        totals[5],
        totals[6],
        totals[7],
        totals[8],
        totals[9],
    )


def solution(mesh):
    small = mesh.shape["dp"] == 4 and mesh.shape["fsdp"] == 8
    program = on_device_blocks if small else on_device
    placed = (
        P(("dp", "fsdp"), None, None),
        P(("dp", "fsdp"), None),
        P(("dp", "fsdp")),
        P(("dp", "fsdp"), None, None),
        P("fsdp", None),
        P("fsdp"),
        P("fsdp", None),
        P("fsdp"),
        P("fsdp", None),
        P("fsdp"),
        P("fsdp", None),
        P("fsdp"),
        P("fsdp", None),
        P("fsdp"),
    )
    return jax.shard_map(
        program,
        mesh=mesh,
        in_specs=placed,
        out_specs=(
            P(("dp", "fsdp"), None, None),
            P(("dp", "fsdp"), None, None),
            P(("dp", "fsdp"), None),
            P("fsdp", None),
            P("fsdp"),
            P("fsdp", None),
            P("fsdp"),
            P("fsdp", None),
            P("fsdp"),
            P("fsdp", None),
            P("fsdp"),
            P("fsdp", None),
            P("fsdp"),
        ),
        check_vma=False,
    )
```

```python
import functools

import jax
import jax.numpy as jnp
from jax import lax
from jax.experimental import pallas as pl
from jax.experimental.pallas import tpu as pltpu
from jax.sharding import PartitionSpec as P

HEADS = 6
HEAD_DIM = 64
MICRO = 2
F32 = jnp.float32
BF16 = jnp.bfloat16
BOTH = ("dp", "fsdp")
NN = (((1,), (0,)), ((), ()))
NT = (((1,), (1,)), ((), ()))
TN = (((0,), (0,)), ((), ()))
LEVELS = (0, 2, 1, 3)


def dot(left, right, dims=NN):
    return lax.dot_general(left, right, dims, preferred_element_type=F32)


def smem():
    return pl.BlockSpec(memory_space=pltpu.SMEM)


def vmem():
    return pl.BlockSpec(memory_space=pltpu.VMEM)


def hbm():
    return pl.BlockSpec(memory_space=pltpu.HBM)


def call(body, name, ids, ins, outs, scratch=(), flops=0, limit=48, far=()):
    fixed = [] if ids is None else [ids]
    return pl.pallas_call(
        body,
        out_shape=[jax.ShapeDtypeStruct(s, t) for s, t in outs],
        in_specs=[smem()] * len(fixed) + [hbm() if i in far else vmem() for i in range(len(ins))],
        out_specs=[vmem()] * len(outs),
        scratch_shapes=list(scratch),
        compiler_params=pltpu.CompilerParams(vmem_limit_bytes=limit * 1024 * 1024),
        cost_estimate=pl.CostEstimate(flops=1, bytes_accessed=1, transcendentals=0),
        name=name,
    )(*fixed, *ins)


def offsets(ids):
    d, f = ids[0], ids[1]
    core = lax.rem(f, 2)
    first = 1 + core
    second = 2 - core
    return d, f, (0, first, second, 3), (0, second, first, 3)


def flip(a, b):
    return lax.bitwise_xor(a, b)


def pick_body(proj, outw, up, down, cond, q_all, c_in, sems):
    d = lax.axis_index("dp")
    rows, width = outw.shape
    at = pl.ds(pl.multiple_of(d * width, 128), width)
    at_proj = pl.ds(pl.multiple_of(lax.min(d, 2) * width, 128), width)
    q_po = q_all.at[pl.ds(0, rows), :]
    copies = [
        pltpu.make_async_copy(cond, c_in, sems.at[0]),
        pltpu.make_async_copy(up.at[:, at], q_all.at[pl.ds(rows, rows), :], sems.at[1]),
        pltpu.make_async_copy(
            down.at[pl.ds(pl.multiple_of(d * rows, 16), rows), :],
            q_all.at[pl.ds(2 * rows, rows), :],
            sems.at[2],
        ),
    ]
    for copy in copies:
        copy.start()

    @pl.when(d < 3)
    def _():
        copy = pltpu.make_async_copy(proj.at[:, at_proj], q_po, sems.at[3])
        copy.start()
        copy.wait()

    @pl.when(d == 3)
    def _():
        copy = pltpu.make_async_copy(outw, q_po, sems.at[3])
        copy.start()
        copy.wait()

    for copy in copies:
        copy.wait()
    c = c_in[...].astype(F32)
    c = c / (1.0 + jnp.exp(-c))
    blank = jnp.zeros((16 - c.shape[0], width), F32)
    q_all[3 * rows :, :] = jnp.concatenate([c, blank], axis=0).astype(BF16)


def one_hot(shape, shift):
    r = lax.broadcasted_iota(jnp.int32, shape, 0)
    c = lax.broadcasted_iota(jnp.int32, shape, 1)
    return jnp.where(c == r + shift, 1.0, 0.0).astype(BF16)


def prepare_body(wmod_own, wmod_other, f0, f1, f2, f3, f4, wmod, placed):
    f = lax.axis_index("fsdp")
    shard = wmod_own.shape[0]
    wmod[0:shard, :] = wmod_own[...]
    wmod[shard:, :] = wmod_other[...]
    rows = []
    for ref in (f0, f1, f2, f3, f4):
        size = ref.shape[0]
        rows.append(dot(ref[...].reshape(1, size), one_hot((size, 8 * size), f * size)))
    bias, b_qv, b_out, b_up, b_down = rows
    feat = b_out.shape[1]
    placed[0:1, :] = bias
    placed[1:2, :] = jnp.concatenate([b_up, b_qv], axis=1)
    placed[2:3, :] = jnp.concatenate([b_out, b_down, jnp.zeros((1, 4 * feat), F32)], axis=1)


def mod_body(ids, q0, q2, q1, q3, wmod, placed, placed_other, keep_lo, keep_hi, c_own):
    f = ids[1]
    rows, wide = wmod.shape
    slots, feat = c_own.shape[0] // 4, c_own.shape[1]
    shard = rows // 2
    at = q0.shape[0] - 16
    r = lax.broadcasted_iota(jnp.int32, (feat, rows), 0)
    c = lax.broadcasted_iota(jnp.int32, (feat, rows), 1)
    start = jnp.where(c < shard, f * shard, flip(f, 1) * shard - shard)
    select = jnp.where(r == c + start, 1.0, 0.0).astype(BF16)
    stacked = jnp.concatenate([ref[at : at + slots, :] for ref in (q0, q2, q1, q3)], axis=0)
    c_own[...] = stacked
    bias = placed[...] + placed_other[...]
    part = dot(dot(stacked, select).astype(BF16), wmod[...]) + bias[0:1]
    for n in range(4):
        keep = (keep_lo, keep_lo, keep_hi, keep_hi)[n]
        keep[n % 2, 0:slots, :] = part[slots * n : slots * (n + 1)]
        keep[n % 2, 2:4, :] = bias[1:3]


def norm_parts(x):
    mean = jnp.mean(x, axis=-1, keepdims=True)
    centered = x - mean
    rstd = lax.rsqrt(jnp.mean(centered * centered, axis=-1, keepdims=True) + 1e-06)
    return centered * rstd, rstd


def lane_masks(rows):
    lane = lax.broadcasted_iota(jnp.int32, (rows, 2 * HEAD_DIM), 1)
    return lane < HEAD_DIM


def attend_body(
    ids, *refs,
):
    d, f, mine, theirs = offsets(ids)
    pieces, (m_proj, m_out, o_proj, o_out, p0, p1, lat, wpo, mod, n1, proj, att) = refs[:8], refs[8:]
    rows, feat = m_out.shape
    whole = ((m_proj, m_out), (o_proj, o_out))
    split = (pieces[:4], mine, f), (pieces[4:], theirs, flip(f, 1))
    for (p_ref, o_ref), (found, flips, base) in zip(whole, split):
        at = pl.multiple_of(base * rows, 16)
        for block in range(3):
            wpo[block, pl.ds(at, rows), :] = p_ref[:, block * feat : (block + 1) * feat]
        wpo[3, pl.ds(at, rows), :] = o_ref[...]
        for n, how in enumerate(flips):
            block = flip(d, how)
            for place, zm in enumerate(LEVELS[1:]):
                get = found[n].at[place]
                at = pl.multiple_of(flip(base, 2 * zm) * rows, 16)
                wpo[block, pl.ds(at, rows), :] = get[0:rows, :]
    mod[...] = p0[0] + p1[...]
    length = lat.shape[1]
    low_half = lane_masks(length)
    qv = mod[2:3, 4 * feat :]

    for i in range(lat.shape[0]):
        xhat, rstd = norm_parts(lat[i].astype(F32))
        row = mod[i : i + 1, :]
        n1[i * length : (i + 1) * length, :] = (
            xhat * (1.0 + row[:, feat : 2 * feat]) + row[:, :feat]
        ).astype(BF16)
    proj[:, 0:feat] = (dot(n1[...], wpo[0]) + qv[:, :feat]).astype(BF16)
    proj[:, feat : 2 * feat] = dot(n1[...], wpo[1]).astype(BF16)
    proj[:, 2 * feat :] = (dot(n1[...], wpo[2]) + qv[:, feat:]).astype(BF16)

    def one(i, carry):
        at = i * length
        for pair in range(HEADS // 2):
            lo = pair * 2 * HEAD_DIM
            hi = lo + 2 * HEAD_DIM
            q = proj[pl.ds(at, length), lo:hi] * jnp.asarray(HEAD_DIM ** (-0.5), BF16)
            k = proj[pl.ds(at, length), feat + lo : feat + hi]
            v = proj[pl.ds(at, length), 2 * feat + lo : 2 * feat + hi]
            zero = jnp.zeros_like(q)
            outs = []
            for side in range(2):
                q_one = jnp.where(low_half, q, zero) if side == 0 else jnp.where(low_half, zero, q)
                s = dot(q_one, k, NT)
                e = jnp.exp(s - jnp.max(s, axis=-1, keepdims=True))
                inv = 1.0 / jnp.sum(e, axis=-1, keepdims=True)
                outs.append(dot((e * inv).astype(BF16), v))
            att[pl.ds(at, length), lo:hi] = jnp.where(low_half, outs[0], outs[1]).astype(BF16)
        return carry

    for i in range(lat.shape[0]):
        one(i, 0)


def spread(tmp, at_row, dm, pieces, rows, f, slot=None):
    keep_odd, keep_even, send_odd, send_even = pieces
    keep = (keep_even, keep_odd)[dm % 2]
    swapped = (0, 2, 1, 3)[dm]
    send = (send_even, send_odd)[swapped % 2]
    for place, zm in enumerate(LEVELS):
        for ref, at, owner in (
            (keep, dm // 2, flip(f, 2 * zm)),
            (send, swapped // 2, flip(f, 2 * zm + 1)),
        ):
            piece = tmp[pl.ds(pl.multiple_of(at_row(owner), 16), rows), :]
            if slot is None:
                ref[at, place] = piece
            else:
                ref[at, place, slot] = piece


def mlp_body(
    ids, *refs,
):
    mlp_steps(ids, refs[:8], *refs[8:])


def mlp_steps(
    ids, pieces, m_up, m_down, o_up, o_down, wout, mod, lat, cot, att,
    res, gmid, gbr, gatt, gsum, gmod, k_odd, k_even, s_odd, s_even,
    wu, wd, n2s, acts, dgs, gmlps, gpres, n2t, tmp, tmpd, brs, xhats, rstds, mlps,
):
    d, f, mine, theirs = offsets(ids)
    count = ids[2]
    rows, feat = m_up.shape[0], m_down.shape[1]
    hidden = wd.shape[0]
    blocks = hidden // feat
    step = 512
    whole = ((m_up, m_down), (o_up, o_down))
    split = (pieces[:4], mine, f), (pieces[4:], theirs, flip(f, 1))
    for (u_ref, d_ref), (found, flips, base) in zip(whole, split):
        at = pl.multiple_of(base * rows, 16)
        wu[pl.ds(at, rows), :] = u_ref[...]
        wd[pl.ds(pl.multiple_of(base * 4 * rows, 16), 4 * rows), :] = d_ref[...]
        for n, how in enumerate(flips):
            block = flip(d, how)
            for place, zm in enumerate(LEVELS[1:]):
                get = found[n].at[place]
                owner = flip(base, 2 * zm)
                wu[
                    pl.ds(pl.multiple_of(owner * rows, 16), rows),
                    pl.ds(pl.multiple_of(block * feat, 128), feat),
                ] = get[rows : 2 * rows, :]
                at = pl.multiple_of((owner * 4 + block) * rows, 16)
                wd[pl.ds(at, rows), :] = get[2 * rows : 3 * rows, :]
    length = lat.shape[1]
    bup = mod[2:3, : 4 * feat]
    bout = mod[3:4, :feat]
    bdown = mod[3:4, feat : 2 * feat]
    members = lat.shape[0]

    def rows_of(i):
        row = mod[i : i + 1, :]
        return (row[:, j * feat : (j + 1) * feat] for j in (2, 3, 4, 5))

    brs[...] = dot(att[...], wout[0]) + bout
    for i in range(members):
        part = slice(i * length, (i + 1) * length)
        gate_one, shift, scale, _ = rows_of(i)
        middle = lat[i].astype(F32) + gate_one * brs[part, :]
        xhat, rstd = norm_parts(middle)
        gmid[i] = middle
        xhats[part, :] = xhat
        rstds[part, :] = jnp.broadcast_to(rstd, (length, 128))
        n2s[part, :] = (xhat * (1.0 + scale) + shift).astype(BF16)
    mlp = None
    for j in range(0, hidden, step):
        cols = slice(j, j + step)
        v = dot(n2s[...], wu[:, cols]) + bup[:, cols]
        square = v * v
        half = 0.5 + 0.5 * jnp.tanh(v * (0.7978845608028654 + 0.035677408136300125 * square))
        act = (v * half).astype(BF16)
        slope = v * (1.5957691216057308 + 0.21406444881780075 * square)
        dgs[:, cols] = half * (1.0 + (1.0 - half) * slope)
        acts[:, cols] = act
        term = dot(act, wd[cols, :])
        mlp = term if mlp is None else mlp + term
    mlps[...] = mlp + bdown
    g_gate_two = []
    for i in range(members):
        part = slice(i * length, (i + 1) * length)
        gate_two = list(rows_of(i))[3]
        alive = jnp.where(i < count, 1.0, 0.0).astype(F32)
        mlp = mlps[part, :]
        res[i] = (alive * (gmid[i] + gate_two * mlp)).astype(BF16)
        upstream = alive * cot[i].astype(F32)
        g_gate_two.append(jnp.sum(upstream * mlp, axis=0, keepdims=True))
        gmlps[part, :] = (gate_two * upstream).astype(BF16)
    gn = None
    for j in range(0, hidden, step):
        cols = slice(j, j + step)
        gpre = (dot(gmlps[...], wd[cols, :], NT) * dgs[:, cols]).astype(BF16)
        gpres[:, cols] = gpre
        term = dot(gpre, wu[:, cols], NT)
        gn = term if gn is None else gn + term
        gsum[:, feat + j : feat + j + step] = jnp.sum(gpre.astype(F32), axis=0, keepdims=True)
    mlps[...] = gn
    for i in range(members):
        part = slice(i * length, (i + 1) * length)
        gate_one, _, scale, _ = rows_of(i)
        alive = jnp.where(i < count, 1.0, 0.0).astype(F32)
        gn, xhat = mlps[part, :], xhats[part, :]
        g_shift = jnp.sum(gn, axis=0, keepdims=True)
        g_scale = jnp.sum(gn * xhat, axis=0, keepdims=True)
        gx = gn * (1.0 + scale)
        gmiddle = alive * cot[i].astype(F32) + rstds[part, 0:1] * (
            gx
            - jnp.mean(gx, axis=-1, keepdims=True)
            - xhat * jnp.mean(gx * xhat, axis=-1, keepdims=True)
        )
        gmid[i] = gmiddle
        g_gate_one = jnp.sum(gmiddle * brs[part, :], axis=0, keepdims=True)
        gbr[part, :] = (gate_one * gmiddle).astype(BF16)
        gmod[i : i + 1, :] = jnp.concatenate([g_gate_one, g_shift, g_scale, g_gate_two[i]], axis=1)
    gatt[...] = dot(gbr[...], wout[0], NT).astype(BF16)
    gsum[:, 0:feat] = jnp.sum(gbr[...].astype(F32), axis=0, keepdims=True)
    gsum[:, 5 * feat : 6 * feat] = jnp.sum(gmlps[...].astype(F32), axis=0, keepdims=True)
    pieces = (k_odd, k_even, s_odd, s_even)
    n2t[...] = n2s[...].T
    for j in range(0, hidden, step):
        cols = slice(j, j + step)
        tmpd[cols, :] = dot(acts[:, cols], gmlps[...], TN).astype(BF16)
        tmp[:, cols] = dot(n2t[...], gpres[:, cols]).astype(BF16)
    for dm in range(4):
        block = flip(d, mine[dm])
        spread(tmpd, lambda o: (o * 4 + block) * rows, dm, pieces, rows, f, 1)
        cut = pl.ds(pl.multiple_of(block * feat, 128), feat)
        spread(tmp.at[:, cut], lambda o: o * rows, dm, pieces, rows, f, 0)


def attend_back_one(proj, gatt, gall, i, length):
    feat = gatt.shape[1]
    low_half = lane_masks(length)

    def one(i, carry):
        part = slice(i * length, (i + 1) * length)
        for pair in range(HEADS // 2):
            lo = pair * 2 * HEAD_DIM
            hi = lo + 2 * HEAD_DIM
            q = proj[part, lo:hi] * jnp.asarray(HEAD_DIM ** (-0.5), BF16)
            k = proj[part, feat + lo : feat + hi]
            v = proj[part, 2 * feat + lo : 2 * feat + hi]
            ga = gatt[part, lo:hi]
            zero = jnp.zeros_like(q)
            gq = jnp.zeros(q.shape, F32)
            gk = jnp.zeros(q.shape, F32)
            gv = jnp.zeros(q.shape, F32)
            for side in range(2):
                own = lambda a: (
                    jnp.where(low_half, a, zero) if side == 0 else jnp.where(low_half, zero, a)
                )
                q_one, ga_one = own(q), own(ga)
                s = dot(k, q_one, NT)
                e = jnp.exp(s - jnp.max(s, axis=0, keepdims=True))
                prob = e * (1.0 / jnp.sum(e, axis=0, keepdims=True))
                gv = gv + dot(prob.astype(BF16), ga_one)
                gp = dot(v, ga_one, NT)
                delta = jnp.sum(gp * prob, axis=0, keepdims=True)
                gs = (prob * (gp - delta)).astype(BF16)
                gk = gk + dot(gs, q_one)
                gq = gq + dot(gs, own(k), TN)
            gall[part, lo:hi] = (gq * HEAD_DIM ** (-0.5)).astype(BF16)
            gall[part, feat + lo : feat + hi] = gk.astype(BF16)
            gall[part, 2 * feat + lo : 2 * feat + hi] = gv.astype(BF16)
        return carry

    one(i, 0)


def attend_back_first_body(proj, gatt, gproj, *, length):
    attend_back_one(proj, gatt, gproj, 0, length)


def attend_back_body(
    ids, proj, gatt, att, gbr, n1, gsum, g_first, gproj, bias, k_odd, k_even, s_odd, s_even,
    gall, xts, tmp, *, length,
):
    d, f, mine, _ = offsets(ids)
    feat = att.shape[1]
    rows = k_odd.shape[2]
    gall[0:length, : 3 * feat] = g_first[...]
    for i in range(1, proj.shape[0] // length):
        attend_back_one(proj, gatt, gall, i, length)
    gproj[...] = gall[:, : 3 * feat]
    gall[:, 3 * feat :] = gbr[...]
    xts[0] = n1[...].T
    xts[1] = att[...].T
    pieces = (k_odd, k_even, s_odd, s_even)
    for dm in (1, 3, 0, 2):
        block = flip(d, mine[dm])
        tmp[...] = dot(
            xts[jnp.where(block == 3, 1, 0)],
            gall[:, pl.ds(pl.multiple_of(block * feat, 128), feat)],
        ).astype(BF16)
        spread(tmp, lambda o: o * rows, dm, pieces, rows, f)
    bias[:, 0:feat] = jnp.sum(gall[:, 0:feat].astype(F32), axis=0, keepdims=True)
    bias[:, feat : 2 * feat] = jnp.sum(
        gall[:, 2 * feat : 3 * feat].astype(F32), axis=0, keepdims=True
    )
    bias[:, 2 * feat :] = gsum[...]


def input_back_body(ids, gproj, wpo, lat, gmid, mod, gmod, bias, lgrad, gm, full):
    length = lat.shape[1]
    feat = lat.shape[2]

    def one(i, carry):
        part = pl.ds(i * length, length)
        row = mod[pl.ds(i, 1), :]
        xhat, rstd = norm_parts(lat[i].astype(F32))
        gn = dot(gproj[part, 0:feat], wpo[0], NT)
        gn = gn + dot(gproj[part, feat : 2 * feat], wpo[1], NT)
        gn = gn + dot(gproj[part, 2 * feat :], wpo[2], NT)
        g_shift = jnp.sum(gn, axis=0, keepdims=True)
        g_scale = jnp.sum(gn * xhat, axis=0, keepdims=True)
        gx = gn * (1.0 + row[:, feat : 2 * feat])
        lgrad[i] = (
            gmid[i]
            + rstd
            * (
                gx
                - jnp.mean(gx, axis=-1, keepdims=True)
                - xhat * jnp.mean(gx * xhat, axis=-1, keepdims=True)
            )
        ).astype(BF16)
        full[pl.ds(i, 1), : 6 * feat] = jnp.concatenate(
            [g_shift, g_scale, gmod[pl.ds(i, 1), :]], axis=1
        )
        return carry

    for i in range(lat.shape[0]):
        one(i, 0)
    full[0:1, 6 * feat :] = bias[:, : 4 * feat]
    full[1:2, 6 * feat :] = bias[:, 4 * feat :]
    gm[...] = full[...].astype(BF16)


def cond_back_body(ids, g0, g2, g1, g3, wmod, lo, hi):
    f = ids[1]
    rows, wide = wmod.shape
    many = g0.shape[0]
    place = one_hot((rows, lo.shape[2]), f * rows)
    grads = jnp.concatenate([ref[:, :wide] for ref in (g0, g2, g1, g3)], axis=0)
    whole = dot(dot(grads, wmod[...], NT).astype(BF16), place).astype(BF16)
    for n, (out, at) in enumerate(((lo, 0), (lo, 1), (hi, 0), (hi, 1))):
        out[at] = jnp.zeros(out.shape[1:], BF16)
        out[at, 0:many, :] = whole[many * n : many * (n + 1)]


def mod_weight_body(ids, e0, e1, e2, e3, wgrad, b_mod, b_qv, b_out, b_up, b_down):
    f = ids[1]
    rows, wide = wgrad.shape
    feat = wide // 6
    grad_wide = e0.shape[1] - feat
    select = one_hot((rows, feat), f * rows)
    total = None
    sums = None
    for ref in (e0, e1, e2, e3):
        own = dot(select, ref[:, grad_wide:], NT).astype(BF16)
        term = dot(own, ref[:, :wide])
        total = term if total is None else total + term
        low = ref[:, :grad_wide].astype(F32)
        sums = low if sums is None else sums + low
    wgrad[...] = total
    low = sums[:, wide:]
    odd = lax.broadcasted_iota(jnp.int32, low.shape, 0) % 2 == 1
    even_sum = jnp.sum(jnp.where(odd, 0.0, low), axis=0, keepdims=True)
    odd_sum = jnp.sum(jnp.where(odd, low, 0.0), axis=0, keepdims=True)
    whole = jnp.concatenate([jnp.sum(sums[:, :wide], axis=0, keepdims=True), even_sum, odd_sum], axis=1)
    at = 0
    for out in (b_mod, b_qv, b_out, b_up, b_down):
        size = out.shape[0]
        vector = jnp.broadcast_to(whole[:, at : at + 8 * size], (8, 8 * size))
        out[...] = pltpu.roll(vector, lax.rem(8 - f, 8) * size, 1)[0, :size]
        at += 8 * size


def sum_body(keep, got, out):
    out[...] = add_low(keep[...], got[...])


def turn_body(keep_ud, in_ud, keep_po, in_po, got_ud, got_po, out, *, at):
    rows = keep_po.shape[2]
    for place in range(out.shape[0]):
        out[place, 0:rows] = add_low(keep_po[at, place], in_po[at, place], got_po[at, place])
        for slot in range(2):
            out[place, (1 + slot) * rows : (2 + slot) * rows] = add_low(
                keep_ud[at, place, slot], in_ud[at, place, slot], got_ud[at, place, slot]
            )


def stack_body(q2, q1, q3, out):
    for n, ref in enumerate((q2, q1, q3)):
        out[n] = ref[0 : out.shape[1], :]


def pair_body(own, other, out):
    out[0 : own.shape[0], :] = own[...]
    out[own.shape[0] :, :] = other[...]


def pack_body(g0, g2, g1, g3, c_own, c_other, out):
    many, wide = g0.shape
    half = many // 2
    for n, ref in enumerate((g0, g2, g1, g3)):
        out[many * n : many * (n + 1), 0:wide] = ref[...]
        out[many * n : many * n + half, wide:] = c_own[half * n : half * (n + 1), :]
        out[many * n + half : many * (n + 1), wide:] = c_other[half * n : half * (n + 1), :]


def join_far_body(base, part, back, out):
    size = base.shape[1]
    out[:, 0:size] = add_low(base[2:], part[2:])
    out[:, size:] = back[...]


def join_near_body(base, part, back, got, out, far):
    size = base.shape[1]
    for at, ref in enumerate((out, far)):
        ref[0:size, :] = add_low(base[at], part[at], got[at, 0:size])
        ref[size:, :] = add_low(back[at], got[at, size:])


def total_body(base, got, out, back):
    size = out.shape[0]
    out[...] = add_low(base[0:size, :], got[0:size, :])
    back[...] = base[size:, :].astype(F32) + got[size:, :].astype(F32)


def final_body(ids, g0, g1, g2, g3, gp, go, gu, gd):
    d, _, mine, _ = offsets(ids)
    rows, feat = go.shape
    for ref, how in zip((g0, g1, g2, g3), mine):
        block = flip(d, how)

        @pl.when(block < 3)
        def _():
            at = pl.multiple_of(lax.min(block, 2) * feat, 128)
            gp[:, pl.ds(at, feat)] = ref[0:rows, :].astype(F32)

        @pl.when(block == 3)
        def _():
            go[...] = ref[0:rows, :].astype(F32)

        gu[:, pl.ds(pl.multiple_of(block * feat, 128), feat)] = ref[rows : 2 * rows, :].astype(F32)
        gd[pl.ds(pl.multiple_of(block * rows, 16), rows), :] = ref[2 * rows : 3 * rows, :].astype(F32)


def routes():
    core, first, second, across = [], [], [], []
    levels = {1: [], 2: []}
    for d in range(4):
        for f in range(8):
            i = d * 8 + f
            core.append((i, i ^ 1))
            a = 1 if f % 2 == 0 else 2
            first.append((i, (d ^ a) * 8 + f))
            second.append((i, (d ^ (3 - a)) * 8 + f))
            across.append((i, (d ^ 3) * 8 + f))
            for m in levels:
                levels[m].append((i, d * 8 + (f ^ (2 * m))))
    return core, first, second, across, levels


def add_low(*parts):
    total = parts[0].astype(F32)
    for part in parts[1:]:
        total = total + part.astype(F32)
    return total.astype(BF16)


def on_device_blocks(
    latents, cond, counts, cotangent, modulation_weight, modulation_bias, projection_weight,
    query_value_bias, output_weight, output_bias, up_weight, up_bias, down_weight, down_bias,
):
    core, first, second, across, levels = routes()

    def move(x, route):
        return lax.ppermute(x, BOTH, route)

    slots, length, feat = latents.shape
    rows = projection_weight.shape[0]
    hidden = up_weight.shape[1]
    wide = modulation_weight.shape[1]
    tokens = slots * length
    d = lax.axis_index("dp")
    f = lax.axis_index("fsdp")
    ids = jnp.stack([d, f, counts[0]]).astype(jnp.int32)

    def after(x, *earlier):
        return lax.optimization_barrier((x,) + earlier)[0]

    (q_all,) = call(
        pick_body, "pick", None,
        [projection_weight, output_weight, up_weight, down_weight, cond],
        [((3 * rows + 16, feat), BF16)],
        [pltpu.VMEM((slots, feat), BF16), pltpu.SemaphoreType.DMA((4,))],
        far=(0, 1, 2, 3, 4), limit=60,
    )

    def over_dp(own):
        a = move(own, first)
        b = move(own, second)
        return [own, a, b, move(a, second)]

    whole = [projection_weight, output_weight, up_weight, down_weight]
    w_whole = whole + [move(after(x, q_all), core) for x in whole]
    wmod_other = move(after(modulation_weight, q_all), core)
    biases = [modulation_bias, query_value_bias, output_bias, up_bias, down_bias]
    wmod, placed = call(
        prepare_body, "prepare", None, [modulation_weight, wmod_other] + biases,
        [((2 * rows, wide), BF16), ((3, wide), F32)],
    )
    q_far = move(q_all, levels[2])
    placed_other = move(placed, core)
    ready = (placed_other, *w_whole[4:])
    q_far = after(q_far, *ready)
    q_near, q_both = move(after(q_all, wmod_other), levels[1]), move(q_far, levels[1])
    (own,) = call(stack_body, "stack", None, [q_far, q_near, q_both], [((3, 3 * rows, feat), BF16)])
    keep_lo, keep_hi, c_own = call(
        mod_body, "modulation", ids, [q_all, q_far, q_near, q_both, wmod, placed, placed_other],
        [((2, 4, wide), F32)] * 2 + [((4 * slots, feat), BF16)],
    )
    a_own, b_own = move(own, first), move(own, second)
    paid_lo = keep_lo + move(keep_hi, levels[1])
    a_own = after(a_own, paid_lo)
    paid_far = move(after(paid_lo[1], a_own), levels[2])
    ab_own = move(a_own, second)
    w_all = [own, a_own, b_own, ab_own]
    w_all = w_all + [move(x, core) for x in w_all[:3]] + [move(after(ab_own, paid_far), core)]

    wpo, mod, n1, proj, att = call(
        attend_body, "attention", ids,
        w_all + [w_whole[k] for k in (0, 1, 4, 5)] + [paid_lo, paid_far, latents],
        [((4, feat, feat), BF16), ((4, wide), F32), ((tokens, feat), BF16),
         ((tokens, 3 * feat), BF16), ((tokens, feat), BF16)],
        flops=2 * tokens * feat * (3 * feat + 4 * length),
    )
    wout = wpo[3:4]
    ud_shape = ((2, 4, 2, rows, feat), BF16)
    po_shape = ((2, 4, rows, feat), BF16)
    res, gmid, gbr, gatt, gsum, gmod, ud_odd, ud_even, ud_odd_out, ud_even_out = call(
        mlp_body, "mlp", ids,
        w_all + [w_whole[k] for k in (2, 3, 6, 7)] + [wout, mod, latents, cotangent, att],
        [((slots, length, feat), BF16), ((slots, length, feat), F32), ((tokens, feat), BF16),
         ((tokens, feat), BF16), ((1, 6 * feat), F32), ((slots, 4 * feat), F32)] + [ud_shape] * 4,
        [
            pltpu.VMEM((feat, hidden), BF16), pltpu.VMEM((hidden, feat), BF16),
            pltpu.VMEM((tokens, feat), BF16), pltpu.VMEM((tokens, hidden), BF16),
            pltpu.VMEM((tokens, hidden), F32), pltpu.VMEM((tokens, feat), BF16),
            pltpu.VMEM((tokens, hidden), BF16), pltpu.VMEM((feat, tokens), BF16),
            pltpu.VMEM((feat, hidden), BF16), pltpu.VMEM((hidden, feat), BF16),
            pltpu.VMEM((tokens, feat), F32), pltpu.VMEM((tokens, feat), F32),
            pltpu.VMEM((tokens, 128), F32), pltpu.VMEM((tokens, feat), F32),
        ],
        flops=2 * tokens * feat * (6 * hidden + 2 * feat),
    )
    ud_odd_in = move(ud_odd_out, core)
    ud_even_in = move(ud_even_out, core)
    (g_first,) = call(
        functools.partial(attend_back_first_body, length=length), "attention_back_first", None,
        [proj, gatt], [((length, 3 * feat), BF16)], flops=tokens * feat * 10 * length,
    )
    (odd_ud,) = call(sum_body, "sum_ud", None, [ud_odd, after(ud_odd_in, g_first)], [ud_shape])
    got_ud = move(odd_ud, first)
    gproj, bias, po_odd, po_even, po_odd_out, po_even_out = call(
        functools.partial(attend_back_body, length=length), "attention_back", ids,
        [proj, gatt, att, gbr, n1, gsum, after(g_first, odd_ud)],
        [((tokens, 3 * feat), BF16), ((1, 8 * feat), F32)] + [po_shape] * 4,
        [pltpu.VMEM((tokens, 4 * feat), BF16), pltpu.VMEM((2, feat, tokens), BF16),
         pltpu.VMEM((feat, feat), BF16)],
        flops=2 * tokens * feat * (4 * feat + 5 * length),
    )
    po_odd_in = move(po_odd_out, core)
    po_even_in = move(po_even_out, core)
    lgrad, gm = call(
        input_back_body, "input_back", ids,
        [gproj, wpo, latents, gmid, mod, gmod, bias],
        [((slots, length, feat), BF16), ((slots, 10 * feat), BF16)],
        [pltpu.VMEM((slots, 10 * feat), F32)],
        flops=2 * tokens * feat * 3 * feat,
    )
    (odd_po,) = call(sum_body, "sum_po", None, [po_odd, after(po_odd_in, gm, got_ud)], [po_shape])
    got_po = move(odd_po, first)
    c_other = move(c_own, core)

    (gm_pair,) = call(pair_body, "pair", None, [after(gm, c_other), move(gm, core)], [((2 * slots, 10 * feat), BF16)])
    gm_far = move(gm_pair, levels[2])

    halves = [ud_even, ud_even_in, po_even, po_even_in, got_ud, after(got_po, gm_far)]
    half_shape = ((4, 3 * rows, feat), BF16)
    (turned,) = call(functools.partial(turn_body, at=1), "turn", None, halves, [half_shape])
    part = move(turned, second)
    (base,) = call(
        functools.partial(turn_body, at=0), "base", None, halves[:5] + [after(got_po, turned)], [half_shape]
    )

    gm_all = [gm_pair, gm_far, move(gm_pair, levels[1]), move(gm_far, levels[1])]
    (every,) = call(
        pack_body, "pack", None, gm_all + [c_own, c_other], [((8 * slots, 11 * feat), BF16)]
    )
    back_lo, back_hi = call(
        cond_back_body, "cond_back", ids, gm_all + [modulation_weight], [((2, 16, feat), BF16)] * 2
    )

    pair_shape = ((2, 3 * rows + 16, feat), BF16)
    (turned,) = call(join_far_body, "join_far", None, [base, part, back_hi], [pair_shape])
    got = move(turned, levels[1])
    every = after(every, turned)
    e_first, e_second, e_both = move(every, first), move(every, second), move(every, across)
    base, far = call(
        join_near_body, "join_near", None, [base, part, back_lo, got], [((3 * rows + 16, feat), BF16)] * 2
    )
    g_mod_weight, *g_biases = call(
        mod_weight_body, "mod_weight", ids, [every, e_first, e_second, e_both],
        [((rows, wide), F32)] + [((size // 8,), F32) for size in (wide, 2 * feat, feat, hidden, feat)],
    )
    total, back = call(
        total_body, "total", None, [base, after(move(far, levels[2]), g_mod_weight)],
        [((3 * rows, feat), BF16), ((16, feat), F32)],
    )
    a_total, b_total = move(total, first), move(total, second)
    shares = [total, a_total, b_total, move(total, across)]
    grad_silu = back[:slots] + move(back[slots : 2 * slots], core)
    cond_full = cond.astype(F32)
    sig = 1.0 / (1.0 + jnp.exp(-cond_full))
    cond_grad = (grad_silu * (sig * (1.0 + cond_full * (1.0 - sig)))).astype(BF16)
    g_proj, g_out, g_up, g_down = call(
        final_body, "final", ids, shares,
        [((rows, 3 * feat), F32), ((rows, feat), F32), ((rows, hidden), F32),
         ((4 * rows, feat), F32)],
    )
    return (
        res, lgrad, cond_grad, g_mod_weight, g_biases[0], g_proj, g_biases[1],
        g_out, g_biases[2], g_up, g_biases[3], g_down, g_biases[4],
    )


def layer_norm(vector):
    row_mean = jnp.mean(vector, axis=-1, keepdims=True)
    centered = vector - row_mean
    variance = jnp.mean(centered * centered, axis=-1, keepdims=True)
    return centered * lax.rsqrt(variance + 1e-06)


def modulate(vector, offset, stretch):
    return layer_norm(vector) * (1.0 + stretch[:, None, :]) + offset[:, None, :]


def forward_pass(gathered, inputs, conditions):
    (
        modulation_weight,
        modulation_bias,
        projection_weight,
        query_value_bias,
        output_weight,
        output_bias,
        up_weight,
        up_bias,
        down_weight,
        down_bias,
    ) = gathered
    members, length, features = inputs.shape
    flat_rows = members * length
    cond_low = jax.nn.silu(conditions).astype(jnp.bfloat16)
    modulation = jnp.dot(cond_low, modulation_weight, preferred_element_type=jnp.float32)
    modulation = modulation + modulation_bias.astype(jnp.float32)
    pieces = jnp.split(modulation, 6, axis=-1)
    normed_one = (
        modulate(inputs, pieces[0], pieces[1]).astype(jnp.bfloat16).reshape(flat_rows, features)
    )
    bias_full = query_value_bias.astype(jnp.float32)
    joined_bias = jnp.concatenate(
        [bias_full[:features], jnp.zeros((features,), jnp.float32), bias_full[features:]]
    )
    projected = (
        jnp.dot(normed_one, projection_weight, preferred_element_type=jnp.float32) + joined_bias
    )
    projected = projected.astype(jnp.bfloat16).reshape(members, length, 3, HEADS, HEAD_DIM)
    queries = projected[:, :, 0]
    key_rows = projected[:, :, 1]
    values = projected[:, :, 2]
    scores = jnp.einsum(
        "bqhd,bkhd->bhqk", queries, key_rows, preferred_element_type=jnp.float32
    ) * HEAD_DIM ** (-0.5)
    row_max = jnp.max(scores, axis=-1, keepdims=True)
    exponent = jnp.exp(scores - row_max)
    row_total = jnp.sum(exponent, axis=-1, keepdims=True)
    probability = exponent / row_total
    log_total = row_max + jnp.log(row_total)
    attended = jnp.einsum(
        "bhqk,bkhd->bqhd",
        probability.astype(jnp.bfloat16),
        values,
        preferred_element_type=jnp.float32,
    )
    attended = attended.astype(jnp.bfloat16).reshape(flat_rows, features)
    branch = jnp.dot(
        attended, output_weight, preferred_element_type=jnp.float32
    ) + output_bias.astype(jnp.float32)
    branch = branch.reshape(members, length, features)
    middle = inputs + pieces[2][:, None, :] * branch
    normed_two = (
        modulate(middle, pieces[3], pieces[4]).astype(jnp.bfloat16).reshape(flat_rows, features)
    )
    pre_act = jnp.dot(normed_two, up_weight, preferred_element_type=jnp.float32) + up_bias.astype(
        jnp.float32
    )
    activated = jax.nn.gelu(pre_act, approximate=True).astype(jnp.bfloat16)
    mlp_out = jnp.dot(
        activated, down_weight, preferred_element_type=jnp.float32
    ) + down_bias.astype(jnp.float32)
    mlp_out = mlp_out.reshape(members, length, features)
    output = middle + pieces[5][:, None, :] * mlp_out
    return (
        output,
        cond_low,
        pieces,
        normed_one,
        queries,
        key_rows,
        values,
        log_total,
        attended,
        branch,
        middle,
        normed_two,
        pre_act,
        activated,
        mlp_out,
    )


def backward_pass(gathered, saved, inputs, conditions, upstream):
    (
        modulation_weight,
        modulation_bias,
        projection_weight,
        query_value_bias,
        output_weight,
        output_bias,
        up_weight,
        up_bias,
        down_weight,
        down_bias,
    ) = gathered
    (
        output,
        cond_low,
        pieces,
        normed_one,
        queries,
        key_rows,
        values,
        log_total,
        attended,
        branch,
        middle,
        normed_two,
        pre_act,
        activated,
        mlp_out,
    ) = saved
    members, length, features = inputs.shape
    flat_rows = members * length
    grad_gate_two = jnp.sum(upstream * mlp_out, axis=1)
    grad_mlp = (pieces[5][:, None, :] * upstream).astype(jnp.bfloat16).reshape(flat_rows, features)
    grad_down = jnp.einsum("nf,nd->fd", activated, grad_mlp, preferred_element_type=jnp.float32)
    grad_down_b = jnp.sum(grad_mlp.astype(jnp.float32), axis=0)
    grad_activated = jnp.einsum(
        "nd,fd->nf", grad_mlp, down_weight, preferred_element_type=jnp.float32
    )
    gelu_out, gelu_pull = jax.vjp(lambda vector: jax.nn.gelu(vector, approximate=True), pre_act)
    grad_pre = gelu_pull(grad_activated)[0].astype(jnp.bfloat16)
    grad_up = jnp.einsum("nd,nf->df", normed_two, grad_pre, preferred_element_type=jnp.float32)
    grad_up_b = jnp.sum(grad_pre.astype(jnp.float32), axis=0)
    grad_normed_two = jnp.einsum(
        "nf,df->nd", grad_pre, up_weight, preferred_element_type=jnp.float32
    )
    second_out, second_pull = jax.vjp(modulate, middle, pieces[3], pieces[4])
    grad_middle, grad_shift_two, grad_scale_two = second_pull(
        grad_normed_two.reshape(members, length, features)
    )
    grad_middle = grad_middle + upstream
    grad_gate_one = jnp.sum(grad_middle * branch, axis=1)
    grad_branch = (
        (pieces[2][:, None, :] * grad_middle).astype(jnp.bfloat16).reshape(flat_rows, features)
    )
    grad_output = jnp.einsum("nd,ne->de", attended, grad_branch, preferred_element_type=jnp.float32)
    grad_output_b = jnp.sum(grad_branch.astype(jnp.float32), axis=0)
    grad_attended = jnp.einsum(
        "ne,de->nd", grad_branch, output_weight, preferred_element_type=jnp.float32
    )
    grad_attended = grad_attended.astype(jnp.bfloat16).reshape(members, length, HEADS, HEAD_DIM)
    scale_factor = HEAD_DIM ** (-0.5)
    scores = (
        jnp.einsum("bqhd,bkhd->bhqk", queries, key_rows, preferred_element_type=jnp.float32)
        * scale_factor
    )
    probability = jnp.exp(scores - log_total)
    grad_values = jnp.einsum(
        "bhqk,bqhd->bkhd",
        probability.astype(jnp.bfloat16),
        grad_attended,
        preferred_element_type=jnp.float32,
    )
    grad_prob = jnp.einsum(
        "bqhd,bkhd->bhqk", grad_attended, values, preferred_element_type=jnp.float32
    )
    row_delta = jnp.sum(grad_prob * probability, axis=-1, keepdims=True)
    grad_scores = (probability * (grad_prob - row_delta)).astype(jnp.bfloat16)
    grad_queries = (
        jnp.einsum("bhqk,bkhd->bqhd", grad_scores, key_rows, preferred_element_type=jnp.float32)
        * scale_factor
    )
    grad_keys = (
        jnp.einsum("bhqk,bqhd->bkhd", grad_scores, queries, preferred_element_type=jnp.float32)
        * scale_factor
    )
    grad_projected = jnp.stack([grad_queries, grad_keys, grad_values], axis=2)
    grad_projected = grad_projected.astype(jnp.bfloat16).reshape(flat_rows, 3 * features)
    grad_projection = jnp.einsum(
        "nd,ne->de", normed_one, grad_projected, preferred_element_type=jnp.float32
    )
    column_sums = jnp.sum(grad_projected.astype(jnp.float32), axis=0)
    grad_query_value = jnp.concatenate([column_sums[:features], column_sums[2 * features :]])
    grad_normed_one = jnp.einsum(
        "ne,de->nd", grad_projected, projection_weight, preferred_element_type=jnp.float32
    )
    first_out, first_pull = jax.vjp(modulate, inputs, pieces[0], pieces[1])
    grad_input, grad_shift_one, grad_scale_one = first_pull(
        grad_normed_one.reshape(members, length, features)
    )
    grad_input = grad_input + grad_middle
    grad_modulation = jnp.concatenate(
        [
            grad_shift_one,
            grad_scale_one,
            grad_gate_one,
            grad_shift_two,
            grad_scale_two,
            grad_gate_two,
        ],
        axis=-1,
    ).astype(jnp.bfloat16)
    grad_mod_weight = jnp.einsum(
        "bc,be->ce", cond_low, grad_modulation, preferred_element_type=jnp.float32
    )
    grad_mod_bias = jnp.sum(grad_modulation.astype(jnp.float32), axis=0)
    grad_silu = jnp.einsum(
        "be,ce->bc", grad_modulation, modulation_weight, preferred_element_type=jnp.float32
    )
    silu_out, silu_pull = jax.vjp(jax.nn.silu, conditions)
    grad_conditions = silu_pull(grad_silu)[0]
    weight_grads = (
        grad_mod_weight,
        grad_mod_bias,
        grad_projection,
        grad_query_value,
        grad_output,
        grad_output_b,
        grad_up,
        grad_up_b,
        grad_down,
        grad_down_b,
    )
    return (weight_grads, grad_input, grad_conditions)


def on_device(
    latents,
    cond,
    counts,
    cotangent,
    modulation_weight,
    modulation_bias,
    projection_weight,
    query_value_bias,
    output_weight,
    output_bias,
    up_weight,
    up_bias,
    down_weight,
    down_bias,
):
    lat_slots = latents.shape[0]
    per_micro = lat_slots // MICRO
    alive_all = (jnp.arange(lat_slots) < counts[0]).astype(jnp.float32)
    kept = (
        lax.all_gather(modulation_weight, "fsdp", axis=0, tiled=True),
        lax.all_gather(modulation_bias, "fsdp", axis=0, tiled=True),
        lax.all_gather(projection_weight, "fsdp", axis=0, tiled=True),
        lax.all_gather(query_value_bias, "fsdp", axis=0, tiled=True),
        lax.all_gather(output_weight, "fsdp", axis=0, tiled=True),
        lax.all_gather(output_bias, "fsdp", axis=0, tiled=True),
        lax.all_gather(up_weight, "fsdp", axis=0, tiled=True),
        lax.all_gather(up_bias, "fsdp", axis=0, tiled=True),
        lax.all_gather(down_weight, "fsdp", axis=0, tiled=True),
        lax.all_gather(down_bias, "fsdp", axis=0, tiled=True),
    )
    outputs = []
    input_grads = []
    cond_grads = []
    totals = None
    for micro_index in range(MICRO):
        start = micro_index * per_micro
        inputs = latents[start : start + per_micro].astype(jnp.float32)
        conditions = cond[start : start + per_micro].astype(jnp.float32)
        alive_mask = alive_all[start : start + per_micro]
        saved = forward_pass(kept, inputs, conditions)
        outputs.append((saved[0] * alive_mask[:, None, None]).astype(jnp.bfloat16))
        upstream = (
            cotangent[start : start + per_micro].astype(jnp.float32) * alive_mask[:, None, None]
        )
        weight_grads, grad_input, grad_conditions = backward_pass(
            kept, saved, inputs, conditions, upstream
        )
        input_grads.append(grad_input.astype(jnp.bfloat16))
        cond_grads.append(grad_conditions.astype(jnp.bfloat16))
        totals = (
            weight_grads
            if totals is None
            else tuple((left + right for left, right in zip(totals, weight_grads)))
        )
    totals = (
        lax.psum_scatter(totals[0], "fsdp", scatter_dimension=0, tiled=True),
        lax.psum_scatter(totals[1], "fsdp", scatter_dimension=0, tiled=True),
        lax.psum_scatter(totals[2], "fsdp", scatter_dimension=0, tiled=True),
        lax.psum_scatter(totals[3], "fsdp", scatter_dimension=0, tiled=True),
        lax.psum_scatter(totals[4], "fsdp", scatter_dimension=0, tiled=True),
        lax.psum_scatter(totals[5], "fsdp", scatter_dimension=0, tiled=True),
        lax.psum_scatter(totals[6], "fsdp", scatter_dimension=0, tiled=True),
        lax.psum_scatter(totals[7], "fsdp", scatter_dimension=0, tiled=True),
        lax.psum_scatter(totals[8], "fsdp", scatter_dimension=0, tiled=True),
        lax.psum_scatter(totals[9], "fsdp", scatter_dimension=0, tiled=True),
    )
    totals = (
        lax.psum(totals[0].astype(jnp.bfloat16), "dp").astype(jnp.float32),
        lax.psum(totals[1].astype(jnp.bfloat16), "dp").astype(jnp.float32),
        lax.psum(totals[2].astype(jnp.bfloat16), "dp").astype(jnp.float32),
        lax.psum(totals[3].astype(jnp.bfloat16), "dp").astype(jnp.float32),
        lax.psum(totals[4].astype(jnp.bfloat16), "dp").astype(jnp.float32),
        lax.psum(totals[5].astype(jnp.bfloat16), "dp").astype(jnp.float32),
        lax.psum(totals[6].astype(jnp.bfloat16), "dp").astype(jnp.float32),
        lax.psum(totals[7].astype(jnp.bfloat16), "dp").astype(jnp.float32),
        lax.psum(totals[8].astype(jnp.bfloat16), "dp").astype(jnp.float32),
        lax.psum(totals[9].astype(jnp.bfloat16), "dp").astype(jnp.float32),
    )
    return (
        jnp.concatenate(outputs, axis=0),
        jnp.concatenate(input_grads, axis=0),
        jnp.concatenate(cond_grads, axis=0),
        totals[0],
        totals[1],
        totals[2],
        totals[3],
        totals[4],
        totals[5],
        totals[6],
        totals[7],
        totals[8],
        totals[9],
    )


def solution(mesh):
    small = mesh.shape["dp"] == 4 and mesh.shape["fsdp"] == 8
    program = on_device_blocks if small else on_device
    placed = (
        P(("dp", "fsdp"), None, None),
        P(("dp", "fsdp"), None),
        P(("dp", "fsdp")),
        P(("dp", "fsdp"), None, None),
        P("fsdp", None),
        P("fsdp"),
        P("fsdp", None),
        P("fsdp"),
        P("fsdp", None),
        P("fsdp"),
        P("fsdp", None),
        P("fsdp"),
        P("fsdp", None),
        P("fsdp"),
    )
    return jax.shard_map(
        program,
        mesh=mesh,
        in_specs=placed,
        out_specs=(
            P(("dp", "fsdp"), None, None),
            P(("dp", "fsdp"), None, None),
            P(("dp", "fsdp"), None),
            P("fsdp", None),
            P("fsdp"),
            P("fsdp", None),
            P("fsdp"),
            P("fsdp", None),
            P("fsdp"),
            P("fsdp", None),
            P("fsdp"),
            P("fsdp", None),
            P("fsdp"),
        ),
        check_vma=False,
    )
```
